128 devices in a mesh: gx: 8 (over x, core), gy: 16 (over z, y).
Axes of the slice: x: 4, y: 4, z: 4, core: 2. Of those that a mesh axis runs over, the one named last changes fastest.
Arguments:
- populations: float32 [19, 128, 256, 128], P(None, 'gx', 'gy'), may hold values from 0.02 to 0.1
- porosity: float32 [128, 256, 128], P('gx', 'gy'), may hold values from 0.05 to 0.95
- adjoint_in: float32 [19, 128, 256, 128], P(None, 'gx', 'gy'), may hold values from -6 to 6
- porous: int32 [128, 256, 128], P('gx', 'gy'), may hold values 0 or 1
- walls: int32 [128, 256, 128], P('gx', 'gy'), may hold values 0 or 1
- owners: int32 [8, 16, 64, 1], P('gx', 'gy'), may hold values from 0 to 127; in each aligned block of 64 rows (0 to 63, 64 to 127, ..., all dimensions but the last counted through in order) at most 2 rows name the same one
- slots: int32 [8, 16, 64], P('gx', 'gy'), may hold values from 0 to 255
Outputs:
- adjoint_out: float32 [19, 128, 256, 128], P(None, 'gx', 'gy')
- patch_sens: float32 [32768], P(('gx', 'gy'))
The draws below stay inside these ranges and needn't reach their ends.
Inputs may be any that keep to these rules, and one draw needn't show every extreme that they name: `owners`: of the 64 panel blocks of one device, at most 2 name the same owner device, and some device's blocks reach 2 for some owner in every draw.
All inputs are finite; a program needn't handle non-finite values. No bound on the sum of `porous` or of `walls` on one device may be relied on, other than what follows from the above.
Results may differ from the reference program's by a relative error of at most 0.0003.
Values sent between devices are 32-bit elements; how exact they have to be, the bound alone decides.
No kernel may reach another device: no remote copies, remote signals or barrier semaphores. Data moves between devices by JAX's collectives and lax.ppermute only.
A program may use at most 128 MiB of HBM per device.

```python
import math
from functools import partial
import jax
import jax.numpy as jnp
import numpy as np
from jax import lax

Q = 19
CX = 16
CY = 16
NZ = 128
BLOCK = 2
PATCH_DEV = 256
NX = 128
NY = 256
BLK_DEV = 64
CAP = 2
PATCHES = 32768
N_GX = 8
N_GY = 16
DEVICES = 128


def plant(drawn, stream_key, low, top_value):
    shape = drawn.shape
    place = [jax.random.randint(jax.random.fold_in(stream_key, axis), (), 0, shape[axis]) for axis in range(len(shape))]
    drawn = drawn.at[tuple(place)].set(low)
    longest = shape.index(max(shape))
    place[longest] = (place[longest] + 1) % shape[longest]
    return drawn.at[tuple(place)].set(top_value)


def levels(key, extent, split, low, top_value):
    def one(dim, parts):
        heights = jax.random.uniform(jax.random.fold_in(jax.random.fold_in(key, 6), dim), (parts,), jnp.float32, low / len(split), top_value / len(split))
        return jnp.repeat(jnp.exp(heights), extent[dim] // parts).reshape((-1,) + (1,) * (len(extent) - dim - 1))

    gain = one(*split[0])
    for cut in split[1:]:
        gain = gain * one(*cut)
    return gain


def assign_block(stream_key, own, number, rows, number_of, top, bound, slope):
    ranking = jax.random.permutation(stream_key, number_of)
    heavy_load, usual = portions_of(number_of, rows * top, bound, slope, True), portions_of(number_of, rows * top, bound, slope, False)
    places = jnp.arange(number_of)

    def named(lengths, turn):
        used = int((lengths > 0).sum())
        fixed = max(1, used // 4)
        moved = fixed + (places - fixed + turn * (used - fixed)) % max(1, number_of - fixed)
        return jnp.zeros((number_of,), jnp.int32).at[ranking[jnp.where(places < fixed, places, moved)]].set(jnp.asarray(lengths, jnp.int32))

    lengths = jnp.where(number % 4 == 0, named(heavy_load, number // 4), named(usual, number - number // 4 - 1))
    mixed = jax.random.permutation(jax.random.fold_in(own, 3), number_of)
    source_of, taker = mixed[0:number_of // 2 * 2:2], mixed[1:number_of // 2 * 2:2]
    slack = jnp.minimum(lengths[source_of] - 1, bound - lengths[taker]) // 2
    slack = jnp.where((source_of == ranking[0]) | (taker == ranking[0]) | (lengths[taker] == 0), 0, jnp.maximum(slack, 0))
    moved = jax.random.randint(jax.random.fold_in(own, 4), (number_of // 2,), 0, 1 << 20) % (slack + 1)
    lengths = lengths.at[source_of].add(-moved).at[taker].add(moved)
    members = jnp.searchsorted(jnp.cumsum(lengths), jnp.arange(rows * top), side="right").astype(jnp.int32)
    grid = members.reshape(top, rows).T
    grid = grid[jax.random.permutation(jax.random.fold_in(own, 1), rows)]
    turn = jax.random.randint(jax.random.fold_in(own, 2), (rows, 1), 0, top)
    return jnp.take_along_axis(grid, (jnp.arange(top)[None, :] + turn) % top, axis=1)


def portions_of(number_of, total, limit, lean, full):
    loads = [(1 << 20) // math.isqrt(rank ** lean) + 1 for rank in range(1, number_of + 1)]
    largest = limit if full else min(limit, max(-(-total // number_of), total * loads[0] // sum(loads)))
    least = 1 if total - largest >= number_of - 1 else 0
    given, spare = [largest] + [least] * (number_of - 1), total - largest - least * (number_of - 1)
    while spare > 0:
        movable = [i for i in range(1, number_of) if given[i] < largest] or [i for i in range(1, number_of) if given[i] < limit]
        mass, remaining = sum([loads[i] for i in movable]), spare
        for i in movable:
            more = min(limit - given[i], max(1, remaining * loads[i] // mass), spare)
            given[i] = given[i] + more
            spare = spare - more
    return np.array(given)


def scatter_about(key, shape, scale, limit, pieces=(), kind=jnp.bfloat16):
    loudness = levels(key, shape, pieces, -0.22, 0.18) if pieces else 1.0
    values = jax.random.normal(key, shape, jnp.float32) * scale * loudness
    return jnp.minimum(jnp.maximum(values, -limit), limit).astype(kind)


def setup_inputs(seed: int = 0) -> dict:
    splits = jax.random.split(jax.random.key(seed), 8)
    populations = jnp.clip(0.02 + 0.08 * jax.random.uniform(splits[0], (Q, NX, NY, NZ), jnp.float32) ** levels(splits[0], (Q, NX, NY, NZ), ((1, 8), (2, 16)), -0.2, 0.2), 0.02, 0.1)
    porosity = jnp.clip(0.05 + 0.9 * jax.random.uniform(splits[1], (NX, NY, NZ), jnp.float32) ** levels(splits[1], (NX, NY, NZ), ((0, 8), (1, 16)), -0.2, 0.2), 0.05, 0.95)
    adjoint_in = scatter_about(splits[2], (Q, NX, NY, NZ), 1.0, 6.0, ((1, 8), (2, 16)), jnp.float32)
    porous = plant((jax.random.randint(splits[3], (NX, NY, NZ), 0, 2) < 1).astype(jnp.int32), jax.random.fold_in(splits[3], 1), 0, 1)
    walls = plant((jax.random.randint(splits[4], (NX, NY, NZ), 0, 8) < 1).astype(jnp.int32), jax.random.fold_in(splits[4], 1), 0, 1)
    owners_keys = jax.random.split(jax.random.fold_in(splits[5], 1), N_GX * N_GY * BLK_DEV // BLK_DEV)
    owners_turns = jax.random.permutation(jax.random.fold_in(splits[5], 3), N_GX * N_GY * BLK_DEV // BLK_DEV)
    owners = jax.vmap(lambda own, number: assign_block(jax.random.fold_in(splits[5], 2), own, number, BLK_DEV, DEVICES, 1, CAP, 2))(owners_keys, owners_turns).reshape((N_GX, N_GY, BLK_DEV, 1))
    slots = plant(jax.random.randint(splits[6], (N_GX, N_GY, BLK_DEV), 0, PATCH_DEV), jax.random.fold_in(splits[6], 1), 0, PATCH_DEV - 1).astype(jnp.int32)
    return {"populations": populations, "porosity": porosity, "adjoint_in": adjoint_in, "porous": porous, "walls": walls, "owners": owners, "slots": slots}


velocities = [[0, 0, 0], [1, 0, 0], [-1, 0, 0], [0, 1, 0], [0, -1, 0], [0, 0, 1], [0, 0, -1], [1, 1, 0], [-1, -1, 0], [1, -1, 0], [-1, 1, 0], [1, 0, 1], [-1, 0, -1], [1, 0, -1], [-1, 0, 1], [0, 1, 1], [0, -1, -1], [0, 1, -1], [0, -1, 1]]
opposite = [0, 2, 1, 4, 3, 6, 5, 8, 7, 10, 9, 12, 11, 14, 13, 16, 15, 18, 17]
lattice_weights = [1.0 / 3.0] + [1.0 / 18.0] * 6 + [1.0 / 36.0] * 12
moment_powers = [[0, 0, 0], [1, 0, 0], [0, 1, 0], [0, 0, 1], [2, 0, 0], [0, 2, 0], [0, 0, 2], [1, 1, 0], [0, 1, 1], [1, 0, 1], [2, 1, 0], [2, 0, 1], [1, 2, 0], [0, 2, 1], [1, 0, 2], [0, 1, 2], [2, 2, 0], [0, 2, 2], [2, 0, 2]]
relax_rates = [0.0] * 4 + [1.25] * 6 + [1.5] * 6 + [1.4] * 3

def invert_table(matrix):
    order = len(matrix)
    table = [list(matrix[row_index]) + [1.0 if row_index == other else 0.0 for other in range(order)] for row_index in range(order)]
    for column in range(order):
        pivot_row = max(range(column, order), key=lambda candidate: abs(table[candidate][column]))
        table[column], table[pivot_row] = (table[pivot_row], table[column])
        leading = table[column][column]
        table[column] = [entry / leading for entry in table[column]]
        for row_index in range(order):
            if row_index != column:
                factor = table[row_index][column]
                table[row_index] = [first - factor * second for first, second in zip(table[row_index], table[column])]
    return [row[order:] for row in table]

def relaxation():
    moments = [[float(vector[0] ** power[0] * vector[1] ** power[1] * vector[2] ** power[2]) for vector in velocities] for power in moment_powers]
    inverse = invert_table(moments)
    return [[sum((inverse[row_index][middle] * relax_rates[middle] * moments[middle][column] for middle in range(19))) for column in range(19)] for row_index in range(19)]

def collide(populations, porosity, porous, walls):
    highest = lax.Precision.HIGHEST
    vectors = jnp.asarray(velocities, dtype=jnp.float32)
    weights = jnp.asarray(lattice_weights, dtype=jnp.float32)
    kernel = jnp.asarray(relaxation(), dtype=jnp.float32)
    density = lax.optimization_barrier(jnp.sum(populations, axis=0))
    momentum = jnp.einsum('iq,ixyz->qxyz', vectors, populations, precision=highest)
    velocity = momentum / density
    projected = jnp.einsum('iq,qxyz->ixyz', vectors, velocity, precision=highest)
    speed_square = lax.optimization_barrier(jnp.sum(velocity * velocity, axis=0))
    equilibrium = weights[:, None, None, None] * density * (1.0 + 3.0 * projected + 4.5 * projected * projected - 1.5 * speed_square)
    relaxed = populations - jnp.einsum('ij,jxyz->ixyz', kernel, populations - equilibrium, precision=highest)
    fraction = jnp.where(walls == 1, jnp.float32(1.0), porous.astype(jnp.float32) * porosity)
    reversed_pop = jnp.stack([populations[index] for index in opposite])
    return (1.0 - fraction) * relaxed + fraction * reversed_pop

def stream(field, direction):
    moved = []
    for lattice_dir in range(19):
        offsets = tuple((int(direction * value) for value in velocities[lattice_dir]))
        moved.append(jnp.roll(field[lattice_dir], offsets, axis=(0, 1, 2)))
    return jnp.stack(moved)

def reference(populations, porosity, adjoint_in, porous, walls, owners, slots):
    collide_here = partial(collide, porous=porous, walls=walls)
    read = stream(collide_here(populations, porosity), 1)
    _, pull_late = jax.vjp(collide_here, read, porosity)
    late_adjoint, late_sens = pull_late(adjoint_in)
    pulled = stream(late_adjoint, -1)
    _, pull_early = jax.vjp(collide_here, populations, porosity)
    adjoint_out, early_sens = pull_early(pulled)
    node_sens = early_sens + late_sens
    blocks = lax.optimization_barrier(jnp.sum(node_sens.reshape(NX // BLOCK, BLOCK, NY // BLOCK, BLOCK, NZ), axis=(1, 3, 4)))
    blocks = blocks.reshape(N_GX, CX // BLOCK, N_GY, CY // BLOCK).transpose(0, 2, 1, 3).reshape(-1)
    patch_ids = (owners.reshape(-1) * PATCH_DEV + slots.reshape(-1)).astype(jnp.int32)
    patch_sens = jax.ops.segment_sum(blocks, patch_ids, num_segments=PATCHES)
    return (adjoint_out, patch_sens)
```

```python
import functools

import jax
import jax.numpy as jnp
from jax import lax
from jax.experimental import pallas as pl
from jax.experimental.pallas import tpu as pltpu
from jax.sharding import PartitionSpec as P

Q = 19
CX = 16
CY = 16
NZ = 128
TILE = 8
PAD_Y = 8
EXT_Y = 32
DEVICES = 128
PATCH_DEV = 256
SLOT_LANE = 64

velocities = [
    (0, 0, 0),
    (1, 0, 0),
    (-1, 0, 0),
    (0, 1, 0),
    (0, -1, 0),
    (0, 0, 1),
    (0, 0, -1),
    (1, 1, 0),
    (-1, -1, 0),
    (1, -1, 0),
    (-1, 1, 0),
    (1, 0, 1),
    (-1, 0, -1),
    (1, 0, -1),
    (-1, 0, 1),
    (0, 1, 1),
    (0, -1, -1),
    (0, 1, -1),
    (0, -1, 1),
]
opposite = [0, 2, 1, 4, 3, 6, 5, 8, 7, 10, 9, 12, 11, 14, 13, 16, 15, 18, 17]
RATE2, RATE3, RATE4 = 1.25, 1.5, 1.4


def moving(axis, sign, direction):
    return [i for i in range(Q) if direction * velocities[i][axis] == sign]


def edge(f, first):
    s, d = f[first] + f[first + 1], f[first] - f[first + 1]
    s2, d2 = f[first + 2] + f[first + 3], f[first + 2] - f[first + 3]
    return s, d, s2, d2


def off_equilibrium(f):
    sx, dx = f[1] + f[2], f[1] - f[2]
    sy, dy = f[3] + f[4], f[3] - f[4]
    sz, dz = f[5] + f[6], f[5] - f[6]
    s7, d7, s9, d9 = edge(f, 7)
    s11, d11, s13, d13 = edge(f, 11)
    s15, d15, s17, d17 = edge(f, 15)
    m220, m110, m120, m210 = s7 + s9, s7 - s9, d7 + d9, d7 - d9
    m202, m101, m102, m201 = s11 + s13, s11 - s13, d11 + d13, d11 - d13
    m022, m011, m012, m021 = s15 + s17, s15 - s17, d15 + d17, d15 - d17
    m200, m020, m002 = sx + m220 + m202, sy + m220 + m022, sz + m202 + m022
    jx, jy, jz = dx + (m120 + m102), dy + (m210 + m012), dz + (m201 + m021)
    rho = f[0] + (sx + sy + sz) + (m220 + m202 + m022)
    inv = 1.0 / rho
    ux, uy, uz = jx * inv, jy * inv, jz * inv
    qx, qy, qz = jx * ux, jy * uy, jz * uz
    third = rho * (1.0 / 3.0)
    ninth = rho * (1.0 / 9.0) - (qx + qy + qz) * (1.0 / 6.0)
    tx, ty, tz = jx * (1.0 / 3.0), jy * (1.0 / 3.0), jz * (1.0 / 3.0)
    e = {
        "200": RATE2 * (m200 - third - qx),
        "020": RATE2 * (m020 - third - qy),
        "002": RATE2 * (m002 - third - qz),
        "110": RATE2 * (m110 - jx * uy),
        "101": RATE2 * (m101 - jx * uz),
        "011": RATE2 * (m011 - jy * uz),
        "120": RATE3 * (m120 - tx),
        "102": RATE3 * (m102 - tx),
        "210": RATE3 * (m210 - ty),
        "012": RATE3 * (m012 - ty),
        "201": RATE3 * (m201 - tz),
        "021": RATE3 * (m021 - tz),
        "220": RATE4 * (m220 - ninth - 0.5 * (qx + qy)),
        "202": RATE4 * (m202 - ninth - 0.5 * (qx + qz)),
        "022": RATE4 * (m022 - ninth - 0.5 * (qy + qz)),
    }
    return (ux, uy, uz), e, (dx, dy, dz, d7, d9, d11, d13, d15, d17)


def spread(t, g, a, b):
    even, odd = t + g, t - g
    plus, minus = a + b, a - b
    return [even + plus, even - plus, odd + minus, odd - minus]


def correction(e):
    q = {k: 0.25 * v for k, v in e.items()}
    xy = spread(q["220"], q["110"], q["120"], q["210"])
    xz = spread(q["202"], q["101"], q["102"], q["201"])
    yz = spread(q["022"], q["011"], q["012"], q["021"])
    faces = []
    for second, fourth, odd in (
        ("200", ("220", "202"), ("120", "102")),
        ("020", ("220", "022"), ("210", "012")),
        ("002", ("202", "022"), ("201", "021")),
    ):
        mean = 0.5 * e[second] - 2.0 * (q[fourth[0]] + q[fourth[1]])
        lean = 2.0 * (q[odd[0]] + q[odd[1]])
        faces += [mean - lean, mean + lean]
    rest = (e["220"] + e["202"] + e["022"]) - (e["200"] + e["020"] + e["002"])
    return [rest] + faces + xy + xz + yz


def covector(b):
    hx, dx = 0.5 * (b[1] + b[2]), b[1] - b[2]
    hy, dy = 0.5 * (b[3] + b[4]), b[3] - b[4]
    hz, dz = 0.5 * (b[5] + b[6]), b[5] - b[6]
    s7, d7, s9, d9 = edge(b, 7)
    s11, d11, s13, d13 = edge(b, 11)
    s15, d15, s17, d17 = edge(b, 15)
    gx, gy, gz = hx - b[0], hy - b[0], hz - b[0]
    kx, ky, kz = 0.5 * dx, 0.5 * dy, 0.5 * dz
    t = {
        "200": gx,
        "020": gy,
        "002": gz,
        "110": 0.25 * (s7 - s9),
        "101": 0.25 * (s11 - s13),
        "011": 0.25 * (s15 - s17),
        "120": 0.25 * (d7 + d9) - kx,
        "102": 0.25 * (d11 + d13) - kx,
        "210": 0.25 * (d7 - d9) - ky,
        "012": 0.25 * (d15 + d17) - ky,
        "201": 0.25 * (d11 - d13) - kz,
        "021": 0.25 * (d15 - d17) - kz,
        "220": 0.25 * (s7 + s9) - gx - hy,
        "202": 0.25 * (s11 + s13) - gx - hz,
        "022": 0.25 * (s15 + s17) - gy - hz,
    }
    return t, (dx, dy, dz, d7, d9, d11, d13, d15, d17)


def pull_back(b, t, u, fraction):
    rates = {k: (RATE2, RATE3, RATE4)[sum(map(int, k)) - 2] for k in t}
    n = {k: rates[k] * v for k, v in t.items()}
    ux, uy, uz = u
    fourth = n["220"] + n["202"] + n["022"]
    second = n["200"] + n["020"] + n["002"]
    part = fourth * (1.0 / 3.0)
    ax = n["200"] + part - 0.5 * n["022"]
    ay = n["020"] + part - 0.5 * n["202"]
    az = n["002"] + part - 0.5 * n["220"]
    rx = 2.0 * ax * ux + n["110"] * uy + n["101"] * uz
    ry = 2.0 * ay * uy + n["110"] * ux + n["011"] * uz
    rz = 2.0 * az * uz + n["101"] * ux + n["011"] * uy
    p0 = second * (1.0 / 3.0) + fourth * (1.0 / 9.0) - 0.5 * (rx * ux + ry * uy + rz * uz)
    px = rx + (n["120"] + n["102"]) * (1.0 / 3.0)
    py = ry + (n["210"] + n["012"]) * (1.0 / 3.0)
    pz = rz + (n["201"] + n["021"]) * (1.0 / 3.0)
    ex, ey, ez = p0 - n["200"], p0 - n["020"], p0 - n["002"]
    h = [p0, ex + px, ex - px, ey + py, ey - py, ez + pz, ez - pz]
    h += spread(ex - n["020"] - n["220"], -n["110"], px - n["120"], py - n["210"])
    h += spread(ex - n["002"] - n["202"], -n["101"], px - n["102"], pz - n["201"])
    h += spread(ey - n["002"] - n["022"], -n["011"], py - n["012"], pz - n["021"])
    open_part = 1.0 - fraction
    return [open_part * (b[i] + h[i]) + fraction * b[opposite[i]] for i in range(Q)]


def put_moved(ext, i, x, row, value, direction):
    cx, cy, cz = (direction * c for c in velocities[i])
    if cz:
        value = pltpu.roll(value, cz % NZ, axis=1)
    ext[i, x + 1 + cx, pl.ds(PAD_Y + row + cy, TILE), :] = value


def fill_messages(ext, direction, x_up, x_down, y_up, y_down):
    for sign, ring, message in ((1, CX + 1, x_up), (-1, 0, x_down)):
        for k, i in enumerate(moving(0, sign, direction)):
            message[pl.ds(k * CY, CY), :] = ext[i, ring, pl.ds(PAD_Y, CY), :]
            cy = direction * velocities[i][1]
            if cy == 1:
                message[pl.ds(80, 1), :] = ext[i, ring, pl.ds(PAD_Y + CY, 1), :]
            elif cy == -1:
                message[pl.ds(81, 1), :] = ext[i, ring, pl.ds(PAD_Y - 1, 1), :]
    for sign, ring, message in ((1, PAD_Y + CY, y_up), (-1, PAD_Y - 1, y_down)):
        for k, i in enumerate(moving(1, sign, direction)):
            for x in range(CX):
                message[pl.ds(k * CX + x, 1), :] = ext[i, x + 1, pl.ds(ring, 1), :]


def fill_ring(ext, direction, x_low, x_high, y_low, y_high):
    for sign, x, message in ((1, 1, x_low), (-1, CX, x_high)):
        for k, i in enumerate(moving(0, sign, direction)):
            ext[i, x, pl.ds(PAD_Y, CY), :] = message[pl.ds(k * CY, CY), :]
    for sign, row, message in ((1, PAD_Y, y_low), (-1, PAD_Y + CY - 1, y_high)):
        for k, i in enumerate(moving(1, sign, direction)):
            for x in range(CX):
                ext[i, x + 1, pl.ds(row, 1), :] = message[pl.ds(k * CX + x, 1), :]


def rows(yt):
    return pl.ds(yt * TILE, TILE)


def forward_kernel(f, porosity, porous, walls, ext, gap, frac, mask, vel, xu, xd, yu, yd):
    @pl.loop(0, CX)
    def _(x):
        for yt in range(CY // TILE):
            at = (x, rows(yt))
            pops = [f[i, x, rows(yt), :] for i in range(Q)]
            wall = walls[at] == 1
            panel = porous[at].astype(jnp.float32)
            fraction = jnp.where(wall, 1.0, panel * porosity[at])
            frac[at] = fraction
            mask[at] = jnp.where(wall, 0.0, panel)
            u, e, _ = off_equilibrium(pops)
            for axis in range(3):
                vel[axis, x, rows(yt), :] = u[axis]
            c = correction(e)
            for i in range(Q):
                relaxed = pops[i] - c[i]
                change = pops[opposite[i]] - relaxed
                gap[i, x, rows(yt), :] = change
                put_moved(ext, i, x, yt * TILE, relaxed + fraction * change, 1)

    fill_messages(ext, 1, xu, xd, yu, yd)


def corner_kernel(x_low, x_high, up_in, down_in, up, down, *, direction):
    ups, downs = moving(1, 1, direction), moving(1, -1, direction)
    for given, message, group, source in ((up_in, up, ups, 80), (down_in, down, downs, 81)):
        del given
        for k, i in enumerate(group):
            cx = direction * velocities[i][0]
            if cx == 1:
                message[pl.ds(k * CX, 1), :] = x_low[pl.ds(source, 1), :]
            elif cx == -1:
                message[pl.ds(k * CX + CX - 1, 1), :] = x_high[pl.ds(source, 1), :]


def late_kernel(
    ext_in, xl, xh, yl, yh, adjoint, frac, mask, ext, late, sens, xu, xd, yu, yd
):
    del ext_in
    fill_ring(ext, 1, xl, xh, yl, yh)

    @pl.loop(0, CX)
    def _(x):
        for yt in range(CY // TILE):
            at = (x, rows(yt))
            read = [ext[i, x + 1, pl.ds(PAD_Y + yt * TILE, TILE), :] for i in range(Q)]
            u, e, df = off_equilibrium(read)
            b = [adjoint[i, x, rows(yt), :] for i in range(Q)]
            t, db = covector(b)
            total = sum(t[k] * e[k] for k in t) - sum(p * q for p, q in zip(db, df))
            sens[at] = mask[at] * total
            out = pull_back(b, t, u, frac[at])
            for i in range(Q):
                put_moved(late, i, x, yt * TILE, out[i], -1)

    fill_messages(late, -1, xu, xd, yu, yd)


def early_sens_kernel(
    late_in, xl, xh, yl, yh, gap, mask, sens, owner_of, place, slot, late, send, scaled
):
    del late_in
    fill_ring(late, -1, xl, xh, yl, yh)

    @pl.loop(0, CX // 2)
    def _(xb):
        for yt in range(CY // TILE):
            total = jnp.zeros((TILE, NZ), jnp.float32)
            for half in range(2):
                x = xb * 2 + half
                dot = jnp.zeros((TILE, NZ), jnp.float32)
                for i in range(Q):
                    pulled = late[i, x + 1, pl.ds(PAD_Y + yt * TILE, TILE), :]
                    dot = dot + pulled * gap[i, x, rows(yt), :]
                total = total + sens[x, rows(yt)] + mask[x, rows(yt)] * dot
            line = pl.ds(pl.multiple_of(xb * CY + yt * TILE, TILE), TILE)
            sums = jnp.sum(total, axis=1, keepdims=True)
            scaled[line, :] = sums * place[line, :] + slot[line, :]

    send[...] = jnp.dot(
        owner_of[...],
        scaled[...],
        precision=lax.Precision.HIGHEST,
        preferred_element_type=jnp.float32,
    )


def adjoint_kernel(late, frac, vel, out, hold, sems):
    copies = []
    for x in range(CX):
        copies.append(
            pltpu.make_async_copy(hold.at[x], out.at[:, x], sems.at[x])
        )

    for x in range(CX):
        for yt in range(CY // TILE):
            at = (x, rows(yt))
            b = [late[i, x + 1, pl.ds(PAD_Y + yt * TILE, TILE), :] for i in range(Q)]
            t, _ = covector(b)
            u = [vel[axis, x, rows(yt), :] for axis in range(3)]
            result = pull_back(b, t, u, frac[at])
            for i in range(Q):
                hold[x, i, rows(yt), :] = result[i]
        copies[x].start()
    for copy in copies:
        copy.wait()


def routing_kernel(owners, slots, owner_of, place, slot):
    shape = (128, 128)
    row = lax.broadcasted_iota(jnp.int32, shape, 0)
    lane = lax.broadcasted_iota(jnp.int32, shape, 1)
    block = jnp.right_shift(row, 1)
    pick = lane == block
    owner_col = jnp.sum(jnp.where(pick, owners[...], 0.0), axis=1, keepdims=True)
    slot_col = jnp.sum(jnp.where(pick, slots[...], 0.0), axis=1, keepdims=True)
    owner_row = jnp.sum(jnp.where(row == lane, owner_col, 0.0), axis=0, keepdims=True)
    owner_of[...] = jnp.where(owner_row == row.astype(jnp.float32), 1.0, 0.0)
    earlier = (owner_row == owner_col) & (jnp.right_shift(lane, 1) < block)
    rank = 0.5 * jnp.sum(jnp.where(earlier, 1.0, 0.0), axis=1, keepdims=True)
    number = lane.astype(jnp.float32)
    place[...] = jnp.where(number == rank, 1.0, 0.0)
    first = (row & 1) == 0
    slot[...] = jnp.where(first & (number == rank + SLOT_LANE), slot_col, 0.0)


def owner_kernel(got, out):
    patch = lax.broadcasted_iota(jnp.int32, (DEVICES, PATCH_DEV), 1).astype(jnp.float32)
    data = got[...]
    total = jnp.zeros((DEVICES, PATCH_DEV), jnp.float32)
    for k in range(2):
        hit = data[:, SLOT_LANE + k : SLOT_LANE + k + 1] == patch
        total = total + jnp.where(hit, data[:, k : k + 1], 0.0)
    out[...] = jnp.sum(total, axis=0, keepdims=True)


VMEM = pl.BlockSpec(memory_space=pltpu.VMEM)
LIMIT = 6 * 2**20


def vmem(*shape):
    return pltpu.VMEM(shape, jnp.float32)


def call(kernel, ins, outs, scratch=(), aliases=None, flops=0):
    held = [pltpu.with_memory_space_constraint(x, pltpu.VMEM) for x in ins]
    return pl.pallas_call(
        kernel,
        out_shape=outs,
        in_specs=[VMEM] * len(ins),
        out_specs=[VMEM] * len(outs),
        scratch_shapes=list(scratch),
        input_output_aliases=aliases or {},
        compiler_params=pltpu.CompilerParams(vmem_limit_bytes=LIMIT),
        cost_estimate=pl.CostEstimate(flops=flops, bytes_accessed=0, transcendentals=0),
    )(*held)


EXT = vmem(Q, CX + 2, EXT_Y, NZ)
FIELD = vmem(Q, CX, CY, NZ)
NODE = vmem(CX, CY, NZ)
X_MESSAGE = vmem(88, NZ)
Y_MESSAGE = vmem(80, NZ)
SQUARE = vmem(128, 128)


def shift(block, axis, step):
    count = lax.axis_size(axis)
    return lax.ppermute(block, axis, [(i, (i + step) % count) for i in range(count)])


def exchange(messages, direction):
    x_up, x_down, y_up, y_down = messages
    x_low = shift(x_up, "gx", 1)
    x_high = shift(x_down, "gx", -1)
    y_up, y_down = call(
        functools.partial(corner_kernel, direction=direction),
        [x_low, x_high, y_up, y_down],
        [Y_MESSAGE, Y_MESSAGE],
        aliases={2: 0, 3: 1},
    )
    y_low = shift(y_up, "gy", 1)
    y_high = shift(y_down, "gy", -1)
    return x_low, x_high, y_low, y_high


def body(populations, porosity, adjoint_in, porous, walls, owners, slots):
    owner_row = jnp.pad(owners.reshape(1, 64).astype(jnp.float32), ((0, 0), (0, 64)))
    slot_row = jnp.pad(slots.reshape(1, 64).astype(jnp.float32), ((0, 0), (0, 64)))
    ext, gap, frac, mask, vel, *messages = call(
        forward_kernel,
        [populations, porosity, porous, walls],
        [EXT, FIELD, NODE, NODE, vmem(3, CX, CY, NZ)] + [X_MESSAGE] * 2 + [Y_MESSAGE] * 2,
    )
    halos = exchange(messages, 1)
    owner_of, place, slot = call(routing_kernel, [owner_row, slot_row], [SQUARE] * 3)
    _, late, sens, *messages = call(
        late_kernel,
        [ext, *halos, adjoint_in, frac, mask],
        [EXT, EXT, NODE] + [X_MESSAGE] * 2 + [Y_MESSAGE] * 2,
        aliases={0: 0},
    )
    halos = exchange(messages, -1)
    late, send = call(
        early_sens_kernel,
        [late, *halos, gap, mask, sens, owner_of, place, slot],
        [EXT, SQUARE],
        scratch=[pltpu.VMEM((128, 128), jnp.float32)],
        aliases={0: 0},
    )
    got = lax.all_to_all(send, ("gx", "gy"), split_axis=0, concat_axis=0, tiled=True)
    held = [pltpu.with_memory_space_constraint(x, pltpu.VMEM) for x in (late, frac, vel)]
    adjoint_out = pl.pallas_call(
        adjoint_kernel,
        out_shape=jax.ShapeDtypeStruct((Q, CX, CY, NZ), jnp.float32),
        in_specs=[VMEM] * 3,
        out_specs=pl.BlockSpec(memory_space=pl.ANY),
        scratch_shapes=[
            pltpu.VMEM((CX, Q, CY, NZ), jnp.float32),
            pltpu.SemaphoreType.DMA((CX,)),
        ],
        compiler_params=pltpu.CompilerParams(vmem_limit_bytes=LIMIT),
        cost_estimate=pl.CostEstimate(
            flops=20_000_000, bytes_accessed=5_000_000, transcendentals=0
        ),
    )(*held)
    (patch,) = call(owner_kernel, [got], [vmem(1, PATCH_DEV)])
    return adjoint_out, patch.reshape(PATCH_DEV)


def solution(mesh):
    return jax.shard_map(
        body,
        mesh=mesh,
        in_specs=(
            P(None, "gx", "gy", None),
            P("gx", "gy", None),
            P(None, "gx", "gy", None),
            P("gx", "gy", None),
            P("gx", "gy", None),
            P("gx", "gy", None, None),
            P("gx", "gy", None),
        ),
        out_specs=(P(None, "gx", "gy", None), P(("gx", "gy"))),
        check_vma=False,
    )
```

```python
import functools

import jax
import jax.numpy as jnp
from jax import lax
from jax.experimental import pallas as pl
from jax.experimental.pallas import tpu as pltpu
from jax.sharding import PartitionSpec as P

Q = 19
CX = 16
CY = 16
NZ = 128
TILE = 8
PAD_Y = 8
EXT_Y = 32
EXT_XB = 10
BLOCK_ROWS = EXT_XB * EXT_Y
DEVICES = 128
PATCH_DEV = 256
SLOT_LANE = 64
FACE = 80
META = 160
MESSAGE_ROWS = 168

velocities = [
    (0, 0, 0),
    (1, 0, 0),
    (-1, 0, 0),
    (0, 1, 0),
    (0, -1, 0),
    (0, 0, 1),
    (0, 0, -1),
    (1, 1, 0),
    (-1, -1, 0),
    (1, -1, 0),
    (-1, 1, 0),
    (1, 0, 1),
    (-1, 0, -1),
    (1, 0, -1),
    (-1, 0, 1),
    (0, 1, 1),
    (0, -1, -1),
    (0, 1, -1),
    (0, -1, 1),
]
opposite = [0, 2, 1, 4, 3, 6, 5, 8, 7, 10, 9, 12, 11, 14, 13, 16, 15, 18, 17]
RATE2, RATE3, RATE4 = 1.25, 1.5, 1.4


def moving(axis, sign, direction):
    return [i for i in range(Q) if direction * velocities[i][axis] == sign]


def edge(f, first):
    s, d = f[first] + f[first + 1], f[first] - f[first + 1]
    s2, d2 = f[first + 2] + f[first + 3], f[first + 2] - f[first + 3]
    return s, d, s2, d2


def off_equilibrium(f):
    sx, dx = f[1] + f[2], f[1] - f[2]
    sy, dy = f[3] + f[4], f[3] - f[4]
    sz, dz = f[5] + f[6], f[5] - f[6]
    s7, d7, s9, d9 = edge(f, 7)
    s11, d11, s13, d13 = edge(f, 11)
    s15, d15, s17, d17 = edge(f, 15)
    m220, m110, m120, m210 = s7 + s9, s7 - s9, d7 + d9, d7 - d9
    m202, m101, m102, m201 = s11 + s13, s11 - s13, d11 + d13, d11 - d13
    m022, m011, m012, m021 = s15 + s17, s15 - s17, d15 + d17, d15 - d17
    m200, m020, m002 = sx + m220 + m202, sy + m220 + m022, sz + m202 + m022
    jx, jy, jz = dx + (m120 + m102), dy + (m210 + m012), dz + (m201 + m021)
    rho = f[0] + (sx + sy + sz) + (m220 + m202 + m022)
    inv = 1.0 / rho
    ux, uy, uz = jx * inv, jy * inv, jz * inv
    qx, qy, qz = jx * ux, jy * uy, jz * uz
    third = rho * (1.0 / 3.0)
    ninth = rho * (1.0 / 9.0) - (qx + qy + qz) * (1.0 / 6.0)
    tx, ty, tz = jx * (1.0 / 3.0), jy * (1.0 / 3.0), jz * (1.0 / 3.0)
    e = {
        "200": RATE2 * (m200 - third - qx),
        "020": RATE2 * (m020 - third - qy),
        "002": RATE2 * (m002 - third - qz),
        "110": RATE2 * (m110 - jx * uy),
        "101": RATE2 * (m101 - jx * uz),
        "011": RATE2 * (m011 - jy * uz),
        "120": RATE3 * (m120 - tx),
        "102": RATE3 * (m102 - tx),
        "210": RATE3 * (m210 - ty),
        "012": RATE3 * (m012 - ty),
        "201": RATE3 * (m201 - tz),
        "021": RATE3 * (m021 - tz),
        "220": RATE4 * (m220 - ninth - 0.5 * (qx + qy)),
        "202": RATE4 * (m202 - ninth - 0.5 * (qx + qz)),
        "022": RATE4 * (m022 - ninth - 0.5 * (qy + qz)),
    }
    return (ux, uy, uz), e, (dx, dy, dz, d7, d9, d11, d13, d15, d17)


def spread(t, g, a, b):
    even, odd = t + g, t - g
    plus, minus = a + b, a - b
    return [even + plus, even - plus, odd + minus, odd - minus]


def correction(e):
    q = {k: 0.25 * v for k, v in e.items()}
    xy = spread(q["220"], q["110"], q["120"], q["210"])
    xz = spread(q["202"], q["101"], q["102"], q["201"])
    yz = spread(q["022"], q["011"], q["012"], q["021"])
    faces = []
    for second, fourth, odd in (
        ("200", ("220", "202"), ("120", "102")),
        ("020", ("220", "022"), ("210", "012")),
        ("002", ("202", "022"), ("201", "021")),
    ):
        mean = 0.5 * e[second] - 2.0 * (q[fourth[0]] + q[fourth[1]])
        lean = 2.0 * (q[odd[0]] + q[odd[1]])
        faces += [mean - lean, mean + lean]
    rest = (e["220"] + e["202"] + e["022"]) - (e["200"] + e["020"] + e["002"])
    return [rest] + faces + xy + xz + yz


def covector(b):
    hx, dx = 0.5 * (b[1] + b[2]), b[1] - b[2]
    hy, dy = 0.5 * (b[3] + b[4]), b[3] - b[4]
    hz, dz = 0.5 * (b[5] + b[6]), b[5] - b[6]
    s7, d7, s9, d9 = edge(b, 7)
    s11, d11, s13, d13 = edge(b, 11)
    s15, d15, s17, d17 = edge(b, 15)
    gx, gy, gz = hx - b[0], hy - b[0], hz - b[0]
    kx, ky, kz = 0.5 * dx, 0.5 * dy, 0.5 * dz
    t = {
        "200": gx,
        "020": gy,
        "002": gz,
        "110": 0.25 * (s7 - s9),
        "101": 0.25 * (s11 - s13),
        "011": 0.25 * (s15 - s17),
        "120": 0.25 * (d7 + d9) - kx,
        "102": 0.25 * (d11 + d13) - kx,
        "210": 0.25 * (d7 - d9) - ky,
        "012": 0.25 * (d15 + d17) - ky,
        "201": 0.25 * (d11 - d13) - kz,
        "021": 0.25 * (d15 - d17) - kz,
        "220": 0.25 * (s7 + s9) - gx - hy,
        "202": 0.25 * (s11 + s13) - gx - hz,
        "022": 0.25 * (s15 + s17) - gy - hz,
    }
    return t, (dx, dy, dz, d7, d9, d11, d13, d15, d17)


def pull_back(b, t, u, fraction):
    rates = {k: (RATE2, RATE3, RATE4)[sum(map(int, k)) - 2] for k in t}
    n = {k: rates[k] * v for k, v in t.items()}
    ux, uy, uz = u
    fourth = n["220"] + n["202"] + n["022"]
    second = n["200"] + n["020"] + n["002"]
    part = fourth * (1.0 / 3.0)
    ax = n["200"] + part - 0.5 * n["022"]
    ay = n["020"] + part - 0.5 * n["202"]
    az = n["002"] + part - 0.5 * n["220"]
    rx = 2.0 * ax * ux + n["110"] * uy + n["101"] * uz
    ry = 2.0 * ay * uy + n["110"] * ux + n["011"] * uz
    rz = 2.0 * az * uz + n["101"] * ux + n["011"] * uy
    p0 = second * (1.0 / 3.0) + fourth * (1.0 / 9.0) - 0.5 * (rx * ux + ry * uy + rz * uz)
    px = rx + (n["120"] + n["102"]) * (1.0 / 3.0)
    py = ry + (n["210"] + n["012"]) * (1.0 / 3.0)
    pz = rz + (n["201"] + n["021"]) * (1.0 / 3.0)
    ex, ey, ez = p0 - n["200"], p0 - n["020"], p0 - n["002"]
    h = [p0, ex + px, ex - px, ey + py, ey - py, ez + pz, ez - pz]
    h += spread(ex - n["020"] - n["220"], -n["110"], px - n["120"], py - n["210"])
    h += spread(ex - n["002"] - n["202"], -n["101"], px - n["102"], pz - n["201"])
    h += spread(ey - n["002"] - n["022"], -n["011"], py - n["012"], pz - n["021"])
    open_part = 1.0 - fraction
    return [open_part * (b[i] + h[i]) + fraction * b[opposite[i]] for i in range(Q)]


def put_moved(field, i, x, yt, value, direction):
    cx, cy, cz = (direction * c for c in velocities[i])
    if cz:
        value = pltpu.roll(value, cz % NZ, axis=1)
    x = (x + cx) & (CX - 1) if cx else x
    row = yt * TILE + cy
    if row < 0:
        field[i, x, pl.ds(0, TILE - 1), :] = value[1:]
        field[i, x, pl.ds(CY - 1, 1), :] = value[:1]
    elif row + TILE > CY:
        field[i, x, pl.ds(row, TILE - 1), :] = value[:-1]
        field[i, x, pl.ds(0, 1), :] = value[-1:]
    else:
        field[i, x, pl.ds(row, TILE), :] = value


def fill_messages(fields, direction, x_up, x_down, y_up, y_down):
    for n, field in enumerate(fields):
        for sign, x, message in ((1, 0, x_up), (-1, CX - 1, x_down)):
            for k, i in enumerate(moving(0, sign, direction)):
                message[pl.ds(n * FACE + k * CY, CY), :] = field[i, x]
        for sign, row, message in ((1, 0, y_up), (-1, CY - 1, y_down)):
            for k, i in enumerate(moving(1, sign, direction)):
                for x in range(CX):
                    message[pl.ds(n * FACE + k * CX + x, 1), :] = field[i, x, pl.ds(row, 1), :]


def fill_ring(fields, direction, x_low, x_high, y_low, y_high):
    for n, field in enumerate(fields):
        for sign, x, message in ((1, 0, x_low), (-1, CX - 1, x_high)):
            for k, i in enumerate(moving(0, sign, direction)):
                field[i, x] = message[pl.ds(n * FACE + k * CY, CY), :]
        for sign, row, message in ((1, 0, y_low), (-1, CY - 1, y_high)):
            for k, i in enumerate(moving(1, sign, direction)):
                for x in range(CX):
                    field[i, x, pl.ds(row, 1), :] = message[pl.ds(n * FACE + k * CX + x, 1), :]


def rows(yt):
    return pl.ds(yt * TILE, TILE)


def iota(shape, dim):
    return lax.broadcasted_iota(jnp.int32, shape, dim)


def column(row, pick):
    return jnp.sum(jnp.where(pick, row, 0.0), axis=1, keepdims=True)


def block_numbers(owners, slots, table, x_up, x_down, y_up, y_down):
    shape = (64, 64)
    row, lane = iota(shape, 0), iota(shape, 1)
    same = row == lane
    owner_row, slot_row = owners[...].astype(jnp.float32), slots[...].astype(jnp.float32)
    owner_col = column(owner_row, same)
    earlier = (owner_row == owner_col) & (lane < row)
    rank = jnp.sum(jnp.where(earlier, 1.0, 0.0), axis=1, keepdims=True)
    number = owner_col * 1024.0 + column(slot_row, same) * 4.0 + rank
    wide = (64, NZ)
    spot = iota(wide, 1) == (iota(wide, 0) & 7) + 1
    spread_out = jnp.where(spot, number, 0.0)
    table[...] = jnp.zeros((16, NZ), jnp.float32)
    for xb in range(8):
        line = jnp.sum(spread_out[xb * 8 : xb * 8 + 8], axis=0, keepdims=True)
        table[pl.ds(xb + 1, 1), :] = line
    held = table[...]
    x_up[pl.ds(META, 1), :] = held[8:9]
    x_down[pl.ds(META, 1), :] = held[1:2]
    eye = iota((16, NZ), 0) == iota((16, NZ), 1)
    for yb, message in ((8, y_up), (1, y_down)):
        part = jnp.where(eye, held[:, yb : yb + 1], 0.0)
        message[pl.ds(META, 1), :] = jnp.sum(part, axis=0, keepdims=True)


def forward_kernel(
    f_hbm, porosity_hbm, adjoint_hbm, porous_hbm, walls_hbm, owners_hbm, slots_hbm,
    moved, gap, adjoint, frac, mask, vel, table, xu, xd, yu, yd,
    f, porosity, porous, walls, owners, slots, f_sems, sems,
):
    def plane(x):
        return pltpu.make_async_copy(f_hbm.at[:, x], f.at[:, x], f_sems.at[x])

    small = [
        pltpu.make_async_copy(source, target, sems.at[k])
        for k, (source, target) in enumerate(
            (
                (owners_hbm, owners),
                (slots_hbm, slots),
                (porosity_hbm, porosity),
                (porous_hbm, porous),
                (walls_hbm, walls),
            )
        )
    ]
    later = pltpu.make_async_copy(adjoint_hbm, adjoint, sems.at[5])
    for copy in small:
        copy.start()
    for x in range(CX):
        plane(x).start()
    later.start()
    small[0].wait()
    small[1].wait()
    block_numbers(owners, slots, table, xu, xd, yu, yd)
    for copy in small[2:]:
        copy.wait()

    @pl.loop(0, CX)
    def _(x):
        plane(x).wait()
        for yt in range(CY // TILE):
            at = (x, rows(yt))
            pops = [f[i, x, rows(yt), :] for i in range(Q)]
            wall = walls[at] == 1
            panel = porous[at].astype(jnp.float32)
            fraction = jnp.where(wall, 1.0, panel * porosity[at])
            open_panel = jnp.where(wall, 0.0, panel)
            frac[at] = fraction
            mask[at] = open_panel
            u, e, _ = off_equilibrium(pops)
            for axis in range(3):
                vel[axis, x, rows(yt), :] = u[axis]
            c = correction(e)
            for i in range(Q):
                relaxed = pops[i] - c[i]
                change = pops[opposite[i]] - relaxed
                put_moved(gap, i, x, yt, open_panel * change, 1)
                put_moved(moved, i, x, yt, relaxed + fraction * change, 1)

    fill_messages((moved, gap), 1, xu, xd, yu, yd)
    later.wait()


def corner_kernel(x_low, x_high, up_in, down_in, up, down, *, direction, fields):
    del up_in, down_in
    for sign, row, message in ((1, 0, up), (-1, CY - 1, down)):
        for k, i in enumerate(moving(1, sign, direction)):
            cx = direction * velocities[i][0]
            if not cx:
                continue
            source, x = (x_low, 0) if cx == 1 else (x_high, CX - 1)
            k_x = moving(0, cx, direction).index(i)
            for n in range(fields):
                message[pl.ds(n * FACE + k * CX + x, 1), :] = source[
                    pl.ds(n * FACE + k_x * CY + row, 1), :
                ]
    if fields == 2:
        lane = iota((1, NZ), 1)
        for yb, message in ((8, up), (1, down)):
            low = jnp.sum(jnp.where(lane == yb, x_low[pl.ds(META, 1), :], 0.0))
            high = jnp.sum(jnp.where(lane == yb, x_high[pl.ds(META, 1), :], 0.0))
            line = message[pl.ds(META, 1), :]
            line = jnp.where(lane == 0, low, jnp.where(lane == 9, high, line))
            message[pl.ds(META, 1), :] = line


def routing_kernel(table, x_low, x_high, y_low, y_high, owner_of, place, slot, ext):
    shape = (16, NZ)
    row, lane = iota(shape, 0), iota(shape, 1)
    eye = row == lane
    low = column(y_low[pl.ds(META, 1), :], eye)
    high = column(y_high[pl.ds(META, 1), :], eye)
    held = jnp.where(row == 0, x_low[pl.ds(META, 1), :], table[...])
    held = jnp.where(row == 9, x_high[pl.ds(META, 1), :], held)
    ext[...] = jnp.where(lane == 0, low, jnp.where(lane == 9, high, held))
    shape = (EXT_Y, NZ)
    row, lane = iota(shape, 0), iota(shape, 1)
    yb = jnp.right_shift(row - 6, 1)
    pick = lane == yb
    side_y = jnp.where(yb == 0, 0, jnp.where(yb == 9, 2, 1))
    used = (row >= PAD_Y - 1) & (row <= PAD_Y + CY)
    first = used & ((yb == 0) | ((row & 1) == 0))
    for xb in range(EXT_XB):
        number = column(ext[pl.ds(xb, 1), :], pick).astype(jnp.int32)
        side = side_y * 6 + (0 if xb == 0 else 4 if xb == 9 else 2)
        spot = side + (number & 3)
        line = pl.ds(xb * EXT_Y, EXT_Y)
        owner_of[line, :] = jnp.where(used & (lane == jnp.right_shift(number, 10)), 1.0, 0.0)
        place[line, :] = jnp.where(lane == spot, 1.0, 0.0)
        patch = (jnp.right_shift(number, 2) & 255).astype(jnp.float32)
        slot[line, :] = jnp.where(first & (lane == spot + SLOT_LANE), patch, 0.0)


def late_kernel(
    moved_in, gap_in, xl, xh, yl, yh, adjoint, frac, mask, owner_of, place, slot,
    moved, gap, late, send, xu, xd, yu, yd, sums, scaled,
):
    del moved_in, gap_in
    fill_ring((moved, gap), 1, xl, xh, yl, yh)
    sums[...] = jnp.zeros((EXT_XB, EXT_Y, NZ), jnp.float32)

    @pl.loop(0, CX // 2)
    def _(xb):
        for yt in range(CY // TILE):
            parts = {}
            for half in range(2):
                x = xb * 2 + half
                at = (x, rows(yt))
                read = [moved[i, x, rows(yt), :] for i in range(Q)]
                u, e, df = off_equilibrium(read)
                b = [adjoint[i, x, rows(yt), :] for i in range(Q)]
                t, db = covector(b)
                total = sum(t[k] * e[k] for k in t) - sum(p * q for p, q in zip(db, df))
                total = mask[at] * total
                out = pull_back(b, t, u, frac[at])
                key = (0, 0)
                parts[key] = parts[key] + total if key in parts else total
                for i in range(Q):
                    cx, cy, _ = velocities[i]
                    key = ((half - cx) // 2, cy)
                    early = out[i] * gap[i, x, rows(yt), :]
                    parts[key] = parts[key] + early if key in parts else early
                    put_moved(late, i, x, yt, out[i], -1)
            for (step, cy), part in parts.items():
                at = (xb + 1 + step, pl.ds(PAD_Y + yt * TILE - cy, TILE))
                sums[at] = sums[at] + part

    for xb in range(EXT_XB):
        line = pl.ds(xb * EXT_Y, EXT_Y)
        scaled[line, :] = (
            jnp.sum(sums[xb], axis=1, keepdims=True) * place[line, :] + slot[line, :]
        )
    send[...] = lax.dot_general(
        owner_of[...],
        scaled[...],
        (((0,), (0,)), ((), ())),
        precision=lax.Precision.HIGHEST,
        preferred_element_type=jnp.float32,
    )
    fill_messages((late,), -1, xu, xd, yu, yd)


def early_kernel(late_in, xl, xh, yl, yh, frac, vel, late, out, hold, sems):
    del late_in
    fill_ring((late,), -1, xl, xh, yl, yh)

    def plane(x):
        return pltpu.make_async_copy(hold.at[x], out.at[:, x], sems.at[x])

    @pl.loop(0, CX)
    def _(x):
        for yt in range(CY // TILE):
            b = [late[i, x, rows(yt), :] for i in range(Q)]
            t, _ = covector(b)
            u = [vel[axis, x, rows(yt), :] for axis in range(3)]
            result = pull_back(b, t, u, frac[x, rows(yt)])
            for i in range(Q):
                hold[x, i, rows(yt), :] = result[i]
        plane(x).start()

    for x in range(CX):
        plane(x).wait()


def owner_kernel(got, out):
    patch = iota((DEVICES, PATCH_DEV), 1).astype(jnp.float32)
    data = got[...]
    total = jnp.zeros((DEVICES, PATCH_DEV), jnp.float32)
    for k in range(18):
        hit = data[:, SLOT_LANE + k : SLOT_LANE + k + 1] == patch
        total = total + jnp.where(hit, data[:, k : k + 1], 0.0)
    out[...] = jnp.sum(total, axis=0, keepdims=True)


VMEM = pl.BlockSpec(memory_space=pltpu.VMEM)
ANY = pl.BlockSpec(memory_space=pl.ANY)
LIMIT = 8 * 2**20


def vmem(*shape):
    return pltpu.VMEM(shape, jnp.float32)


def call(kernel, ins, outs, scratch=(), aliases=None, flops=0, hbm_ins=0, hbm_outs=()):
    held = list(ins[:hbm_ins])
    held += [pltpu.with_memory_space_constraint(x, pltpu.VMEM) for x in ins[hbm_ins:]]
    return pl.pallas_call(
        kernel,
        out_shape=[*outs, *hbm_outs],
        in_specs=[ANY] * hbm_ins + [VMEM] * (len(ins) - hbm_ins),
        out_specs=[VMEM] * len(outs) + [ANY] * len(hbm_outs),
        scratch_shapes=list(scratch),
        input_output_aliases=aliases or {},
        compiler_params=pltpu.CompilerParams(vmem_limit_bytes=LIMIT),
        cost_estimate=pl.CostEstimate(flops=flops, bytes_accessed=0, transcendentals=0),
    )(*held)


FIELD = vmem(Q, CX, CY, NZ)
NODE = vmem(CX, CY, NZ)
MESSAGE = vmem(MESSAGE_ROWS, NZ)
SHORT_MESSAGE = vmem(FACE, NZ)
LINES = vmem(BLOCK_ROWS, NZ)


def shift(block, axis, step):
    count = lax.axis_size(axis)
    return lax.ppermute(block, axis, [(i, (i + step) % count) for i in range(count)])


def exchange(messages, direction, fields):
    x_up, x_down, y_up, y_down = messages
    x_low = shift(x_up, "gx", 1)
    x_high = shift(x_down, "gx", -1)
    y_up, y_down = call(
        functools.partial(corner_kernel, direction=direction, fields=fields),
        [x_low, x_high, y_up, y_down],
        [MESSAGE if fields == 2 else SHORT_MESSAGE] * 2,
        aliases={2: 0, 3: 1},
    )
    y_low = shift(y_up, "gy", 1)
    y_high = shift(y_down, "gy", -1)
    return x_low, x_high, y_low, y_high


def body(populations, porosity, adjoint_in, porous, walls, owners, slots):
    ints = pltpu.VMEM((CX, CY, NZ), jnp.int32)
    moved, gap, adjoint, frac, mask, vel, table, *messages = call(
        forward_kernel,
        [populations, porosity, adjoint_in, porous, walls]
        + [owners.reshape(1, 64), slots.reshape(1, 64)],
        [FIELD] * 3 + [NODE] * 2 + [vmem(3, CX, CY, NZ), vmem(16, NZ)] + [MESSAGE] * 4,
        scratch=[FIELD, NODE, ints, ints]
        + [pltpu.VMEM((1, 64), jnp.int32)] * 2
        + [pltpu.SemaphoreType.DMA((CX,)), pltpu.SemaphoreType.DMA((6,))],
        hbm_ins=7,
    )
    halos = exchange(messages, 1, 2)
    owner_of, place, slot = call(
        routing_kernel, [table, *halos], [LINES] * 3, scratch=[vmem(16, NZ)]
    )
    _, _, late, send, *messages = call(
        late_kernel,
        [moved, gap, *halos, adjoint, frac, mask, owner_of, place, slot],
        [FIELD] * 3 + [vmem(DEVICES, NZ)] + [SHORT_MESSAGE] * 4,
        scratch=[vmem(EXT_XB, EXT_Y, NZ), LINES],
        aliases={0: 0, 1: 1},
    )
    got = lax.all_to_all(send, ("gx", "gy"), split_axis=0, concat_axis=0, tiled=True)
    halos = exchange(messages, -1, 1)
    _, adjoint_out = call(
        early_kernel,
        [late, *halos, frac, vel],
        [FIELD],
        hbm_outs=[jax.ShapeDtypeStruct((Q, CX, CY, NZ), jnp.float32)],
        scratch=[vmem(CX, Q, CY, NZ), pltpu.SemaphoreType.DMA((CX,))],
        aliases={0: 0},
    )
    (patch,) = call(owner_kernel, [got], [vmem(1, PATCH_DEV)])
    return adjoint_out, patch.reshape(PATCH_DEV)


def solution(mesh):
    return jax.shard_map(
        body,
        mesh=mesh,
        in_specs=(
            P(None, "gx", "gy", None),
            P("gx", "gy", None),
            P(None, "gx", "gy", None),
            P("gx", "gy", None),
            P("gx", "gy", None),
            P("gx", "gy", None, None),
            P("gx", "gy", None),
        ),
        out_specs=(P(None, "gx", "gy", None), P(("gx", "gy"))),
        check_vma=False,
    )
```

```python
import functools

import jax
import jax.numpy as jnp
from jax import lax
from jax.experimental import pallas as pl
from jax.experimental.pallas import tpu as pltpu
from jax.sharding import PartitionSpec as P

Q = 19
CX = 16
CY = 16
NZ = 128
TILE = 8
PAD_Y = 8
EXT_Y = 32
EXT_XB = 10
BLOCK_ROWS = EXT_XB * EXT_Y
DEVICES = 128
PATCH_DEV = 256
SLOT_LANE = 64
FACE = 80
META = 160
MESSAGE_ROWS = 168

velocities = [
    (0, 0, 0),
    (1, 0, 0),
    (-1, 0, 0),
    (0, 1, 0),
    (0, -1, 0),
    (0, 0, 1),
    (0, 0, -1),
    (1, 1, 0),
    (-1, -1, 0),
    (1, -1, 0),
    (-1, 1, 0),
    (1, 0, 1),
    (-1, 0, -1),
    (1, 0, -1),
    (-1, 0, 1),
    (0, 1, 1),
    (0, -1, -1),
    (0, 1, -1),
    (0, -1, 1),
]
opposite = [0, 2, 1, 4, 3, 6, 5, 8, 7, 10, 9, 12, 11, 14, 13, 16, 15, 18, 17]
RATE2, RATE3, RATE4 = 1.25, 1.5, 1.4


def moving(axis, sign, direction):
    return [i for i in range(Q) if direction * velocities[i][axis] == sign]


def edge(f, first):
    s, d = f[first] + f[first + 1], f[first] - f[first + 1]
    s2, d2 = f[first + 2] + f[first + 3], f[first + 2] - f[first + 3]
    return s, d, s2, d2


def off_equilibrium(f):
    sx, dx = f[1] + f[2], f[1] - f[2]
    sy, dy = f[3] + f[4], f[3] - f[4]
    sz, dz = f[5] + f[6], f[5] - f[6]
    s7, d7, s9, d9 = edge(f, 7)
    s11, d11, s13, d13 = edge(f, 11)
    s15, d15, s17, d17 = edge(f, 15)
    m220, m110, m120, m210 = s7 + s9, s7 - s9, d7 + d9, d7 - d9
    m202, m101, m102, m201 = s11 + s13, s11 - s13, d11 + d13, d11 - d13
    m022, m011, m012, m021 = s15 + s17, s15 - s17, d15 + d17, d15 - d17
    m200, m020, m002 = sx + m220 + m202, sy + m220 + m022, sz + m202 + m022
    jx, jy, jz = dx + (m120 + m102), dy + (m210 + m012), dz + (m201 + m021)
    rho = f[0] + (sx + sy + sz) + (m220 + m202 + m022)
    inv = 1.0 / rho
    ux, uy, uz = jx * inv, jy * inv, jz * inv
    qx, qy, qz = jx * ux, jy * uy, jz * uz
    third = rho * (1.0 / 3.0)
    ninth = rho * (1.0 / 9.0) - (qx + qy + qz) * (1.0 / 6.0)
    tx, ty, tz = jx * (1.0 / 3.0), jy * (1.0 / 3.0), jz * (1.0 / 3.0)
    e = {
        "200": RATE2 * (m200 - third - qx),
        "020": RATE2 * (m020 - third - qy),
        "002": RATE2 * (m002 - third - qz),
        "110": RATE2 * (m110 - jx * uy),
        "101": RATE2 * (m101 - jx * uz),
        "011": RATE2 * (m011 - jy * uz),
        "120": RATE3 * (m120 - tx),
        "102": RATE3 * (m102 - tx),
        "210": RATE3 * (m210 - ty),
        "012": RATE3 * (m012 - ty),
        "201": RATE3 * (m201 - tz),
        "021": RATE3 * (m021 - tz),
        "220": RATE4 * (m220 - ninth - 0.5 * (qx + qy)),
        "202": RATE4 * (m202 - ninth - 0.5 * (qx + qz)),
        "022": RATE4 * (m022 - ninth - 0.5 * (qy + qz)),
    }
    return (ux, uy, uz), e, (dx, dy, dz, d7, d9, d11, d13, d15, d17)


def spread(t, g, a, b):
    even, odd = t + g, t - g
    plus, minus = a + b, a - b
    return [even + plus, even - plus, odd + minus, odd - minus]


def correction(e):
    q = {k: 0.25 * v for k, v in e.items()}
    xy = spread(q["220"], q["110"], q["120"], q["210"])
    xz = spread(q["202"], q["101"], q["102"], q["201"])
    yz = spread(q["022"], q["011"], q["012"], q["021"])
    faces = []
    for second, fourth, odd in (
        ("200", ("220", "202"), ("120", "102")),
        ("020", ("220", "022"), ("210", "012")),
        ("002", ("202", "022"), ("201", "021")),
    ):
        mean = 0.5 * e[second] - 2.0 * (q[fourth[0]] + q[fourth[1]])
        lean = 2.0 * (q[odd[0]] + q[odd[1]])
        faces += [mean - lean, mean + lean]
    rest = (e["220"] + e["202"] + e["022"]) - (e["200"] + e["020"] + e["002"])
    return [rest] + faces + xy + xz + yz


def covector(b):
    hx, dx = 0.5 * (b[1] + b[2]), b[1] - b[2]
    hy, dy = 0.5 * (b[3] + b[4]), b[3] - b[4]
    hz, dz = 0.5 * (b[5] + b[6]), b[5] - b[6]
    s7, d7, s9, d9 = edge(b, 7)
    s11, d11, s13, d13 = edge(b, 11)
    s15, d15, s17, d17 = edge(b, 15)
    gx, gy, gz = hx - b[0], hy - b[0], hz - b[0]
    kx, ky, kz = 0.5 * dx, 0.5 * dy, 0.5 * dz
    t = {
        "200": gx,
        "020": gy,
        "002": gz,
        "110": 0.25 * (s7 - s9),
        "101": 0.25 * (s11 - s13),
        "011": 0.25 * (s15 - s17),
        "120": 0.25 * (d7 + d9) - kx,
        "102": 0.25 * (d11 + d13) - kx,
        "210": 0.25 * (d7 - d9) - ky,
        "012": 0.25 * (d15 + d17) - ky,
        "201": 0.25 * (d11 - d13) - kz,
        "021": 0.25 * (d15 - d17) - kz,
        "220": 0.25 * (s7 + s9) - gx - hy,
        "202": 0.25 * (s11 + s13) - gx - hz,
        "022": 0.25 * (s15 + s17) - gy - hz,
    }
    return t, (dx, dy, dz, d7, d9, d11, d13, d15, d17)


def pull_back(b, t, u, fraction):
    rates = {k: (RATE2, RATE3, RATE4)[sum(map(int, k)) - 2] for k in t}
    n = {k: rates[k] * v for k, v in t.items()}
    ux, uy, uz = u
    fourth = n["220"] + n["202"] + n["022"]
    second = n["200"] + n["020"] + n["002"]
    part = fourth * (1.0 / 3.0)
    ax = n["200"] + part - 0.5 * n["022"]
    ay = n["020"] + part - 0.5 * n["202"]
    az = n["002"] + part - 0.5 * n["220"]
    rx = 2.0 * ax * ux + n["110"] * uy + n["101"] * uz
    ry = 2.0 * ay * uy + n["110"] * ux + n["011"] * uz
    rz = 2.0 * az * uz + n["101"] * ux + n["011"] * uy
    p0 = second * (1.0 / 3.0) + fourth * (1.0 / 9.0) - 0.5 * (rx * ux + ry * uy + rz * uz)
    px = rx + (n["120"] + n["102"]) * (1.0 / 3.0)
    py = ry + (n["210"] + n["012"]) * (1.0 / 3.0)
    pz = rz + (n["201"] + n["021"]) * (1.0 / 3.0)
    ex, ey, ez = p0 - n["200"], p0 - n["020"], p0 - n["002"]
    h = [p0, ex + px, ex - px, ey + py, ey - py, ez + pz, ez - pz]
    h += spread(ex - n["020"] - n["220"], -n["110"], px - n["120"], py - n["210"])
    h += spread(ex - n["002"] - n["202"], -n["101"], px - n["102"], pz - n["201"])
    h += spread(ey - n["002"] - n["022"], -n["011"], py - n["012"], pz - n["021"])
    open_part = 1.0 - fraction
    return [open_part * (b[i] + h[i]) + fraction * b[opposite[i]] for i in range(Q)]


def put_moved(field, i, x, yt, value, direction):
    cx, cy, cz = (direction * c for c in velocities[i])
    if cz:
        value = pltpu.roll(value, cz % NZ, axis=1)
    x = (x + cx) & (CX - 1) if cx else x
    row = yt * TILE + cy
    if row < 0:
        field[i, x, pl.ds(0, TILE - 1), :] = value[1:]
        field[i, x, pl.ds(CY - 1, 1), :] = value[:1]
    elif row + TILE > CY:
        field[i, x, pl.ds(row, TILE - 1), :] = value[:-1]
        field[i, x, pl.ds(0, 1), :] = value[-1:]
    else:
        field[i, x, pl.ds(row, TILE), :] = value


def fill_messages(fields, direction, x_up, x_down, y_up, y_down):
    for n, field in enumerate(fields):
        for sign, x, message in ((1, 0, x_up), (-1, CX - 1, x_down)):
            for k, i in enumerate(moving(0, sign, direction)):
                message[pl.ds(n * FACE + k * CY, CY), :] = field[i, x]
        for sign, row, message in ((1, 0, y_up), (-1, CY - 1, y_down)):
            for k, i in enumerate(moving(1, sign, direction)):
                for x in range(CX):
                    message[pl.ds(n * FACE + k * CX + x, 1), :] = field[i, x, pl.ds(row, 1), :]


def fill_ring(fields, direction, x_low, x_high, y_low, y_high):
    for n, field in enumerate(fields):
        for sign, x, message in ((1, 0, x_low), (-1, CX - 1, x_high)):
            for k, i in enumerate(moving(0, sign, direction)):
                field[i, x] = message[pl.ds(n * FACE + k * CY, CY), :]
        for sign, row, message in ((1, 0, y_low), (-1, CY - 1, y_high)):
            for k, i in enumerate(moving(1, sign, direction)):
                for x in range(CX):
                    field[i, x, pl.ds(row, 1), :] = message[pl.ds(n * FACE + k * CX + x, 1), :]


def rows(yt):
    return pl.ds(yt * TILE, TILE)


def iota(shape, dim):
    return lax.broadcasted_iota(jnp.int32, shape, dim)


def column(row, pick):
    return jnp.sum(jnp.where(pick, row, 0.0), axis=1, keepdims=True)


def block_numbers(owners, slots, table, x_up, x_down, y_up, y_down):
    shape = (64, 64)
    row, lane = iota(shape, 0), iota(shape, 1)
    same = row == lane
    owner_row, slot_row = owners[...].astype(jnp.float32), slots[...].astype(jnp.float32)
    owner_col = column(owner_row, same)
    earlier = (owner_row == owner_col) & (lane < row)
    rank = jnp.sum(jnp.where(earlier, 1.0, 0.0), axis=1, keepdims=True)
    number = owner_col * 1024.0 + column(slot_row, same) * 4.0 + rank
    wide = (64, NZ)
    spot = iota(wide, 1) == (iota(wide, 0) & 7) + 1
    spread_out = jnp.where(spot, number, 0.0)
    table[...] = jnp.zeros((16, NZ), jnp.float32)
    for xb in range(8):
        line = jnp.sum(spread_out[xb * 8 : xb * 8 + 8], axis=0, keepdims=True)
        table[pl.ds(xb + 1, 1), :] = line
    held = table[...]
    x_up[pl.ds(META, 1), :] = held[8:9]
    x_down[pl.ds(META, 1), :] = held[1:2]
    eye = iota((16, NZ), 0) == iota((16, NZ), 1)
    for yb, message in ((8, y_up), (1, y_down)):
        part = jnp.where(eye, held[:, yb : yb + 1], 0.0)
        message[pl.ds(META, 1), :] = jnp.sum(part, axis=0, keepdims=True)


def forward_kernel(
    f_hbm, porosity_hbm, adjoint_hbm, porous_hbm, walls_hbm, owners_hbm, slots_hbm,
    moved, gap, adjoint, frac, mask, vel, table, xu, xd, yu, yd,
    f, porosity, porous, walls, owners, slots, f_sems, sems,
):
    def plane(x):
        return pltpu.make_async_copy(f_hbm.at[:, x], f.at[:, x], f_sems.at[x])

    small = [
        pltpu.make_async_copy(source, target, sems.at[k])
        for k, (source, target) in enumerate(
            (
                (owners_hbm, owners),
                (slots_hbm, slots),
                (porosity_hbm, porosity),
                (porous_hbm, porous),
                (walls_hbm, walls),
            )
        )
    ]
    later = pltpu.make_async_copy(adjoint_hbm, adjoint, sems.at[5])
    for copy in small:
        copy.start()
    for x in range(CX):
        plane(x).start()
    later.start()
    small[0].wait()
    small[1].wait()
    block_numbers(owners, slots, table, xu, xd, yu, yd)
    for copy in small[2:]:
        copy.wait()

    @pl.loop(0, CX)
    def _(x):
        plane(x).wait()
        for yt in range(CY // TILE):
            at = (x, rows(yt))
            pops = [f[i, x, rows(yt), :] for i in range(Q)]
            wall = walls[at] == 1
            panel = porous[at].astype(jnp.float32)
            fraction = jnp.where(wall, 1.0, panel * porosity[at])
            open_panel = jnp.where(wall, 0.0, panel)
            frac[at] = fraction
            mask[at] = open_panel
            u, e, _ = off_equilibrium(pops)
            for axis in range(3):
                vel[axis, x, rows(yt), :] = u[axis]
            c = correction(e)
            for i in range(Q):
                relaxed = pops[i] - c[i]
                change = pops[opposite[i]] - relaxed
                put_moved(gap, i, x, yt, open_panel * change, 1)
                put_moved(moved, i, x, yt, relaxed + fraction * change, 1)

    fill_messages((moved, gap), 1, xu, xd, yu, yd)
    later.wait()


def corner_kernel(x_low, x_high, up_in, down_in, up, down, *, direction, fields):
    del up_in, down_in
    for sign, row, message in ((1, 0, up), (-1, CY - 1, down)):
        for k, i in enumerate(moving(1, sign, direction)):
            cx = direction * velocities[i][0]
            if not cx:
                continue
            source, x = (x_low, 0) if cx == 1 else (x_high, CX - 1)
            k_x = moving(0, cx, direction).index(i)
            for n in range(fields):
                message[pl.ds(n * FACE + k * CX + x, 1), :] = source[
                    pl.ds(n * FACE + k_x * CY + row, 1), :
                ]
    if fields == 2:
        lane = iota((1, NZ), 1)
        for yb, message in ((8, up), (1, down)):
            low = jnp.sum(jnp.where(lane == yb, x_low[pl.ds(META, 1), :], 0.0))
            high = jnp.sum(jnp.where(lane == yb, x_high[pl.ds(META, 1), :], 0.0))
            line = message[pl.ds(META, 1), :]
            line = jnp.where(lane == 0, low, jnp.where(lane == 9, high, line))
            message[pl.ds(META, 1), :] = line


def routing_kernel(table, x_low, x_high, y_low, y_high, owner_of, place, slot, ext):
    shape = (16, NZ)
    row, lane = iota(shape, 0), iota(shape, 1)
    eye = row == lane
    low = column(y_low[pl.ds(META, 1), :], eye)
    high = column(y_high[pl.ds(META, 1), :], eye)
    held = jnp.where(row == 0, x_low[pl.ds(META, 1), :], table[...])
    held = jnp.where(row == 9, x_high[pl.ds(META, 1), :], held)
    ext[...] = jnp.where(lane == 0, low, jnp.where(lane == 9, high, held))
    shape = (EXT_Y, NZ)
    row, lane = iota(shape, 0), iota(shape, 1)
    yb = jnp.right_shift(row - 6, 1)
    pick = lane == yb
    side_y = jnp.where(yb == 0, 0, jnp.where(yb == 9, 2, 1))
    used = (row >= PAD_Y - 1) & (row <= PAD_Y + CY)
    first = used & ((yb == 0) | ((row & 1) == 0))
    for xb in range(EXT_XB):
        number = column(ext[pl.ds(xb, 1), :], pick).astype(jnp.int32)
        side = side_y * 6 + (0 if xb == 0 else 4 if xb == 9 else 2)
        spot = side + (number & 3)
        line = pl.ds(xb * EXT_Y, EXT_Y)
        owner_of[line, :] = jnp.where(used & (lane == jnp.right_shift(number, 10)), 1.0, 0.0)
        place[line, :] = jnp.where(lane == spot, 1.0, 0.0)
        patch = (jnp.right_shift(number, 2) & 255).astype(jnp.float32)
        slot[line, :] = jnp.where(first & (lane == spot + SLOT_LANE), patch, 0.0)


def late_kernel(
    moved_in, gap_in, xl, xh, yl, yh, adjoint, frac, mask, owner_of, place, slot,
    moved, gap, late, send, xu, xd, yu, yd, sums, scaled,
):
    del moved_in, gap_in
    fill_ring((moved, gap), 1, xl, xh, yl, yh)
    sums[...] = jnp.zeros((EXT_XB, EXT_Y, NZ), jnp.float32)

    @pl.loop(0, CX // 2)
    def _(xb):
        for yt in range(CY // TILE):
            parts = {}
            for half in range(2):
                x = xb * 2 + half
                at = (x, rows(yt))
                read = [moved[i, x, rows(yt), :] for i in range(Q)]
                u, e, df = off_equilibrium(read)
                b = [adjoint[i, x, rows(yt), :] for i in range(Q)]
                t, db = covector(b)
                total = sum(t[k] * e[k] for k in t) - sum(p * q for p, q in zip(db, df))
                total = mask[at] * total
                out = pull_back(b, t, u, frac[at])
                key = (0, 0)
                parts[key] = parts[key] + total if key in parts else total
                for i in range(Q):
                    cx, cy, _ = velocities[i]
                    key = ((half - cx) // 2, cy)
                    early = out[i] * gap[i, x, rows(yt), :]
                    parts[key] = parts[key] + early if key in parts else early
                    put_moved(late, i, x, yt, out[i], -1)
            for (step, cy), part in parts.items():
                at = (xb + 1 + step, pl.ds(PAD_Y + yt * TILE - cy, TILE))
                sums[at] = sums[at] + part

    for xb in range(EXT_XB):
        line = pl.ds(xb * EXT_Y, EXT_Y)
        scaled[line, :] = (
            jnp.sum(sums[xb], axis=1, keepdims=True) * place[line, :] + slot[line, :]
        )
    send[...] = lax.dot_general(
        owner_of[...],
        scaled[...],
        (((0,), (0,)), ((), ())),
        precision=lax.Precision.HIGHEST,
        preferred_element_type=jnp.float32,
    )
    fill_messages((late,), -1, xu, xd, yu, yd)


def early_kernel(late_in, xl, xh, yl, yh, frac, vel, late, out, hold, sems):
    del late_in
    fill_ring((late,), -1, xl, xh, yl, yh)

    def plane(x):
        return pltpu.make_async_copy(hold.at[x], out.at[:, x], sems.at[x])

    @pl.loop(0, CX)
    def _(x):
        for yt in range(CY // TILE):
            b = [late[i, x, rows(yt), :] for i in range(Q)]
            t, _ = covector(b)
            u = [vel[axis, x, rows(yt), :] for axis in range(3)]
            result = pull_back(b, t, u, frac[x, rows(yt)])
            for i in range(Q):
                hold[x, i, rows(yt), :] = result[i]
        plane(x).start()

    for x in range(CX):
        plane(x).wait()


def owner_kernel(late, got, out):
    del late
    patch = iota((DEVICES, PATCH_DEV), 1).astype(jnp.float32)
    data = got[...]
    total = jnp.zeros((DEVICES, PATCH_DEV), jnp.float32)
    for k in range(18):
        hit = data[:, SLOT_LANE + k : SLOT_LANE + k + 1] == patch
        total = total + jnp.where(hit, data[:, k : k + 1], 0.0)
    out[...] = jnp.sum(total, axis=0, keepdims=True)


VMEM = pl.BlockSpec(memory_space=pltpu.VMEM)
ANY = pl.BlockSpec(memory_space=pl.ANY)
LIMIT = 8 * 2**20


def vmem(*shape):
    return pltpu.VMEM(shape, jnp.float32)


def call(kernel, ins, outs, scratch=(), aliases=None, flops=0, hbm_ins=0, hbm_outs=()):
    held = [pltpu.with_memory_space_constraint(x, pltpu.HBM) for x in ins[:hbm_ins]]
    held += [pltpu.with_memory_space_constraint(x, pltpu.VMEM) for x in ins[hbm_ins:]]
    return pl.pallas_call(
        kernel,
        out_shape=[*outs, *hbm_outs],
        in_specs=[ANY] * hbm_ins + [VMEM] * (len(ins) - hbm_ins),
        out_specs=[VMEM] * len(outs) + [ANY] * len(hbm_outs),
        scratch_shapes=list(scratch),
        input_output_aliases=aliases or {},
        compiler_params=pltpu.CompilerParams(vmem_limit_bytes=LIMIT),
        cost_estimate=pl.CostEstimate(flops=flops, bytes_accessed=0, transcendentals=0),
    )(*held)


FIELD = vmem(Q, CX, CY, NZ)
NODE = vmem(CX, CY, NZ)
MESSAGE = vmem(MESSAGE_ROWS, NZ)
SHORT_MESSAGE = vmem(FACE, NZ)
LINES = vmem(BLOCK_ROWS, NZ)


def shift(block, axis, step):
    count = lax.axis_size(axis)
    return lax.ppermute(block, axis, [(i, (i + step) % count) for i in range(count)])


def exchange(messages, direction, fields):
    x_up, x_down, y_up, y_down = messages
    x_low = shift(x_up, "gx", 1)
    x_high = shift(x_down, "gx", -1)
    y_up, y_down = call(
        functools.partial(corner_kernel, direction=direction, fields=fields),
        [x_low, x_high, y_up, y_down],
        [MESSAGE if fields == 2 else SHORT_MESSAGE] * 2,
        aliases={2: 0, 3: 1},
    )
    y_low = shift(y_up, "gy", 1)
    y_high = shift(y_down, "gy", -1)
    return x_low, x_high, y_low, y_high


def body(populations, porosity, adjoint_in, porous, walls, owners, slots):
    ints = pltpu.VMEM((CX, CY, NZ), jnp.int32)
    moved, gap, adjoint, frac, mask, vel, table, *messages = call(
        forward_kernel,
        [populations, porosity, adjoint_in, porous, walls]
        + [owners.reshape(1, 64), slots.reshape(1, 64)],
        [FIELD] * 3 + [NODE] * 2 + [vmem(3, CX, CY, NZ), vmem(16, NZ)] + [MESSAGE] * 4,
        scratch=[FIELD, NODE, ints, ints]
        + [pltpu.VMEM((1, 64), jnp.int32)] * 2
        + [pltpu.SemaphoreType.DMA((CX,)), pltpu.SemaphoreType.DMA((6,))],
        hbm_ins=7,
    )
    halos = exchange(messages, 1, 2)
    owner_of, place, slot = call(
        routing_kernel, [table, *halos], [LINES] * 3, scratch=[vmem(16, NZ)]
    )
    _, _, late, send, *messages = call(
        late_kernel,
        [moved, gap, *halos, adjoint, frac, mask, owner_of, place, slot],
        [FIELD] * 3 + [vmem(DEVICES, NZ)] + [SHORT_MESSAGE] * 4,
        scratch=[vmem(EXT_XB, EXT_Y, NZ), LINES],
        aliases={0: 0, 1: 1},
    )
    got = lax.all_to_all(send, ("gx", "gy"), split_axis=0, concat_axis=0, tiled=True)
    halos = exchange(messages, -1, 1)
    late, adjoint_out = call(
        early_kernel,
        [late, *halos, frac, vel],
        [FIELD],
        hbm_outs=[jax.ShapeDtypeStruct((Q, CX, CY, NZ), jnp.float32)],
        scratch=[vmem(CX, Q, CY, NZ), pltpu.SemaphoreType.DMA((CX,))],
        aliases={0: 0},
    )
    (patch,) = call(owner_kernel, [late, got], [vmem(1, PATCH_DEV)])
    return adjoint_out, patch.reshape(PATCH_DEV)


def solution(mesh):
    return jax.shard_map(
        body,
        mesh=mesh,
        in_specs=(
            P(None, "gx", "gy", None),
            P("gx", "gy", None),
            P(None, "gx", "gy", None),
            P("gx", "gy", None),
            P("gx", "gy", None),
            P("gx", "gy", None, None),
            P("gx", "gy", None),
        ),
        out_specs=(P(None, "gx", "gy", None), P(("gx", "gy"))),
        check_vma=False,
    )
```

```python
import jax
import jax.numpy as jnp
from jax import lax
from jax.experimental import pallas as pl
from jax.experimental.pallas import tpu as pltpu
from jax.sharding import PartitionSpec as P

Q = 19
CX = 16
CY = 16
NZ = 128
TILE = 8
PAD_Y = 8
EXT_Y = 32
EXT_XB = 10
BLOCK_ROWS = EXT_XB * EXT_Y
DEVICES = 128
PATCH_DEV = 256
SLOT_LANE = 64
FACE = 80
META = 160
MESSAGE_ROWS = 168
PLANES = 4

velocities = [
    (0, 0, 0),
    (1, 0, 0),
    (-1, 0, 0),
    (0, 1, 0),
    (0, -1, 0),
    (0, 0, 1),
    (0, 0, -1),
    (1, 1, 0),
    (-1, -1, 0),
    (1, -1, 0),
    (-1, 1, 0),
    (1, 0, 1),
    (-1, 0, -1),
    (1, 0, -1),
    (-1, 0, 1),
    (0, 1, 1),
    (0, -1, -1),
    (0, 1, -1),
    (0, -1, 1),
]
opposite = [0, 2, 1, 4, 3, 6, 5, 8, 7, 10, 9, 12, 11, 14, 13, 16, 15, 18, 17]
RATE2, RATE3, RATE4 = 1.25, 1.5, 1.4


def moving(axis, sign, direction):
    return [i for i in range(Q) if direction * velocities[i][axis] == sign]


def edge(f, first):
    s, d = f[first] + f[first + 1], f[first] - f[first + 1]
    s2, d2 = f[first + 2] + f[first + 3], f[first + 2] - f[first + 3]
    return s, d, s2, d2


def off_equilibrium(f):
    sx, dx = f[1] + f[2], f[1] - f[2]
    sy, dy = f[3] + f[4], f[3] - f[4]
    sz, dz = f[5] + f[6], f[5] - f[6]
    s7, d7, s9, d9 = edge(f, 7)
    s11, d11, s13, d13 = edge(f, 11)
    s15, d15, s17, d17 = edge(f, 15)
    m220, m110, m120, m210 = s7 + s9, s7 - s9, d7 + d9, d7 - d9
    m202, m101, m102, m201 = s11 + s13, s11 - s13, d11 + d13, d11 - d13
    m022, m011, m012, m021 = s15 + s17, s15 - s17, d15 + d17, d15 - d17
    m200, m020, m002 = sx + m220 + m202, sy + m220 + m022, sz + m202 + m022
    jx, jy, jz = dx + (m120 + m102), dy + (m210 + m012), dz + (m201 + m021)
    rho = f[0] + (sx + sy + sz) + (m220 + m202 + m022)
    inv = 1.0 / rho
    ux, uy, uz = jx * inv, jy * inv, jz * inv
    qx, qy, qz = jx * ux, jy * uy, jz * uz
    third = rho * (1.0 / 3.0)
    ninth = rho * (1.0 / 9.0) - (qx + qy + qz) * (1.0 / 6.0)
    tx, ty, tz = jx * (1.0 / 3.0), jy * (1.0 / 3.0), jz * (1.0 / 3.0)
    e = {
        "200": RATE2 * (m200 - third - qx),
        "020": RATE2 * (m020 - third - qy),
        "002": RATE2 * (m002 - third - qz),
        "110": RATE2 * (m110 - jx * uy),
        "101": RATE2 * (m101 - jx * uz),
        "011": RATE2 * (m011 - jy * uz),
        "120": RATE3 * (m120 - tx),
        "102": RATE3 * (m102 - tx),
        "210": RATE3 * (m210 - ty),
        "012": RATE3 * (m012 - ty),
        "201": RATE3 * (m201 - tz),
        "021": RATE3 * (m021 - tz),
        "220": RATE4 * (m220 - ninth - 0.5 * (qx + qy)),
        "202": RATE4 * (m202 - ninth - 0.5 * (qx + qz)),
        "022": RATE4 * (m022 - ninth - 0.5 * (qy + qz)),
    }
    return (ux, uy, uz), e, (dx, dy, dz, d7, d9, d11, d13, d15, d17)


def spread(t, g, a, b):
    even, odd = t + g, t - g
    plus, minus = a + b, a - b
    return [even + plus, even - plus, odd + minus, odd - minus]


def correction(e):
    q = {k: 0.25 * v for k, v in e.items()}
    xy = spread(q["220"], q["110"], q["120"], q["210"])
    xz = spread(q["202"], q["101"], q["102"], q["201"])
    yz = spread(q["022"], q["011"], q["012"], q["021"])
    faces = []
    for second, fourth, odd in (
        ("200", ("220", "202"), ("120", "102")),
        ("020", ("220", "022"), ("210", "012")),
        ("002", ("202", "022"), ("201", "021")),
    ):
        mean = 0.5 * e[second] - 2.0 * (q[fourth[0]] + q[fourth[1]])
        lean = 2.0 * (q[odd[0]] + q[odd[1]])
        faces += [mean - lean, mean + lean]
    rest = (e["220"] + e["202"] + e["022"]) - (e["200"] + e["020"] + e["002"])
    return [rest] + faces + xy + xz + yz


def covector(b):
    hx, dx = 0.5 * (b[1] + b[2]), b[1] - b[2]
    hy, dy = 0.5 * (b[3] + b[4]), b[3] - b[4]
    hz, dz = 0.5 * (b[5] + b[6]), b[5] - b[6]
    s7, d7, s9, d9 = edge(b, 7)
    s11, d11, s13, d13 = edge(b, 11)
    s15, d15, s17, d17 = edge(b, 15)
    gx, gy, gz = hx - b[0], hy - b[0], hz - b[0]
    kx, ky, kz = 0.5 * dx, 0.5 * dy, 0.5 * dz
    t = {
        "200": gx,
        "020": gy,
        "002": gz,
        "110": 0.25 * (s7 - s9),
        "101": 0.25 * (s11 - s13),
        "011": 0.25 * (s15 - s17),
        "120": 0.25 * (d7 + d9) - kx,
        "102": 0.25 * (d11 + d13) - kx,
        "210": 0.25 * (d7 - d9) - ky,
        "012": 0.25 * (d15 + d17) - ky,
        "201": 0.25 * (d11 - d13) - kz,
        "021": 0.25 * (d15 - d17) - kz,
        "220": 0.25 * (s7 + s9) - gx - hy,
        "202": 0.25 * (s11 + s13) - gx - hz,
        "022": 0.25 * (s15 + s17) - gy - hz,
    }
    return t, (dx, dy, dz, d7, d9, d11, d13, d15, d17)


def pull_back(b, t, u, fraction):
    rates = {k: (RATE2, RATE3, RATE4)[sum(map(int, k)) - 2] for k in t}
    n = {k: rates[k] * v for k, v in t.items()}
    ux, uy, uz = u
    fourth = n["220"] + n["202"] + n["022"]
    second = n["200"] + n["020"] + n["002"]
    part = fourth * (1.0 / 3.0)
    ax = n["200"] + part - 0.5 * n["022"]
    ay = n["020"] + part - 0.5 * n["202"]
    az = n["002"] + part - 0.5 * n["220"]
    rx = 2.0 * ax * ux + n["110"] * uy + n["101"] * uz
    ry = 2.0 * ay * uy + n["110"] * ux + n["011"] * uz
    rz = 2.0 * az * uz + n["101"] * ux + n["011"] * uy
    p0 = second * (1.0 / 3.0) + fourth * (1.0 / 9.0) - 0.5 * (rx * ux + ry * uy + rz * uz)
    px = rx + (n["120"] + n["102"]) * (1.0 / 3.0)
    py = ry + (n["210"] + n["012"]) * (1.0 / 3.0)
    pz = rz + (n["201"] + n["021"]) * (1.0 / 3.0)
    ex, ey, ez = p0 - n["200"], p0 - n["020"], p0 - n["002"]
    h = [p0, ex + px, ex - px, ey + py, ey - py, ez + pz, ez - pz]
    h += spread(ex - n["020"] - n["220"], -n["110"], px - n["120"], py - n["210"])
    h += spread(ex - n["002"] - n["202"], -n["101"], px - n["102"], pz - n["201"])
    h += spread(ey - n["002"] - n["022"], -n["011"], py - n["012"], pz - n["021"])
    open_part = 1.0 - fraction
    return [open_part * (b[i] + h[i]) + fraction * b[opposite[i]] for i in range(Q)]


def store_wrapped(put, first, step, value):
    row = first + step
    if row < 0:
        put(0, value[1:])
        put(CY - 1, value[:1])
    elif row + TILE > CY:
        put(row, value[:-1])
        put(0, value[-1:])
    else:
        put(row, value)


def put_moved(field, i, x, yt, value, direction):
    cx, cy, cz = (direction * c for c in velocities[i])
    if cz:
        value = pltpu.roll(value, cz % NZ, axis=1)
    x = (x + cx) & (CX - 1) if cx else x

    def put(row, part):
        field[i, x, pl.ds(row, part.shape[0]), :] = part

    store_wrapped(put, yt * TILE, cy, value)


def x_faces(fields, direction, x_up, x_down):
    for n, field in enumerate(fields):
        for sign, x, message in ((1, 0, x_up), (-1, CX - 1, x_down)):
            for k, i in enumerate(moving(0, sign, direction)):
                message[pl.ds(n * FACE + k * CY, CY), :] = field[i, x]


def y_faces(fields, direction, y_up, y_down):
    for n, field in enumerate(fields):
        for sign, row, message in ((1, 0, y_up), (-1, CY - 1, y_down)):
            for k, i in enumerate(moving(1, sign, direction)):
                for x in range(CX):
                    message[pl.ds(n * FACE + k * CX + x, 1), :] = field[i, x, pl.ds(row, 1), :]


def fill_x(fields, direction, x_low, x_high):
    for n, field in enumerate(fields):
        for sign, x, message in ((1, 0, x_low), (-1, CX - 1, x_high)):
            for k, i in enumerate(moving(0, sign, direction)):
                field[i, x] = message[pl.ds(n * FACE + k * CY, CY), :]


def fill_y(fields, direction, y_low, y_high):
    for n, field in enumerate(fields):
        for sign, row, message in ((1, 0, y_low), (-1, CY - 1, y_high)):
            for k, i in enumerate(moving(1, sign, direction)):
                for x in range(CX):
                    field[i, x, pl.ds(row, 1), :] = message[pl.ds(n * FACE + k * CX + x, 1), :]


def rows(yt):
    return pl.ds(yt * TILE, TILE)


def unrolled(start, stop, count, step):
    @pl.loop(0, (stop - start) // count)
    def _(n):
        for k in range(count):
            step(start + n * count + k)


def iota(shape, dim):
    return lax.broadcasted_iota(jnp.int32, shape, dim)


def column(row, pick):
    return jnp.sum(jnp.where(pick, row, 0.0), axis=1, keepdims=True)


def block_numbers(owners, slots, table, y_up, y_down):
    shape = (64, 64)
    row, lane = iota(shape, 0), iota(shape, 1)
    same = row == lane
    owner_row, slot_row = owners[...].astype(jnp.float32), slots[...].astype(jnp.float32)
    owner_col = column(owner_row, same)
    earlier = (owner_row == owner_col) & (lane < row)
    rank = jnp.sum(jnp.where(earlier, 1.0, 0.0), axis=1, keepdims=True)
    number = owner_col * 1024.0 + column(slot_row, same) * 4.0 + rank
    wide = (64, NZ)
    spot = iota(wide, 1) == (iota(wide, 0) & 7) + 1
    spread_out = jnp.where(spot, number, 0.0)
    table[...] = jnp.zeros((16, NZ), jnp.float32)
    for xb in range(8):
        line = jnp.sum(spread_out[xb * 8 : xb * 8 + 8], axis=0, keepdims=True)
        table[pl.ds(xb + 1, 1), :] = line
    held = table[...]
    eye = iota((16, NZ), 0) == iota((16, NZ), 1)
    for yb, message in ((8, y_up), (1, y_down)):
        part = jnp.where(eye, held[:, yb : yb + 1], 0.0)
        message[pl.ds(META, 1), :] = jnp.sum(part, axis=0, keepdims=True)


def solidity(porosity, porous, walls):
    wall = walls == 1
    panel = porous.astype(jnp.float32)
    return jnp.where(wall, 1.0, panel * porosity), jnp.where(wall, 0.0, panel)


def edge_kernel(
    f_hbm, porosity_hbm, porous_hbm, walls_hbm, owners_hbm, slots_hbm,
    table, yu, yd, f, porosity, porous, walls, owners, slots, sems,
):
    numbers = [
        pltpu.make_async_copy(owners_hbm, owners, sems.at[0]),
        pltpu.make_async_copy(slots_hbm, slots, sems.at[1]),
    ]
    lines = []
    for n, y in enumerate((CY - 1, 0)):
        lines += [
            pltpu.make_async_copy(f_hbm.at[:, :, y, :], f.at[n], sems.at[4 * n + 2]),
            pltpu.make_async_copy(porosity_hbm.at[:, y, :], porosity.at[n], sems.at[4 * n + 3]),
            pltpu.make_async_copy(porous_hbm.at[:, y, :], porous.at[n], sems.at[4 * n + 4]),
            pltpu.make_async_copy(walls_hbm.at[:, y, :], walls.at[n], sems.at[4 * n + 5]),
        ]
    for copy in numbers + lines:
        copy.start()
    for copy in numbers:
        copy.wait()
    block_numbers(owners, slots, table, yu, yd)
    for copy in lines:
        copy.wait()
    for n, (sign, message) in enumerate(((1, yu), (-1, yd))):
        for xt in range(CX // TILE):
            at = (n, rows(xt))
            pops = [f[n, i, rows(xt), :] for i in range(Q)]
            fraction, open_panel = solidity(porosity[at], porous[at], walls[at])
            c = correction(off_equilibrium(pops)[1])
            for k, i in enumerate(moving(1, sign, 1)):
                relaxed = pops[i] - c[i]
                change = pops[opposite[i]] - relaxed
                pair = (relaxed + fraction * change, open_panel * change)
                for field, value in enumerate(pair):
                    cx, _, cz = velocities[i]
                    if cz:
                        value = pltpu.roll(value, cz % NZ, axis=1)

                    def put(row, part, base=field * FACE + k * CX, message=message):
                        message[pl.ds(base + row, part.shape[0]), :] = part

                    store_wrapped(put, xt * TILE, cx, value)


def forward_kernel(
    f_hbm, porosity_hbm, porous_hbm, walls_hbm, adjoint_hbm,
    moved, gap, adjoint, frac, mask, vel,
    f, porosity, porous, walls, f_sems, sems,
):
    def planes(n):
        part = pl.ds(n * PLANES, PLANES)
        return pltpu.make_async_copy(f_hbm.at[:, part], f.at[:, part], f_sems.at[n])

    small = [
        pltpu.make_async_copy(porosity_hbm, porosity, sems.at[0]),
        pltpu.make_async_copy(porous_hbm, porous, sems.at[1]),
        pltpu.make_async_copy(walls_hbm, walls, sems.at[2]),
    ]
    later = pltpu.make_async_copy(adjoint_hbm, adjoint, sems.at[3])
    for copy in small:
        copy.start()
    for n in range(CX // PLANES):
        planes(n).start()
    later.start()
    for copy in small:
        copy.wait()

    def plane(x):
        for yt in range(CY // TILE):
            at = (x, rows(yt))
            pops = [f[i, x, rows(yt), :] for i in range(Q)]
            fraction, open_panel = solidity(porosity[at], porous[at], walls[at])
            frac[at] = fraction
            mask[at] = open_panel
            u, e, _ = off_equilibrium(pops)
            for axis in range(3):
                vel[axis, x, rows(yt), :] = u[axis]
            c = correction(e)
            for i in range(Q):
                relaxed = pops[i] - c[i]
                change = pops[opposite[i]] - relaxed
                put_moved(gap, i, x, yt, open_panel * change, 1)
                put_moved(moved, i, x, yt, relaxed + fraction * change, 1)

    @pl.loop(0, CX // PLANES)
    def _(n):
        planes(n).wait()
        for k in range(PLANES):
            plane(n * PLANES + k)

    later.wait()


def turn_kernel(moved_in, gap_in, table, y_low, y_high, moved, gap, ext, x_up, x_down):
    del moved_in, gap_in
    fill_y((moved, gap), 1, y_low, y_high)
    x_faces((moved, gap), 1, x_up, x_down)
    shape = (16, NZ)
    row, lane = iota(shape, 0), iota(shape, 1)
    low = column(y_low[pl.ds(META, 1), :], row == lane)
    high = column(y_high[pl.ds(META, 1), :], row == lane)
    held = jnp.where(lane == 0, low, jnp.where(lane == 9, high, table[...]))
    ext[...] = held
    x_up[pl.ds(META, 1), :] = held[8:9]
    x_down[pl.ds(META, 1), :] = held[1:2]


def corner_kernel(x_low, x_high, up_in, down_in, up, down):
    del up_in, down_in
    for sign, row, message in ((1, 0, up), (-1, CY - 1, down)):
        for k, i in enumerate(moving(1, sign, -1)):
            cx = -velocities[i][0]
            if cx:
                source, x = (x_low, 0) if cx == 1 else (x_high, CX - 1)
                corner = moving(0, cx, -1).index(i) * CY + row
                message[pl.ds(k * CX + x, 1), :] = source[pl.ds(corner, 1), :]


def late_blocks(xb, take, adjoint, frac, mask, late, sums):
    for yt in range(CY // TILE):
        parts = {}
        for half in range(2):
            x = xb * 2 + half
            at = (x, rows(yt))
            read = [take(0, i, x, yt) for i in range(Q)]
            u, e, df = off_equilibrium(read)
            b = [adjoint[i, x, rows(yt), :] for i in range(Q)]
            t, db = covector(b)
            total = sum(t[k] * e[k] for k in t) - sum(p * q for p, q in zip(db, df))
            total = mask[at] * total
            out = pull_back(b, t, u, frac[at])
            key = (0, 0)
            parts[key] = parts[key] + total if key in parts else total
            for i in range(Q):
                cx, cy, _ = velocities[i]
                key = ((half - cx) // 2, cy)
                early = out[i] * take(1, i, x, yt)
                parts[key] = parts[key] + early if key in parts else early
                put_moved(late, i, x, yt, out[i], -1)
        for (step, cy), part in parts.items():
            at = (xb + 1 + step, pl.ds(PAD_Y + yt * TILE - cy, TILE))
            sums[at] = sums[at] + part


def late_kernel(moved, gap, adjoint, frac, mask, late, sums):
    fields = (moved, gap)
    sums[...] = jnp.zeros((EXT_XB, EXT_Y, NZ), jnp.float32)

    def take(n, i, x, yt):
        return fields[n][i, x, rows(yt), :]

    def step(xb):
        late_blocks(xb, take, adjoint, frac, mask, late, sums)

    unrolled(1, CX // 2 - 1, 2, step)


def late_rest_kernel(
    late_in, sums_in, moved, gap, ext_in, x_low, x_high, adjoint, frac, mask,
    late, sums, send, xu, xd, yu, yd, ext, owner_of, scaled,
):
    del late_in, sums_in
    fields = (moved, gap)

    def take(n, i, x, yt):
        cx = velocities[i][0]
        for sign, place, message in ((1, 0, x_low), (-1, CX - 1, x_high)):
            if cx == sign and x == place:
                first = n * FACE + moving(0, sign, 1).index(i) * CY + yt * TILE
                return message[pl.ds(first, TILE), :]
        return fields[n][i, x, rows(yt), :]

    for xb in (0, CX // 2 - 1):
        late_blocks(xb, take, adjoint, frac, mask, late, sums)
    x_faces((late,), -1, xu, xd)
    y_faces((late,), -1, yu, yd)

    row = iota((16, NZ), 0)
    held = jnp.where(row == 0, x_low[pl.ds(META, 1), :], ext_in[...])
    ext[...] = jnp.where(row == 9, x_high[pl.ds(META, 1), :], held)
    shape = (EXT_Y, NZ)
    row, lane = iota(shape, 0), iota(shape, 1)
    yb = jnp.right_shift(row - 6, 1)
    pick = lane == yb
    side_y = jnp.where(yb == 0, 0, jnp.where(yb == 9, 2, 1))
    used = (row >= PAD_Y - 1) & (row <= PAD_Y + CY)
    first = used & ((yb == 0) | ((row & 1) == 0))
    for xb in range(EXT_XB):
        number = column(ext[pl.ds(xb, 1), :], pick).astype(jnp.int32)
        side = side_y * 6 + (0 if xb == 0 else 4 if xb == 9 else 2)
        spot = side + (number & 3)
        line = pl.ds(xb * EXT_Y, EXT_Y)
        owner_of[line, :] = jnp.where(used & (lane == jnp.right_shift(number, 10)), 1.0, 0.0)
        patch = (jnp.right_shift(number, 2) & 255).astype(jnp.float32)
        value = jnp.where(lane == spot, jnp.sum(sums[xb], axis=1, keepdims=True), 0.0)
        scaled[line, :] = jnp.where(first & (lane == spot + SLOT_LANE), patch, value)
    send[...] = lax.dot_general(
        owner_of[...],
        scaled[...],
        (((0,), (0,)), ((), ())),
        precision=lax.Precision.HIGHEST,
        preferred_element_type=jnp.float32,
    )


def early_kernel(late_in, xl, xh, yl, yh, frac, vel, late, out, hold, sems):
    del late_in
    fill_x((late,), -1, xl, xh)
    fill_y((late,), -1, yl, yh)

    def planes(n):
        part = pl.ds(n * PLANES, PLANES)
        return pltpu.make_async_copy(hold.at[:, part], out.at[:, part], sems.at[n])

    @pl.loop(0, CX // PLANES)
    def _(n):
        for k in range(PLANES):
            x = n * PLANES + k
            for yt in range(CY // TILE):
                b = [late[i, x, rows(yt), :] for i in range(Q)]
                t, _ = covector(b)
                u = [vel[axis, x, rows(yt), :] for axis in range(3)]
                result = pull_back(b, t, u, frac[x, rows(yt)])
                for i in range(Q):
                    hold[i, x, rows(yt), :] = result[i]
        planes(n).start()

    for n in range(CX // PLANES):
        planes(n).wait()


def owner_kernel(late, got, out):
    del late
    patch = iota((DEVICES, PATCH_DEV), 1).astype(jnp.float32)
    data = got[...]
    total = jnp.zeros((DEVICES, PATCH_DEV), jnp.float32)
    for k in range(18):
        hit = data[:, SLOT_LANE + k : SLOT_LANE + k + 1] == patch
        total = total + jnp.where(hit, data[:, k : k + 1], 0.0)
    out[...] = jnp.sum(total, axis=0, keepdims=True)


VMEM = pl.BlockSpec(memory_space=pltpu.VMEM)
ANY = pl.BlockSpec(memory_space=pl.ANY)
LIMIT = 8 * 2**20


def vmem(*shape):
    return pltpu.VMEM(shape, jnp.float32)


def call(kernel, ins, outs, scratch=(), aliases=None, flops=0, hbm_ins=0, hbm_outs=()):
    held = [pltpu.with_memory_space_constraint(x, pltpu.HBM) for x in ins[:hbm_ins]]
    held += [pltpu.with_memory_space_constraint(x, pltpu.VMEM) for x in ins[hbm_ins:]]
    return pl.pallas_call(
        kernel,
        out_shape=[*outs, *hbm_outs],
        in_specs=[ANY] * hbm_ins + [VMEM] * (len(ins) - hbm_ins),
        out_specs=[VMEM] * len(outs) + [ANY] * len(hbm_outs),
        scratch_shapes=list(scratch),
        input_output_aliases=aliases or {},
        compiler_params=pltpu.CompilerParams(vmem_limit_bytes=LIMIT),
        cost_estimate=pl.CostEstimate(flops=flops, bytes_accessed=0, transcendentals=0),
    )(*held)


FIELD = vmem(Q, CX, CY, NZ)
NODE = vmem(CX, CY, NZ)
MESSAGE = vmem(MESSAGE_ROWS, NZ)
SHORT_MESSAGE = vmem(FACE, NZ)
LINES = vmem(BLOCK_ROWS, NZ)


def shift(block, axis, step):
    count = lax.axis_size(axis)
    return lax.ppermute(block, axis, [(i, (i + step) % count) for i in range(count)])


def body(populations, porosity, adjoint_in, porous, walls, owners, slots):
    ints = pltpu.VMEM((CX, CY, NZ), jnp.int32)
    dma = pltpu.SemaphoreType.DMA
    table, y_up, y_down = call(
        edge_kernel,
        [populations, porosity, porous, walls, owners.reshape(1, 64), slots.reshape(1, 64)],
        [vmem(16, NZ), MESSAGE, MESSAGE],
        scratch=[vmem(2, Q, CX, NZ), vmem(2, CX, NZ)]
        + [pltpu.VMEM((2, CX, NZ), jnp.int32)] * 2
        + [pltpu.VMEM((1, 64), jnp.int32)] * 2
        + [dma((10,))],
        hbm_ins=6,
    )
    y_low = shift(y_up, "gy", 1)
    y_high = shift(y_down, "gy", -1)
    moved, gap, adjoint, frac, mask, vel = call(
        forward_kernel,
        [populations, porosity, porous, walls, adjoint_in],
        [FIELD] * 3 + [NODE] * 2 + [vmem(3, CX, CY, NZ)],
        scratch=[FIELD, NODE, ints, ints, dma((CX // PLANES,)), dma((4,))],
        hbm_ins=5,
        flops=20_000_000,
    )
    moved, gap, ext, x_up, x_down = call(
        turn_kernel,
        [moved, gap, table, y_low, y_high],
        [FIELD, FIELD, vmem(16, NZ), MESSAGE, MESSAGE],
        aliases={0: 0, 1: 1},
    )
    x_low = shift(x_up, "gx", 1)
    x_high = shift(x_down, "gx", -1)
    late, sums = call(
        late_kernel,
        [moved, gap, adjoint, frac, mask],
        [FIELD, vmem(EXT_XB, EXT_Y, NZ)],
        flops=20_000_000,
    )
    late, _, send, x_up, x_down, y_up, y_down = call(
        late_rest_kernel,
        [late, sums, moved, gap, ext, x_low, x_high, adjoint, frac, mask],
        [FIELD, vmem(EXT_XB, EXT_Y, NZ), vmem(DEVICES, NZ)] + [SHORT_MESSAGE] * 4,
        scratch=[vmem(16, NZ)] + [LINES] * 2,
        aliases={0: 0, 1: 1},
    )
    got = lax.all_to_all(send, ("gx", "gy"), split_axis=0, concat_axis=0, tiled=True)
    x_low = shift(x_up, "gx", 1)
    x_high = shift(x_down, "gx", -1)
    y_up, y_down = call(
        corner_kernel,
        [x_low, x_high, y_up, y_down],
        [SHORT_MESSAGE] * 2,
        aliases={2: 0, 3: 1},
    )
    y_low = shift(y_up, "gy", 1)
    y_high = shift(y_down, "gy", -1)
    late, adjoint_out = call(
        early_kernel,
        [late, x_low, x_high, y_low, y_high, frac, vel],
        [FIELD],
        hbm_outs=[jax.ShapeDtypeStruct((Q, CX, CY, NZ), jnp.float32)],
        scratch=[FIELD, dma((CX // PLANES,))],
        aliases={0: 0},
    )
    (patch,) = call(owner_kernel, [late, got], [vmem(1, PATCH_DEV)])
    return adjoint_out, patch.reshape(PATCH_DEV)


def solution(mesh):
    return jax.shard_map(
        body,
        mesh=mesh,
        in_specs=(
            P(None, "gx", "gy", None),
            P("gx", "gy", None),
            P(None, "gx", "gy", None),
            P("gx", "gy", None),
            P("gx", "gy", None),
            P("gx", "gy", None, None),
            P("gx", "gy", None),
        ),
        out_specs=(P(None, "gx", "gy", None), P(("gx", "gy"))),
        check_vma=False,
    )
```

```python
import jax
import jax.numpy as jnp
from jax import lax
from jax.experimental import pallas as pl
from jax.experimental.pallas import tpu as pltpu
from jax.sharding import PartitionSpec as P

Q = 19
CX = 16
CY = 16
NZ = 128
TILE = 8
PAD_Y = 8
EXT_Y = 32
EXT_XB = 10
RING = 80
LINE_COUNT = 112
DEVICES = 128
N_GX, N_GY = 8, 16
PATCH_DEV = 256
SLOT_LANE = 64
PARTS = 14
FACE = 80
META = 160
MESSAGE_ROWS = 168
PLANES = 4

velocities = [
    (0, 0, 0),
    (1, 0, 0),
    (-1, 0, 0),
    (0, 1, 0),
    (0, -1, 0),
    (0, 0, 1),
    (0, 0, -1),
    (1, 1, 0),
    (-1, -1, 0),
    (1, -1, 0),
    (-1, 1, 0),
    (1, 0, 1),
    (-1, 0, -1),
    (1, 0, -1),
    (-1, 0, 1),
    (0, 1, 1),
    (0, -1, -1),
    (0, 1, -1),
    (0, -1, 1),
]
opposite = [0, 2, 1, 4, 3, 6, 5, 8, 7, 10, 9, 12, 11, 14, 13, 16, 15, 18, 17]
RATE2, RATE3, RATE4 = 1.25, 1.5, 1.4


def moving(axis, sign, direction):
    return [i for i in range(Q) if direction * velocities[i][axis] == sign]


def edge(f, first):
    s, d = f[first] + f[first + 1], f[first] - f[first + 1]
    s2, d2 = f[first + 2] + f[first + 3], f[first + 2] - f[first + 3]
    return s, d, s2, d2


def off_equilibrium(f):
    sx, dx = f[1] + f[2], f[1] - f[2]
    sy, dy = f[3] + f[4], f[3] - f[4]
    sz, dz = f[5] + f[6], f[5] - f[6]
    s7, d7, s9, d9 = edge(f, 7)
    s11, d11, s13, d13 = edge(f, 11)
    s15, d15, s17, d17 = edge(f, 15)
    m220, m110, m120, m210 = s7 + s9, s7 - s9, d7 + d9, d7 - d9
    m202, m101, m102, m201 = s11 + s13, s11 - s13, d11 + d13, d11 - d13
    m022, m011, m012, m021 = s15 + s17, s15 - s17, d15 + d17, d15 - d17
    m200, m020, m002 = sx + m220 + m202, sy + m220 + m022, sz + m202 + m022
    jx, jy, jz = dx + (m120 + m102), dy + (m210 + m012), dz + (m201 + m021)
    rho = f[0] + (sx + sy + sz) + (m220 + m202 + m022)
    inv = 1.0 / rho
    ux, uy, uz = jx * inv, jy * inv, jz * inv
    qx, qy, qz = jx * ux, jy * uy, jz * uz
    third = rho * (1.0 / 3.0)
    ninth = rho * (1.0 / 9.0) - (qx + qy + qz) * (1.0 / 6.0)
    tx, ty, tz = jx * (1.0 / 3.0), jy * (1.0 / 3.0), jz * (1.0 / 3.0)
    e = {
        "200": RATE2 * (m200 - third - qx),
        "020": RATE2 * (m020 - third - qy),
        "002": RATE2 * (m002 - third - qz),
        "110": RATE2 * (m110 - jx * uy),
        "101": RATE2 * (m101 - jx * uz),
        "011": RATE2 * (m011 - jy * uz),
        "120": RATE3 * (m120 - tx),
        "102": RATE3 * (m102 - tx),
        "210": RATE3 * (m210 - ty),
        "012": RATE3 * (m012 - ty),
        "201": RATE3 * (m201 - tz),
        "021": RATE3 * (m021 - tz),
        "220": RATE4 * (m220 - ninth - 0.5 * (qx + qy)),
        "202": RATE4 * (m202 - ninth - 0.5 * (qx + qz)),
        "022": RATE4 * (m022 - ninth - 0.5 * (qy + qz)),
    }
    return (ux, uy, uz), e, (dx, dy, dz, d7, d9, d11, d13, d15, d17)


def spread(t, g, a, b):
    even, odd = t + g, t - g
    plus, minus = a + b, a - b
    return [even + plus, even - plus, odd + minus, odd - minus]


def correction(e):
    q = {k: 0.25 * v for k, v in e.items()}
    xy = spread(q["220"], q["110"], q["120"], q["210"])
    xz = spread(q["202"], q["101"], q["102"], q["201"])
    yz = spread(q["022"], q["011"], q["012"], q["021"])
    faces = []
    for second, fourth, odd in (
        ("200", ("220", "202"), ("120", "102")),
        ("020", ("220", "022"), ("210", "012")),
        ("002", ("202", "022"), ("201", "021")),
    ):
        mean = 0.5 * e[second] - 2.0 * (q[fourth[0]] + q[fourth[1]])
        lean = 2.0 * (q[odd[0]] + q[odd[1]])
        faces += [mean - lean, mean + lean]
    rest = (e["220"] + e["202"] + e["022"]) - (e["200"] + e["020"] + e["002"])
    return [rest] + faces + xy + xz + yz


def covector(b):
    hx, dx = 0.5 * (b[1] + b[2]), b[1] - b[2]
    hy, dy = 0.5 * (b[3] + b[4]), b[3] - b[4]
    hz, dz = 0.5 * (b[5] + b[6]), b[5] - b[6]
    s7, d7, s9, d9 = edge(b, 7)
    s11, d11, s13, d13 = edge(b, 11)
    s15, d15, s17, d17 = edge(b, 15)
    gx, gy, gz = hx - b[0], hy - b[0], hz - b[0]
    kx, ky, kz = 0.5 * dx, 0.5 * dy, 0.5 * dz
    t = {
        "200": gx,
        "020": gy,
        "002": gz,
        "110": 0.25 * (s7 - s9),
        "101": 0.25 * (s11 - s13),
        "011": 0.25 * (s15 - s17),
        "120": 0.25 * (d7 + d9) - kx,
        "102": 0.25 * (d11 + d13) - kx,
        "210": 0.25 * (d7 - d9) - ky,
        "012": 0.25 * (d15 + d17) - ky,
        "201": 0.25 * (d11 - d13) - kz,
        "021": 0.25 * (d15 - d17) - kz,
        "220": 0.25 * (s7 + s9) - gx - hy,
        "202": 0.25 * (s11 + s13) - gx - hz,
        "022": 0.25 * (s15 + s17) - gy - hz,
    }
    return t, (dx, dy, dz, d7, d9, d11, d13, d15, d17)


def pull_back(b, t, u, fraction):
    rates = {k: (RATE2, RATE3, RATE4)[sum(map(int, k)) - 2] for k in t}
    n = {k: rates[k] * v for k, v in t.items()}
    ux, uy, uz = u
    fourth = n["220"] + n["202"] + n["022"]
    second = n["200"] + n["020"] + n["002"]
    part = fourth * (1.0 / 3.0)
    ax = n["200"] + part - 0.5 * n["022"]
    ay = n["020"] + part - 0.5 * n["202"]
    az = n["002"] + part - 0.5 * n["220"]
    rx = 2.0 * ax * ux + n["110"] * uy + n["101"] * uz
    ry = 2.0 * ay * uy + n["110"] * ux + n["011"] * uz
    rz = 2.0 * az * uz + n["101"] * ux + n["011"] * uy
    p0 = second * (1.0 / 3.0) + fourth * (1.0 / 9.0) - 0.5 * (rx * ux + ry * uy + rz * uz)
    px = rx + (n["120"] + n["102"]) * (1.0 / 3.0)
    py = ry + (n["210"] + n["012"]) * (1.0 / 3.0)
    pz = rz + (n["201"] + n["021"]) * (1.0 / 3.0)
    ex, ey, ez = p0 - n["200"], p0 - n["020"], p0 - n["002"]
    h = [p0, ex + px, ex - px, ey + py, ey - py, ez + pz, ez - pz]
    h += spread(ex - n["020"] - n["220"], -n["110"], px - n["120"], py - n["210"])
    h += spread(ex - n["002"] - n["202"], -n["101"], px - n["102"], pz - n["201"])
    h += spread(ey - n["002"] - n["022"], -n["011"], py - n["012"], pz - n["021"])
    open_part = 1.0 - fraction
    return [open_part * (b[i] + h[i]) + fraction * b[opposite[i]] for i in range(Q)]


def store_wrapped(put, first, step, value):
    row = first + step
    if row < 0:
        put(0, value[1:])
        put(CY - 1, value[:1])
    elif row + TILE > CY:
        put(row, value[:-1])
        put(0, value[-1:])
    else:
        put(row, value)


def put_moved(field, i, x, yt, value, direction):
    cx, cy, cz = (direction * c for c in velocities[i])
    if cz:
        value = pltpu.roll(value, cz % NZ, axis=1)
    x = (x + cx) & (CX - 1) if cx else x

    def put(row, part):
        field[i, x, pl.ds(row, part.shape[0]), :] = part

    store_wrapped(put, yt * TILE, cy, value)


def by_parity(even, odd):
    is_odd = jnp.full(even.shape, lax.axis_index("gx") & 1, jnp.int32) == 1
    return jnp.where(is_odd, odd, even)


def x_faces(fields, direction, first, second):
    for n, field in enumerate(fields):
        pairs = zip(moving(0, 1, direction), moving(0, -1, direction))
        for k, (i_up, i_down) in enumerate(pairs):
            up, down = field[i_up, 0], field[i_down, CX - 1]
            line = pl.ds(n * FACE + k * CY, CY)
            first[line, :] = by_parity(down, up)
            second[line, :] = by_parity(up, down)


def x_arrived(sign, line, first, second):
    a, b = first[line, :], second[line, :]
    return by_parity(a, b) if sign == 1 else by_parity(b, a)


def y_faces(fields, direction, y_up, y_down):
    for n, field in enumerate(fields):
        for sign, row, message in ((1, 0, y_up), (-1, CY - 1, y_down)):
            for k, i in enumerate(moving(1, sign, direction)):
                for x in range(CX):
                    message[pl.ds(n * FACE + k * CX + x, 1), :] = field[i, x, pl.ds(row, 1), :]


def fill_x(fields, direction, first, second):
    for n, field in enumerate(fields):
        for sign, x in ((1, 0), (-1, CX - 1)):
            for k, i in enumerate(moving(0, sign, direction)):
                line = pl.ds(n * FACE + k * CY, CY)
                field[i, x] = x_arrived(sign, line, first, second)


def fill_y(fields, direction, y_low, y_high):
    for n, field in enumerate(fields):
        for sign, row, message in ((1, 0, y_low), (-1, CY - 1, y_high)):
            for k, i in enumerate(moving(1, sign, direction)):
                for x in range(CX):
                    field[i, x, pl.ds(row, 1), :] = message[pl.ds(n * FACE + k * CX + x, 1), :]


def rows(yt):
    return pl.ds(yt * TILE, TILE)


def unrolled(start, stop, count, step):
    @pl.loop(0, (stop - start) // count)
    def _(n):
        for k in range(count):
            step(start + n * count + k)


def iota(shape, dim):
    return lax.broadcasted_iota(jnp.int32, shape, dim)


def column(row, pick):
    return jnp.sum(jnp.where(pick, row, 0.0), axis=1, keepdims=True)


def block_numbers(owners, slots, table, y_up, y_down):
    shape = (64, 64)
    row, lane = iota(shape, 0), iota(shape, 1)
    same = row == lane
    owner_row, slot_row = owners[...].astype(jnp.float32), slots[...].astype(jnp.float32)
    owner_col = column(owner_row, same)
    earlier = (owner_row == owner_col) & (lane < row)
    rank = jnp.sum(jnp.where(earlier, 1.0, 0.0), axis=1, keepdims=True)
    number = owner_col * 1024.0 + column(slot_row, same) * 4.0 + rank
    wide = (64, NZ)
    spot = iota(wide, 1) == (iota(wide, 0) & 7) + 1
    spread_out = jnp.where(spot, number, 0.0)
    table[...] = jnp.zeros((16, NZ), jnp.float32)
    for xb in range(8):
        line = jnp.sum(spread_out[xb * 8 : xb * 8 + 8], axis=0, keepdims=True)
        table[pl.ds(xb + 1, 1), :] = line
    held = table[...]
    eye = iota((16, NZ), 0) == iota((16, NZ), 1)
    for yb, message in ((8, y_up), (1, y_down)):
        part = jnp.where(eye, held[:, yb : yb + 1], 0.0)
        message[pl.ds(META, 1), :] = jnp.sum(part, axis=0, keepdims=True)


def solidity(porosity, porous, walls):
    wall = walls == 1
    panel = porous.astype(jnp.float32)
    return jnp.where(wall, 1.0, panel * porosity), jnp.where(wall, 0.0, panel)


def edge_kernel(
    f_hbm, porosity_hbm, porous_hbm, walls_hbm, owners_hbm, slots_hbm,
    table, yu, yd, f, porosity, porous, walls, owners, slots, sems,
):
    numbers = [
        pltpu.make_async_copy(owners_hbm, owners, sems.at[0]),
        pltpu.make_async_copy(slots_hbm, slots, sems.at[1]),
    ]
    lines = []
    for n, y in enumerate((CY - 1, 0)):
        lines += [
            pltpu.make_async_copy(f_hbm.at[:, :, y, :], f.at[n], sems.at[4 * n + 2]),
            pltpu.make_async_copy(porosity_hbm.at[:, y, :], porosity.at[n], sems.at[4 * n + 3]),
            pltpu.make_async_copy(porous_hbm.at[:, y, :], porous.at[n], sems.at[4 * n + 4]),
            pltpu.make_async_copy(walls_hbm.at[:, y, :], walls.at[n], sems.at[4 * n + 5]),
        ]
    for copy in numbers + lines:
        copy.start()
    for copy in numbers:
        copy.wait()
    block_numbers(owners, slots, table, yu, yd)
    for copy in lines:
        copy.wait()
    for n, (sign, message) in enumerate(((1, yu), (-1, yd))):
        for xt in range(CX // TILE):
            at = (n, rows(xt))
            pops = [f[n, i, rows(xt), :] for i in range(Q)]
            fraction, open_panel = solidity(porosity[at], porous[at], walls[at])
            c = correction(off_equilibrium(pops)[1])
            for k, i in enumerate(moving(1, sign, 1)):
                relaxed = pops[i] - c[i]
                change = pops[opposite[i]] - relaxed
                pair = (relaxed + fraction * change, open_panel * change)
                for field, value in enumerate(pair):
                    cx, _, cz = velocities[i]
                    if cz:
                        value = pltpu.roll(value, cz % NZ, axis=1)

                    def put(row, part, base=field * FACE + k * CX, message=message):
                        message[pl.ds(base + row, part.shape[0]), :] = part

                    store_wrapped(put, xt * TILE, cx, value)


def forward_kernel(
    f_hbm, porosity_hbm, porous_hbm, walls_hbm, adjoint_hbm,
    moved, gap, adjoint, frac, mask, vel,
    f, porosity, porous, walls, f_sems, sems,
):
    def planes(n):
        part = pl.ds(n * PLANES, PLANES)
        return pltpu.make_async_copy(f_hbm.at[:, part], f.at[:, part], f_sems.at[n])

    small = [
        pltpu.make_async_copy(porosity_hbm, porosity, sems.at[0]),
        pltpu.make_async_copy(porous_hbm, porous, sems.at[1]),
        pltpu.make_async_copy(walls_hbm, walls, sems.at[2]),
    ]
    later = pltpu.make_async_copy(adjoint_hbm, adjoint, sems.at[3])
    for copy in small:
        copy.start()
    for n in range(CX // PLANES):
        planes(n).start()
    later.start()
    for copy in small:
        copy.wait()

    def plane(x):
        for yt in range(CY // TILE):
            at = (x, rows(yt))
            pops = [f[i, x, rows(yt), :] for i in range(Q)]
            fraction, open_panel = solidity(porosity[at], porous[at], walls[at])
            frac[at] = fraction
            mask[at] = open_panel
            u, e, _ = off_equilibrium(pops)
            for axis in range(3):
                vel[axis, x, rows(yt), :] = u[axis]
            c = correction(e)
            for i in range(Q):
                relaxed = pops[i] - c[i]
                change = pops[opposite[i]] - relaxed
                put_moved(gap, i, x, yt, open_panel * change, 1)
                put_moved(moved, i, x, yt, relaxed + fraction * change, 1)

    @pl.loop(0, CX // PLANES)
    def _(n):
        planes(n).wait()
        for k in range(PLANES):
            plane(n * PLANES + k)

    later.wait()


def turn_kernel(moved_in, gap_in, table, y_low, y_high, moved, gap, ext, first, second):
    del moved_in, gap_in
    fill_y((moved, gap), 1, y_low, y_high)
    x_faces((moved, gap), 1, first, second)
    shape = (16, NZ)
    row, lane = iota(shape, 0), iota(shape, 1)
    low = column(y_low[pl.ds(META, 1), :], row == lane)
    high = column(y_high[pl.ds(META, 1), :], row == lane)
    held = jnp.where(lane == 0, low, jnp.where(lane == 9, high, table[...]))
    ext[...] = held
    first[pl.ds(META, 1), :] = by_parity(held[1:2], held[8:9])
    second[pl.ds(META, 1), :] = by_parity(held[8:9], held[1:2])


def late_blocks(xb, halves, take, adjoint, frac, mask, late, sums):
    for yt in range(CY // TILE):
        parts = {}
        for half in halves:
            x = xb * 2 + half
            at = (x, rows(yt))
            read = [take(0, i, x, yt) for i in range(Q)]
            u, e, df = off_equilibrium(read)
            b = [adjoint[i, x, rows(yt), :] for i in range(Q)]
            t, db = covector(b)
            total = sum(t[k] * e[k] for k in t) - sum(p * q for p, q in zip(db, df))
            total = mask[at] * total
            out = pull_back(b, t, u, frac[at])
            key = (0, 0)
            parts[key] = parts[key] + total if key in parts else total
            for i in range(Q):
                cx, cy, _ = velocities[i]
                key = ((half - cx) // 2, cy)
                early = out[i] * take(1, i, x, yt)
                parts[key] = parts[key] + early if key in parts else early
                put_moved(late, i, x, yt, out[i], -1)
        for (step, cy), part in parts.items():
            at = (xb + 1 + step, pl.ds(PAD_Y + yt * TILE - cy, TILE))
            sums[at] = sums[at] + part


def late_kernel(moved, gap, adjoint, frac, mask, late, sums):
    fields = (moved, gap)
    sums[...] = jnp.zeros((EXT_XB, EXT_Y, NZ), jnp.float32)

    def take(n, i, x, yt):
        return fields[n][i, x, rows(yt), :]

    def step(xb, halves=(0, 1)):
        late_blocks(xb, halves, take, adjoint, frac, mask, late, sums)

    step(0, (1,))
    step(CX // 2 - 1, (0,))
    unrolled(1, CX // 2 - 1, 2, step)


def late_rest_kernel(
    late_in, sums_in, moved, gap, ext_in, first, second, adjoint, frac, mask,
    late, sums, xf, xs, yu, yd, send_hbm, ext, ring, owner_of, scaled, send, sem,
):
    del late_in, sums_in
    fields = (moved, gap)

    def take(n, i, x, yt):
        cx = velocities[i][0]
        if (cx, x) in ((1, 0), (-1, CX - 1)):
            start = n * FACE + moving(0, cx, 1).index(i) * CY + yt * TILE
            return x_arrived(cx, pl.ds(start, TILE), first, second)
        return fields[n][i, x, rows(yt), :]

    for xb, half in ((0, 0), (CX // 2 - 1, 1)):
        late_blocks(xb, (half,), take, adjoint, frac, mask, late, sums)

    row = iota((16, NZ), 0)
    numbers = pl.ds(META, 1)
    held = jnp.where(row == 0, x_arrived(1, numbers, first, second), ext_in[...])
    ext[...] = jnp.where(row == 9, x_arrived(-1, numbers, first, second), held)

    def put_lines(start, number, spot, total):
        number = number.astype(jnp.int32)
        lane = iota((total.shape[0], NZ), 1)
        spot = spot + (number & 3) if isinstance(spot, int) else spot(number & 3)
        line = pl.ds(start, total.shape[0])
        owner_of[line, :] = jnp.where(lane == jnp.right_shift(number, 10), 1.0, 0.0)
        patch = (jnp.right_shift(number, 2) & 255).astype(jnp.float32)
        value = jnp.where(lane == spot, jnp.sum(total, axis=1, keepdims=True), 0.0)
        scaled[line, :] = jnp.where(lane == spot + SLOT_LANE, patch, value)

    pick = iota((8, NZ), 1) == iota((8, NZ), 0) + 1
    for xb in range(EXT_XB):
        total = sums[xb, pl.ds(PAD_Y, 8, stride=2), :] + sums[xb, pl.ds(PAD_Y + 1, 8, stride=2), :]
        spot = 2 if xb == 0 else 4 if xb == 9 else 0
        put_lines(xb * 8, column(ext[pl.ds(xb, 1), :], pick), spot, total)
    ring[...] = jnp.zeros((32, NZ), jnp.float32)
    for xb in range(EXT_XB):
        ring[pl.ds(xb, 1), :] = sums[xb, pl.ds(PAD_Y - 1, 1), :]
        ring[pl.ds(16 + xb, 1), :] = sums[xb, pl.ds(PAD_Y + CY, 1), :]
    row = iota((16, 1), 0)
    for n, (face, corner, lane) in enumerate(((6, 10, 0), (8, 12, 9))):

        def spot(rank, face=face, corner=corner):
            side = jnp.where(row == 9, corner + 1, face + rank)
            return jnp.where(row == 0, corner, side)

        pick = (iota((16, NZ), 1) == lane) & (iota((16, NZ), 0) < EXT_XB)
        total = ring[pl.ds(16 * n, 16), :]
        put_lines(RING + 16 * n, column(ext[...], pick), spot, total)
    send[pl.ds(0, DEVICES, stride=2), :] = lax.dot_general(
        owner_of[...],
        scaled[...],
        (((0,), (0,)), ((), ())),
        precision=lax.Precision.HIGHEST,
        preferred_element_type=jnp.float32,
    )
    for there, i, x, y in corners(1):
        send[pl.ds(2 * there + 1, 1), :] = late[i, x, pl.ds(y, 1), :]
    copy = pltpu.make_async_copy(send, send_hbm, sem)
    copy.start()
    x_faces((late,), -1, xf, xs)
    y_faces((late,), -1, yu, yd)
    copy.wait()


def corners(direction):
    gx, gy = lax.axis_index("gx"), lax.axis_index("gy")
    for ex in (1, -1):
        for ey in (1, -1):
            there_x = (gx + direction * ex) & (N_GX - 1)
            there_y = (gy + direction * ey) & (N_GY - 1)
            i = velocities.index((-ex, -ey, 0))
            x, y = 0 if ex == 1 else CX - 1, 0 if ey == 1 else CY - 1
            yield there_x * N_GY + there_y, i, x, y


def early_plane(x, late, frac, vel, put):
    for yt in range(CY // TILE):
        b = [late[i, x, rows(yt), :] for i in range(Q)]
        t, _ = covector(b)
        u = [vel[axis, x, rows(yt), :] for axis in range(3)]
        result = pull_back(b, t, u, frac[x, rows(yt)])
        for i in range(Q):
            put(i, yt, result[i])


def early_kernel(late_in, yl, yh, frac, vel, late, out, hold, sems):
    del late_in
    fill_y((late,), -1, yl, yh)

    def planes(n):
        part = pl.ds(1 + n * 2, 2)
        return pltpu.make_async_copy(hold.at[:, part], out.at[:, part], sems.at[n])

    @pl.loop(0, CX // 2 - 1)
    def _(n):
        for k in range(2):
            x = 1 + n * 2 + k

            def put(i, yt, value, x=x):
                hold[i, x, rows(yt), :] = value

            early_plane(x, late, frac, vel, put)
        planes(n).start()

    for n in range(CX // 2 - 1):
        planes(n).wait()


def last_kernel(
    out_in, late_in, first, second, got, frac, vel, late, out, patch_out, hold, patch, sems
):
    del out_in, late_in
    fill_x((late,), -1, first, second)
    for here, i, x, y in corners(-1):
        late[i, x, pl.ds(y, 1), :] = got[pl.ds(2 * here + 1, 1), :]
    copies = []
    for n, x in enumerate((0, CX - 1)):

        def put(i, yt, value, n=n):
            hold[n, i, rows(yt), :] = value

        early_plane(x, late, frac, vel, put)
        copies.append(pltpu.make_async_copy(hold.at[n], out.at[:, x], sems.at[n]))
        copies[n].start()
    data = got[pl.ds(0, DEVICES, stride=2), :].T
    part = 64
    for start in range(0, PATCH_DEV, part):
        number = (iota((part, DEVICES), 0) + start).astype(jnp.float32)
        total = jnp.zeros((part, DEVICES), jnp.float32)
        for k in range(PARTS):
            hit = data[SLOT_LANE + k : SLOT_LANE + k + 1] == number
            total = total + jnp.where(hit, data[k : k + 1], 0.0)
        patch[:, pl.ds(start, part)] = jnp.sum(total, axis=1)[None]
    copies.append(pltpu.make_async_copy(patch, patch_out, sems.at[2]))
    copies[2].start()
    for copy in copies:
        copy.wait()


VMEM = pl.BlockSpec(memory_space=pltpu.VMEM)
ANY = pl.BlockSpec(memory_space=pl.ANY)
LIMIT = 8 * 2**20


def vmem(*shape):
    return pltpu.VMEM(shape, jnp.float32)


def call(kernel, ins, outs, scratch=(), aliases=None, flops=0, hbm_ins=0, hbm_outs=()):
    held = [pltpu.with_memory_space_constraint(x, pltpu.HBM) for x in ins[:hbm_ins]]
    held += [pltpu.with_memory_space_constraint(x, pltpu.VMEM) for x in ins[hbm_ins:]]
    return pl.pallas_call(
        kernel,
        out_shape=[*outs, *hbm_outs],
        in_specs=[ANY] * hbm_ins + [VMEM] * (len(ins) - hbm_ins),
        out_specs=[VMEM] * len(outs) + [ANY] * len(hbm_outs),
        scratch_shapes=list(scratch),
        input_output_aliases=aliases or {},
        compiler_params=pltpu.CompilerParams(vmem_limit_bytes=LIMIT),
        cost_estimate=pl.CostEstimate(flops=flops, bytes_accessed=0, transcendentals=0),
    )(*held)


FIELD = vmem(Q, CX, CY, NZ)
NODE = vmem(CX, CY, NZ)
MESSAGE = vmem(MESSAGE_ROWS, NZ)
SHORT_MESSAGE = vmem(FACE, NZ)
LINES = vmem(LINE_COUNT, NZ)


def shift(block, axis, step):
    count = lax.axis_size(axis)
    return lax.ppermute(block, axis, [(i, (i + step) % count) for i in range(count)])


def swap(block, axis, step):
    count = lax.axis_size(axis)
    return lax.ppermute(
        block, axis, [(i, (i + (-step if i % 2 else step)) % count) for i in range(count)]
    )


def body(populations, porosity, adjoint_in, porous, walls, owners, slots):
    ints = pltpu.VMEM((CX, CY, NZ), jnp.int32)
    dma = pltpu.SemaphoreType.DMA
    table, y_up, y_down = call(
        edge_kernel,
        [populations, porosity, porous, walls, owners.reshape(1, 64), slots.reshape(1, 64)],
        [vmem(16, NZ), MESSAGE, MESSAGE],
        scratch=[vmem(2, Q, CX, NZ), vmem(2, CX, NZ)]
        + [pltpu.VMEM((2, CX, NZ), jnp.int32)] * 2
        + [pltpu.VMEM((1, 64), jnp.int32)] * 2
        + [dma((10,))],
        hbm_ins=6,
    )
    y_low = shift(y_up, "gy", 1)
    y_high = shift(y_down, "gy", -1)
    moved, gap, adjoint, frac, mask, vel = call(
        forward_kernel,
        [populations, porosity, porous, walls, adjoint_in],
        [FIELD] * 3 + [NODE] * 2 + [vmem(3, CX, CY, NZ)],
        scratch=[FIELD, NODE, ints, ints, dma((CX // PLANES,)), dma((4,))],
        hbm_ins=5,
        flops=20_000_000,
    )
    moved, gap, ext, first, second = call(
        turn_kernel,
        [moved, gap, table, y_low, y_high],
        [FIELD, FIELD, vmem(16, NZ), MESSAGE, MESSAGE],
        aliases={0: 0, 1: 1},
    )
    first = swap(first, "gx", -1)
    second = swap(second, "gx", 1)
    late, sums = call(
        late_kernel,
        [moved, gap, adjoint, frac, mask],
        [FIELD, vmem(EXT_XB, EXT_Y, NZ)],
        flops=20_000_000,
    )
    late, _, first, second, y_up, y_down, send = call(
        late_rest_kernel,
        [late, sums, moved, gap, ext, first, second, adjoint, frac, mask],
        [FIELD, vmem(EXT_XB, EXT_Y, NZ)] + [SHORT_MESSAGE] * 4,
        hbm_outs=[jax.ShapeDtypeStruct((2 * DEVICES, NZ), jnp.float32)],
        scratch=[vmem(16, NZ), vmem(32, NZ), LINES, LINES, vmem(2 * DEVICES, NZ), dma],
        aliases={0: 0, 1: 1},
    )
    got = lax.all_to_all(send, ("gx", "gy"), split_axis=0, concat_axis=0, tiled=True)
    y_low = shift(y_up, "gy", 1)
    y_high = shift(y_down, "gy", -1)
    first = swap(first, "gx", -1)
    second = swap(second, "gx", 1)
    adjoint_shape = jax.ShapeDtypeStruct((Q, CX, CY, NZ), jnp.float32)
    late, adjoint_out = call(
        early_kernel,
        [late, y_low, y_high, frac, vel],
        [FIELD],
        hbm_outs=[adjoint_shape],
        scratch=[FIELD, dma((CX // 2 - 1,))],
        aliases={0: 0},
        flops=20_000_000,
    )
    _, adjoint_out, patch = call(
        last_kernel,
        [adjoint_out, late, first, second, got, frac, vel],
        [FIELD],
        hbm_ins=1,
        hbm_outs=[adjoint_shape, jax.ShapeDtypeStruct((1, PATCH_DEV), jnp.float32)],
        scratch=[vmem(2, Q, CY, NZ), vmem(1, PATCH_DEV), dma((3,))],
        aliases={0: 1, 1: 0},
    )
    return adjoint_out, patch.reshape(PATCH_DEV)


def solution(mesh):
    return jax.shard_map(
        body,
        mesh=mesh,
        in_specs=(
            P(None, "gx", "gy", None),
            P("gx", "gy", None),
            P(None, "gx", "gy", None),
            P("gx", "gy", None),
            P("gx", "gy", None),
            P("gx", "gy", None, None),
            P("gx", "gy", None),
        ),
        out_specs=(P(None, "gx", "gy", None), P(("gx", "gy"))),
        check_vma=False,
    )
```

```python
import jax
import jax.numpy as jnp
from jax import lax
from jax.experimental import pallas as pl
from jax.experimental.pallas import tpu as pltpu
from jax.sharding import PartitionSpec as P

Q = 19
CX = 16
CY = 16
NZ = 128
TILE = 8
PAD_Y = 8
EXT_Y = 32
EXT_XB = 10
RING = 80
LINE_COUNT = 112
DEVICES = 128
N_GX, N_GY = 8, 16
PATCH_DEV = 256
SLOT_LANE = 64
PARTS = 14
FACE = 80
META = 160
MESSAGE_ROWS = 168
PLANES = 4

velocities = [
    (0, 0, 0),
    (1, 0, 0),
    (-1, 0, 0),
    (0, 1, 0),
    (0, -1, 0),
    (0, 0, 1),
    (0, 0, -1),
    (1, 1, 0),
    (-1, -1, 0),
    (1, -1, 0),
    (-1, 1, 0),
    (1, 0, 1),
    (-1, 0, -1),
    (1, 0, -1),
    (-1, 0, 1),
    (0, 1, 1),
    (0, -1, -1),
    (0, 1, -1),
    (0, -1, 1),
]
opposite = [0, 2, 1, 4, 3, 6, 5, 8, 7, 10, 9, 12, 11, 14, 13, 16, 15, 18, 17]
RATE2, RATE3, RATE4 = 1.25, 1.5, 1.4


def moving(axis, sign, direction):
    return [i for i in range(Q) if direction * velocities[i][axis] == sign]


def edge(f, first):
    s, d = f[first] + f[first + 1], f[first] - f[first + 1]
    s2, d2 = f[first + 2] + f[first + 3], f[first + 2] - f[first + 3]
    return s, d, s2, d2


def off_equilibrium(f):
    sx, dx = f[1] + f[2], f[1] - f[2]
    sy, dy = f[3] + f[4], f[3] - f[4]
    sz, dz = f[5] + f[6], f[5] - f[6]
    s7, d7, s9, d9 = edge(f, 7)
    s11, d11, s13, d13 = edge(f, 11)
    s15, d15, s17, d17 = edge(f, 15)
    m220, m110, m120, m210 = s7 + s9, s7 - s9, d7 + d9, d7 - d9
    m202, m101, m102, m201 = s11 + s13, s11 - s13, d11 + d13, d11 - d13
    m022, m011, m012, m021 = s15 + s17, s15 - s17, d15 + d17, d15 - d17
    m200, m020, m002 = sx + m220 + m202, sy + m220 + m022, sz + m202 + m022
    jx, jy, jz = dx + (m120 + m102), dy + (m210 + m012), dz + (m201 + m021)
    rho = f[0] + (sx + sy + sz) + (m220 + m202 + m022)
    inv = 1.0 / rho
    ux, uy, uz = jx * inv, jy * inv, jz * inv
    qx, qy, qz = jx * ux, jy * uy, jz * uz
    third = rho * (1.0 / 3.0)
    ninth = rho * (1.0 / 9.0) - (qx + qy + qz) * (1.0 / 6.0)
    tx, ty, tz = jx * (1.0 / 3.0), jy * (1.0 / 3.0), jz * (1.0 / 3.0)
    e = {
        "200": RATE2 * (m200 - third - qx),
        "020": RATE2 * (m020 - third - qy),
        "002": RATE2 * (m002 - third - qz),
        "110": RATE2 * (m110 - jx * uy),
        "101": RATE2 * (m101 - jx * uz),
        "011": RATE2 * (m011 - jy * uz),
        "120": RATE3 * (m120 - tx),
        "102": RATE3 * (m102 - tx),
        "210": RATE3 * (m210 - ty),
        "012": RATE3 * (m012 - ty),
        "201": RATE3 * (m201 - tz),
        "021": RATE3 * (m021 - tz),
        "220": RATE4 * (m220 - ninth - 0.5 * (qx + qy)),
        "202": RATE4 * (m202 - ninth - 0.5 * (qx + qz)),
        "022": RATE4 * (m022 - ninth - 0.5 * (qy + qz)),
    }
    return (ux, uy, uz), e, (dx, dy, dz, d7, d9, d11, d13, d15, d17)


def spread(t, g, a, b):
    even, odd = t + g, t - g
    plus, minus = a + b, a - b
    return [even + plus, even - plus, odd + minus, odd - minus]


def correction(e):
    q = {k: 0.25 * v for k, v in e.items()}
    xy = spread(q["220"], q["110"], q["120"], q["210"])
    xz = spread(q["202"], q["101"], q["102"], q["201"])
    yz = spread(q["022"], q["011"], q["012"], q["021"])
    faces = []
    for second, fourth, odd in (
        ("200", ("220", "202"), ("120", "102")),
        ("020", ("220", "022"), ("210", "012")),
        ("002", ("202", "022"), ("201", "021")),
    ):
        mean = 0.5 * e[second] - 2.0 * (q[fourth[0]] + q[fourth[1]])
        lean = 2.0 * (q[odd[0]] + q[odd[1]])
        faces += [mean - lean, mean + lean]
    rest = (e["220"] + e["202"] + e["022"]) - (e["200"] + e["020"] + e["002"])
    return [rest] + faces + xy + xz + yz


def covector(b):
    hx, dx = 0.5 * (b[1] + b[2]), b[1] - b[2]
    hy, dy = 0.5 * (b[3] + b[4]), b[3] - b[4]
    hz, dz = 0.5 * (b[5] + b[6]), b[5] - b[6]
    s7, d7, s9, d9 = edge(b, 7)
    s11, d11, s13, d13 = edge(b, 11)
    s15, d15, s17, d17 = edge(b, 15)
    gx, gy, gz = hx - b[0], hy - b[0], hz - b[0]
    kx, ky, kz = 0.5 * dx, 0.5 * dy, 0.5 * dz
    t = {
        "200": gx,
        "020": gy,
        "002": gz,
        "110": 0.25 * (s7 - s9),
        "101": 0.25 * (s11 - s13),
        "011": 0.25 * (s15 - s17),
        "120": 0.25 * (d7 + d9) - kx,
        "102": 0.25 * (d11 + d13) - kx,
        "210": 0.25 * (d7 - d9) - ky,
        "012": 0.25 * (d15 + d17) - ky,
        "201": 0.25 * (d11 - d13) - kz,
        "021": 0.25 * (d15 - d17) - kz,
        "220": 0.25 * (s7 + s9) - gx - hy,
        "202": 0.25 * (s11 + s13) - gx - hz,
        "022": 0.25 * (s15 + s17) - gy - hz,
    }
    return t, (dx, dy, dz, d7, d9, d11, d13, d15, d17)


def pull_back(b, t, u, fraction):
    rates = {k: (RATE2, RATE3, RATE4)[sum(map(int, k)) - 2] for k in t}
    n = {k: rates[k] * v for k, v in t.items()}
    ux, uy, uz = u
    fourth = n["220"] + n["202"] + n["022"]
    second = n["200"] + n["020"] + n["002"]
    part = fourth * (1.0 / 3.0)
    ax = n["200"] + part - 0.5 * n["022"]
    ay = n["020"] + part - 0.5 * n["202"]
    az = n["002"] + part - 0.5 * n["220"]
    rx = 2.0 * ax * ux + n["110"] * uy + n["101"] * uz
    ry = 2.0 * ay * uy + n["110"] * ux + n["011"] * uz
    rz = 2.0 * az * uz + n["101"] * ux + n["011"] * uy
    p0 = second * (1.0 / 3.0) + fourth * (1.0 / 9.0) - 0.5 * (rx * ux + ry * uy + rz * uz)
    px = rx + (n["120"] + n["102"]) * (1.0 / 3.0)
    py = ry + (n["210"] + n["012"]) * (1.0 / 3.0)
    pz = rz + (n["201"] + n["021"]) * (1.0 / 3.0)
    ex, ey, ez = p0 - n["200"], p0 - n["020"], p0 - n["002"]
    h = [p0, ex + px, ex - px, ey + py, ey - py, ez + pz, ez - pz]
    h += spread(ex - n["020"] - n["220"], -n["110"], px - n["120"], py - n["210"])
    h += spread(ex - n["002"] - n["202"], -n["101"], px - n["102"], pz - n["201"])
    h += spread(ey - n["002"] - n["022"], -n["011"], py - n["012"], pz - n["021"])
    open_part = 1.0 - fraction
    return [open_part * (b[i] + h[i]) + fraction * b[opposite[i]] for i in range(Q)]


def store_wrapped(put, first, step, value):
    row = first + step
    if row < 0:
        put(0, value[1:])
        put(CY - 1, value[:1])
    elif row + TILE > CY:
        put(row, value[:-1])
        put(0, value[-1:])
    else:
        put(row, value)


def put_moved(field, i, x, yt, value, direction):
    cx, cy, cz = (direction * c for c in velocities[i])
    if cz:
        value = pltpu.roll(value, cz % NZ, axis=1)
    x = (x + cx) & (CX - 1) if cx else x

    def put(row, part):
        field[i, x, pl.ds(row, part.shape[0]), :] = part

    store_wrapped(put, yt * TILE, cy, value)


def by_parity(axis, even, odd):
    is_odd = jnp.full(even.shape, lax.axis_index(axis) & 1, jnp.int32) == 1
    return jnp.where(is_odd, odd, even)


def pair_up(up, down, first, second):
    first[...] = by_parity("gx", down[...], up[...])
    second[...] = by_parity("gx", up[...], down[...])


def x_arrived(sign, line, first, second):
    a, b = first[line, :], second[line, :]
    return by_parity("gx", a, b) if sign == 1 else by_parity("gx", b, a)


def y_arrived(sign, line, low, high):
    return low[line, :] if sign == 1 else high[line, :]


def x_faces(fields, direction, x_up, x_down):
    for n, field in enumerate(fields):
        for sign, x, message in ((1, 0, x_up), (-1, CX - 1, x_down)):
            for k, i in enumerate(moving(0, sign, direction)):
                message[pl.ds(n * FACE + k * CY, CY), :] = field[i, x]


def y_faces(field, y_up, y_down):
    for sign, row, message in ((1, 0, y_up), (-1, CY - 1, y_down)):
        for k, i in enumerate(moving(1, sign, -1)):
            for x in range(CX):
                message[pl.ds(k * CX + x, 1), :] = field[i, x, pl.ds(row, 1), :]


def fill_x(fields, direction, first, second):
    for n, field in enumerate(fields):
        for sign, x in ((1, 0), (-1, CX - 1)):
            for k, i in enumerate(moving(0, sign, direction)):
                line = pl.ds(n * FACE + k * CY, CY)
                field[i, x] = x_arrived(sign, line, first, second)


def fill_y(fields, direction, first, second):
    for n, field in enumerate(fields):
        for sign, row in ((1, 0), (-1, CY - 1)):
            for k, i in enumerate(moving(1, sign, direction)):
                line = pl.ds(n * FACE + k * CX, CX)
                face = y_arrived(sign, line, first, second)
                for x in range(CX):
                    field[i, x, pl.ds(row, 1), :] = face[x : x + 1]


def rows(yt):
    return pl.ds(yt * TILE, TILE)


def unrolled(start, stop, count, step):
    @pl.loop(0, (stop - start) // count)
    def _(n):
        for k in range(count):
            step(start + n * count + k)


def iota(shape, dim):
    return lax.broadcasted_iota(jnp.int32, shape, dim)


def column(row, pick):
    return jnp.sum(jnp.where(pick, row, 0.0), axis=1, keepdims=True)


def block_numbers(owners, slots, table, y_up, y_down):
    shape = (64, 64)
    row, lane = iota(shape, 0), iota(shape, 1)
    same = row == lane
    owner_row, slot_row = owners[...].astype(jnp.float32), slots[...].astype(jnp.float32)
    owner_col = column(owner_row, same)
    earlier = (owner_row == owner_col) & (lane < row)
    rank = jnp.sum(jnp.where(earlier, 1.0, 0.0), axis=1, keepdims=True)
    number = owner_col * 1024.0 + column(slot_row, same) * 4.0 + rank
    wide = (64, NZ)
    spot = iota(wide, 1) == (iota(wide, 0) & 7) + 1
    spread_out = jnp.where(spot, number, 0.0)
    table[...] = jnp.zeros((16, NZ), jnp.float32)
    for xb in range(8):
        line = jnp.sum(spread_out[xb * 8 : xb * 8 + 8], axis=0, keepdims=True)
        table[pl.ds(xb + 1, 1), :] = line
    held = table[...]
    eye = iota((16, NZ), 0) == iota((16, NZ), 1)
    for yb, message in ((8, y_up), (1, y_down)):
        part = jnp.where(eye, held[:, yb : yb + 1], 0.0)
        message[pl.ds(META, 1), :] = jnp.sum(part, axis=0, keepdims=True)


def solidity(porosity, porous, walls):
    wall = walls == 1
    panel = porous.astype(jnp.float32)
    return jnp.where(wall, 1.0, panel * porosity), jnp.where(wall, 0.0, panel)


def edge_kernel(
    f_hbm, porosity_hbm, porous_hbm, walls_hbm, owners_hbm, slots_hbm,
    table, y_up, y_down, f, porosity, porous, walls, owners, slots, sems,
):
    numbers = [
        pltpu.make_async_copy(owners_hbm, owners, sems.at[0]),
        pltpu.make_async_copy(slots_hbm, slots, sems.at[1]),
    ]
    faces = [(1, CY - 1, y_up), (-1, 0, y_down)]
    lines = []
    for n, (_, y, _) in enumerate(faces):
        copies = [pltpu.make_async_copy(f_hbm.at[:, :, y, :], f.at[n], sems.at[4 * n + 2])]
        for k, (source, target) in enumerate(
            ((porosity_hbm, porosity), (porous_hbm, porous), (walls_hbm, walls))
        ):
            node = source.at[:, y, :]
            copies.append(pltpu.make_async_copy(node, target.at[n], sems.at[4 * n + 3 + k]))
        lines.append(copies)
    for copy in sum(lines, numbers):
        copy.start()
    for copy in numbers:
        copy.wait()
    block_numbers(owners, slots, table, y_up, y_down)
    for n, (sign, _, message) in enumerate(faces):
        for copy in lines[n]:
            copy.wait()
        for tile in range(CX // TILE):
            at = (n, rows(tile))
            pops = [f[n, i, rows(tile), :] for i in range(Q)]
            fraction, open_panel = solidity(porosity[at], porous[at], walls[at])
            c = correction(off_equilibrium(pops)[1])
            for k, i in enumerate(moving(1, sign, 1)):
                relaxed = pops[i] - c[i]
                change = pops[opposite[i]] - relaxed
                pair = (relaxed + fraction * change, open_panel * change)
                for field, value in enumerate(pair):
                    if velocities[i][2]:
                        value = pltpu.roll(value, velocities[i][2] % NZ, axis=1)

                    def put(row, part, base=field * FACE + k * CX, message=message):
                        message[pl.ds(base + row, part.shape[0]), :] = part

                    store_wrapped(put, tile * TILE, velocities[i][0], value)


def turn_kernel(y_first, y_second, frac, first, second, up, down):
    del frac
    for sx, message in ((1, up), (-1, down)):
        for n, sy in enumerate((1, -1)):
            k = moving(1, sy, 1).index(velocities.index((sx, sy, 0)))
            row = k * CX + (0 if sx == 1 else CX - 1)
            for field in range(2):
                line = pl.ds(field * FACE + row, 1)
                value = y_arrived(sy, line, y_first, y_second)
                message[pl.ds(2 * n + field, 1), :] = value
            numbers = y_arrived(sy, pl.ds(META, 1), y_first, y_second)
            message[pl.ds(4 + n, 1), :] = numbers
    pair_up(up, down, first, second)


def corner_arrived(sx, sy, row, messages):
    n = 0 if sy == 1 else 1
    line = pl.ds(4 + n if row == 2 else 2 * n + row, 1)
    return x_arrived(sx, line, *messages)


def forward_kernel(
    f_hbm, porosity_hbm, porous_hbm, walls_hbm, adjoint_hbm, table,
    moved, gap, adjoint, frac, mask, vel, x_first, x_second,
    f, porosity, porous, walls, x_up, x_down, f_sems, sems,
):
    def planes(n):
        part = pl.ds(n * PLANES, PLANES)
        return pltpu.make_async_copy(f_hbm.at[:, part], f.at[:, part], f_sems.at[n])

    small = [
        pltpu.make_async_copy(porosity_hbm, porosity, sems.at[0]),
        pltpu.make_async_copy(porous_hbm, porous, sems.at[1]),
        pltpu.make_async_copy(walls_hbm, walls, sems.at[2]),
    ]
    later = pltpu.make_async_copy(adjoint_hbm, adjoint, sems.at[3])
    for copy in small:
        copy.start()
    for n in range(CX // PLANES):
        planes(n).start()
    later.start()
    for copy in small:
        copy.wait()

    def plane(x):
        for yt in range(CY // TILE):
            at = (x, rows(yt))
            pops = [f[i, x, rows(yt), :] for i in range(Q)]
            fraction, open_panel = solidity(porosity[at], porous[at], walls[at])
            frac[at] = fraction
            mask[at] = open_panel
            u, e, _ = off_equilibrium(pops)
            for axis in range(3):
                vel[axis, x, rows(yt), :] = u[axis]
            c = correction(e)
            for i in range(Q):
                relaxed = pops[i] - c[i]
                change = pops[opposite[i]] - relaxed
                put_moved(gap, i, x, yt, open_panel * change, 1)
                put_moved(moved, i, x, yt, relaxed + fraction * change, 1)

    @pl.loop(0, CX // PLANES)
    def _(n):
        planes(n).wait()
        for k in range(PLANES):
            plane(n * PLANES + k)

    x_faces((moved, gap), 1, x_up, x_down)
    x_up[pl.ds(META, 1), :] = table[pl.ds(8, 1), :]
    x_down[pl.ds(META, 1), :] = table[pl.ds(1, 1), :]
    pair_up(x_up, x_down, x_first, x_second)
    later.wait()


def late_blocks(xb, halves, fields, adjoint, frac, mask, late, sums):
    for yt in range(CY // TILE):
        parts = {}
        for half in halves:
            x = xb * 2 + half
            at = (x, rows(yt))
            read = [fields[0][i, x, rows(yt), :] for i in range(Q)]
            u, e, df = off_equilibrium(read)
            b = [adjoint[i, x, rows(yt), :] for i in range(Q)]
            t, db = covector(b)
            total = sum(t[k] * e[k] for k in t) - sum(p * q for p, q in zip(db, df))
            total = mask[at] * total
            out = pull_back(b, t, u, frac[at])
            key = (0, 0)
            parts[key] = parts[key] + total if key in parts else total
            for i in range(Q):
                cx, cy, _ = velocities[i]
                key = ((half - cx) // 2, cy)
                early = out[i] * fields[1][i, x, rows(yt), :]
                parts[key] = parts[key] + early if key in parts else early
                put_moved(late, i, x, yt, out[i], -1)
        for (step, cy), part in parts.items():
            at = (xb + 1 + step, pl.ds(PAD_Y + yt * TILE - cy, TILE))
            sums[at] = sums[at] + part


def late_kernel(
    moved_in, gap_in, y_first, y_second, adjoint, frac, mask, moved, gap, late, sums
):
    del moved_in, gap_in
    fields = (moved, gap)
    fill_y(fields, 1, y_first, y_second)
    sums[...] = jnp.zeros((EXT_XB, EXT_Y, NZ), jnp.float32)

    def step(xb, halves=(0, 1)):
        late_blocks(xb, halves, fields, adjoint, frac, mask, late, sums)

    step(0, (1,))
    step(CX // 2 - 1, (0,))
    unrolled(1, CX // 2 - 1, 2, step)


def late_rest_kernel(
    late_in, sums_in, moved_in, gap_in, table, xf_in, xs_in, yf_in, ys_in,
    c_first, c_second, adjoint, frac, mask,
    late, sums, moved, gap, xf, xs, yu, yd, send_hbm,
    xu, xd, ext, ring, owner_of, scaled, send, sem,
):
    del late_in, sums_in, moved_in, gap_in
    fields = (moved, gap)
    messages = (c_first, c_second)
    fill_x(fields, 1, xf_in, xs_in)
    for sx, x in ((1, 0), (-1, CX - 1)):
        for sy, y in ((1, 0), (-1, CY - 1)):
            i = velocities.index((sx, sy, 0))
            for n, field in enumerate(fields):
                field[i, x, pl.ds(y, 1), :] = corner_arrived(sx, sy, n, messages)
    for xb, half in ((0, 0), (CX // 2 - 1, 1)):
        late_blocks(xb, (half,), fields, adjoint, frac, mask, late, sums)

    row, lane = iota((16, NZ), 0), iota((16, NZ), 1)
    numbers = pl.ds(META, 1)
    held = table[...]
    for sign, place in ((1, 0), (-1, 9)):
        here = x_arrived(sign, numbers, xf_in, xs_in)
        held = jnp.where(row == place, here, held)
    for sign, place in ((1, 0), (-1, 9)):
        here = column(y_arrived(sign, numbers, yf_in, ys_in), row == lane)
        held = jnp.where((lane == place) & (row > 0) & (row < 9), here, held)
    for sx, x in ((1, 0), (-1, 9)):
        for sy, y in ((1, 0), (-1, 9)):
            there = iota((1, NZ), 1) == (8 if sx == 1 else 1)
            here = column(corner_arrived(sx, sy, 2, messages), there)
            held = jnp.where((row == x) & (lane == y), here, held)
    ext[...] = held

    def put_lines(start, number, spot, total):
        number = number.astype(jnp.int32)
        lane = iota((total.shape[0], NZ), 1)
        spot = spot + (number & 3) if isinstance(spot, int) else spot(number & 3)
        line = pl.ds(start, total.shape[0])
        owner_of[line, :] = jnp.where(lane == jnp.right_shift(number, 10), 1.0, 0.0)
        patch = (jnp.right_shift(number, 2) & 255).astype(jnp.float32)
        value = jnp.where(lane == spot, jnp.sum(total, axis=1, keepdims=True), 0.0)
        scaled[line, :] = jnp.where(lane == spot + SLOT_LANE, patch, value)

    pick = iota((8, NZ), 1) == iota((8, NZ), 0) + 1
    for xb in range(EXT_XB):
        total = sums[xb, pl.ds(PAD_Y, 8, stride=2), :] + sums[xb, pl.ds(PAD_Y + 1, 8, stride=2), :]
        spot = 2 if xb == 0 else 4 if xb == 9 else 0
        put_lines(xb * 8, column(ext[pl.ds(xb, 1), :], pick), spot, total)
    ring[...] = jnp.zeros((32, NZ), jnp.float32)
    for xb in range(EXT_XB):
        ring[pl.ds(xb, 1), :] = sums[xb, pl.ds(PAD_Y - 1, 1), :]
        ring[pl.ds(16 + xb, 1), :] = sums[xb, pl.ds(PAD_Y + CY, 1), :]
    row = iota((16, 1), 0)
    for n, (face, corner, lane) in enumerate(((6, 10, 0), (8, 12, 9))):

        def spot(rank, face=face, corner=corner):
            side = jnp.where(row == 9, corner + 1, face + rank)
            return jnp.where(row == 0, corner, side)

        pick = (iota((16, NZ), 1) == lane) & (iota((16, NZ), 0) < EXT_XB)
        total = ring[pl.ds(16 * n, 16), :]
        put_lines(RING + 16 * n, column(ext[...], pick), spot, total)
    send[pl.ds(0, DEVICES, stride=2), :] = lax.dot_general(
        owner_of[...],
        scaled[...],
        (((0,), (0,)), ((), ())),
        precision=lax.Precision.HIGHEST,
        preferred_element_type=jnp.float32,
    )
    for there, i, x, y in corners(1):
        send[pl.ds(2 * there + 1, 1), :] = late[i, x, pl.ds(y, 1), :]
    copy = pltpu.make_async_copy(send, send_hbm, sem)
    copy.start()
    x_faces((late,), -1, xu, xd)
    y_faces(late, yu, yd)
    pair_up(xu, xd, xf, xs)
    copy.wait()


def corners(direction):
    gx, gy = lax.axis_index("gx"), lax.axis_index("gy")
    for ex in (1, -1):
        for ey in (1, -1):
            there_x = (gx + direction * ex) & (N_GX - 1)
            there_y = (gy + direction * ey) & (N_GY - 1)
            i = velocities.index((-ex, -ey, 0))
            x, y = 0 if ex == 1 else CX - 1, 0 if ey == 1 else CY - 1
            yield there_x * N_GY + there_y, i, x, y


def early_plane(x, late, frac, vel, put):
    for yt in range(CY // TILE):
        b = [late[i, x, rows(yt), :] for i in range(Q)]
        t, _ = covector(b)
        u = [vel[axis, x, rows(yt), :] for axis in range(3)]
        result = pull_back(b, t, u, frac[x, rows(yt)])
        for i in range(Q):
            put(i, yt, result[i])


def early_kernel(late_in, y_first, y_second, frac, vel, late, out, hold, sems):
    del late_in
    fill_y((late,), -1, y_first, y_second)

    def planes(n):
        part = pl.ds(1 + n * 2, 2)
        return pltpu.make_async_copy(hold.at[:, part], out.at[:, part], sems.at[n])

    @pl.loop(0, CX // 2 - 1)
    def _(n):
        for k in range(2):
            x = 1 + n * 2 + k

            def put(i, yt, value, x=x):
                hold[i, x, rows(yt), :] = value

            early_plane(x, late, frac, vel, put)
        planes(n).start()

    for n in range(CX // 2 - 1):
        planes(n).wait()


def last_kernel(
    out_in, late_in, first, second, got, frac, vel, late, out, patch_out, hold, patch, sems
):
    del out_in, late_in
    fill_x((late,), -1, first, second)
    for here, i, x, y in corners(-1):
        late[i, x, pl.ds(y, 1), :] = got[pl.ds(2 * here + 1, 1), :]
    copies = []
    for n, x in enumerate((0, CX - 1)):

        def put(i, yt, value, n=n):
            hold[n, i, rows(yt), :] = value

        early_plane(x, late, frac, vel, put)
        copies.append(pltpu.make_async_copy(hold.at[n], out.at[:, x], sems.at[n]))
        copies[n].start()
    data = got[pl.ds(0, DEVICES, stride=2), :].T
    part = 64
    for start in range(0, PATCH_DEV, part):
        number = (iota((part, DEVICES), 0) + start).astype(jnp.float32)
        total = jnp.zeros((part, DEVICES), jnp.float32)
        for k in range(PARTS):
            hit = data[SLOT_LANE + k : SLOT_LANE + k + 1] == number
            total = total + jnp.where(hit, data[k : k + 1], 0.0)
        patch[:, pl.ds(start, part)] = jnp.sum(total, axis=1)[None]
    copies.append(pltpu.make_async_copy(patch, patch_out, sems.at[2]))
    copies[2].start()
    for copy in copies:
        copy.wait()


VMEM = pl.BlockSpec(memory_space=pltpu.VMEM)
ANY = pl.BlockSpec(memory_space=pl.ANY)
LIMIT = 8 * 2**20


def vmem(*shape):
    return pltpu.VMEM(shape, jnp.float32)


def call(kernel, ins, outs, scratch=(), aliases=None, flops=0, hbm_ins=0, hbm_outs=()):
    held = [pltpu.with_memory_space_constraint(x, pltpu.HBM) for x in ins[:hbm_ins]]
    held += [pltpu.with_memory_space_constraint(x, pltpu.VMEM) for x in ins[hbm_ins:]]
    return pl.pallas_call(
        kernel,
        out_shape=[*outs, *hbm_outs],
        in_specs=[ANY] * hbm_ins + [VMEM] * (len(ins) - hbm_ins),
        out_specs=[VMEM] * len(outs) + [ANY] * len(hbm_outs),
        scratch_shapes=list(scratch),
        input_output_aliases=aliases or {},
        compiler_params=pltpu.CompilerParams(vmem_limit_bytes=LIMIT),
        cost_estimate=pl.CostEstimate(flops=flops, bytes_accessed=0, transcendentals=0),
    )(*held)


FIELD = vmem(Q, CX, CY, NZ)
NODE = vmem(CX, CY, NZ)
MESSAGE = vmem(MESSAGE_ROWS, NZ)
SHORT_MESSAGE = vmem(FACE, NZ)
LINES = vmem(LINE_COUNT, NZ)


def shift(block, axis, step):
    count = lax.axis_size(axis)
    return lax.ppermute(block, axis, [(i, (i + step) % count) for i in range(count)])


def swap(block, axis, step):
    count = lax.axis_size(axis)
    return lax.ppermute(
        block, axis, [(i, (i + (-step if i % 2 else step)) % count) for i in range(count)]
    )


def body(populations, porosity, adjoint_in, porous, walls, owners, slots):
    ints = pltpu.VMEM((CX, CY, NZ), jnp.int32)
    dma = pltpu.SemaphoreType.DMA
    table, yf, ys = call(
        edge_kernel,
        [populations, porosity, porous, walls, owners.reshape(1, 64), slots.reshape(1, 64)],
        [vmem(16, NZ), MESSAGE, MESSAGE],
        scratch=[vmem(2, Q, CX, NZ), vmem(2, CX, NZ)]
        + [pltpu.VMEM((2, CX, NZ), jnp.int32)] * 2
        + [pltpu.VMEM((1, 64), jnp.int32)] * 2
        + [dma((10,))],
        hbm_ins=6,
    )
    yf = shift(yf, "gy", 1)
    ys = shift(ys, "gy", -1)
    moved, gap, adjoint, frac, mask, vel, xf, xs = call(
        forward_kernel,
        [populations, porosity, porous, walls, adjoint_in, table],
        [FIELD] * 3 + [NODE] * 2 + [vmem(3, CX, CY, NZ), MESSAGE, MESSAGE],
        scratch=[FIELD, NODE, ints, ints, MESSAGE, MESSAGE, dma((CX // PLANES,)), dma((4,))],
        hbm_ins=5,
        flops=20_000_000,
    )
    xf = swap(xf, "gx", -1)
    xs = swap(xs, "gx", 1)
    corner = call(
        turn_kernel, [yf, ys, frac], [vmem(TILE, NZ)] * 2, scratch=[vmem(TILE, NZ)] * 2
    )
    corner = [swap(corner[0], "gx", -1), swap(corner[1], "gx", 1)]
    sums_shape = vmem(EXT_XB, EXT_Y, NZ)
    moved, gap, late, sums = call(
        late_kernel,
        [moved, gap, yf, ys, adjoint, frac, mask],
        [FIELD, FIELD, FIELD, sums_shape],
        aliases={0: 0, 1: 1},
        flops=20_000_000,
    )
    late, _, _, _, xf, xs, yf, ys, send = call(
        late_rest_kernel,
        [late, sums, moved, gap, table, xf, xs, yf, ys, *corner, adjoint, frac, mask],
        [FIELD, sums_shape, FIELD, FIELD] + [SHORT_MESSAGE] * 4,
        hbm_outs=[jax.ShapeDtypeStruct((2 * DEVICES, NZ), jnp.float32)],
        scratch=[SHORT_MESSAGE] * 2
        + [vmem(16, NZ), vmem(32, NZ), LINES, LINES, vmem(2 * DEVICES, NZ), dma],
        aliases={0: 0, 1: 1, 2: 2, 3: 3},
    )
    got = lax.all_to_all(send, ("gx", "gy"), split_axis=0, concat_axis=0, tiled=True)
    yf = shift(yf, "gy", 1)
    xf = swap(xf, "gx", -1)
    xs = swap(xs, "gx", 1)
    ys = shift(ys, "gy", -1)
    adjoint_shape = jax.ShapeDtypeStruct((Q, CX, CY, NZ), jnp.float32)
    late, adjoint_out = call(
        early_kernel,
        [late, yf, ys, frac, vel],
        [FIELD],
        hbm_outs=[adjoint_shape],
        scratch=[FIELD, dma((CX // 2 - 1,))],
        aliases={0: 0},
        flops=20_000_000,
    )
    _, adjoint_out, patch = call(
        last_kernel,
        [adjoint_out, late, xf, xs, got, frac, vel],
        [FIELD],
        hbm_ins=1,
        hbm_outs=[adjoint_shape, jax.ShapeDtypeStruct((1, PATCH_DEV), jnp.float32)],
        scratch=[vmem(2, Q, CY, NZ), vmem(1, PATCH_DEV), dma((3,))],
        aliases={0: 1, 1: 0},
    )
    return adjoint_out, patch.reshape(PATCH_DEV)


def solution(mesh):
    return jax.shard_map(
        body,
        mesh=mesh,
        in_specs=(
            P(None, "gx", "gy", None),
            P("gx", "gy", None),
            P(None, "gx", "gy", None),
            P("gx", "gy", None),
            P("gx", "gy", None),
            P("gx", "gy", None, None),
            P("gx", "gy", None),
        ),
        out_specs=(P(None, "gx", "gy", None), P(("gx", "gy"))),
        check_vma=False,
    )
```

```python
import jax
import jax.numpy as jnp
from jax import lax
from jax.experimental import pallas as pl
from jax.experimental.pallas import tpu as pltpu
from jax.sharding import PartitionSpec as P

Q = 19
CX = 16
CY = 16
NZ = 128
TILE = 8
PAD_Y = 8
EXT_Y = 32
EXT_XB = 10
RING = 80
LINE_COUNT = 112
DEVICES = 128
N_GX, N_GY = 8, 16
PATCH_DEV = 256
SLOT_LANE = 64
PARTS = 14
FACE = 80
META = 160
MESSAGE_ROWS = 168
PLANES = 4

velocities = [
    (0, 0, 0),
    (1, 0, 0),
    (-1, 0, 0),
    (0, 1, 0),
    (0, -1, 0),
    (0, 0, 1),
    (0, 0, -1),
    (1, 1, 0),
    (-1, -1, 0),
    (1, -1, 0),
    (-1, 1, 0),
    (1, 0, 1),
    (-1, 0, -1),
    (1, 0, -1),
    (-1, 0, 1),
    (0, 1, 1),
    (0, -1, -1),
    (0, 1, -1),
    (0, -1, 1),
]
opposite = [0, 2, 1, 4, 3, 6, 5, 8, 7, 10, 9, 12, 11, 14, 13, 16, 15, 18, 17]
RATE2, RATE3, RATE4 = 1.25, 1.5, 1.4


def moving(axis, sign, direction):
    return [i for i in range(Q) if direction * velocities[i][axis] == sign]


def edge(f, first):
    s, d = f[first] + f[first + 1], f[first] - f[first + 1]
    s2, d2 = f[first + 2] + f[first + 3], f[first + 2] - f[first + 3]
    return s, d, s2, d2


def off_equilibrium(f):
    sx, dx = f[1] + f[2], f[1] - f[2]
    sy, dy = f[3] + f[4], f[3] - f[4]
    sz, dz = f[5] + f[6], f[5] - f[6]
    s7, d7, s9, d9 = edge(f, 7)
    s11, d11, s13, d13 = edge(f, 11)
    s15, d15, s17, d17 = edge(f, 15)
    m220, m110, m120, m210 = s7 + s9, s7 - s9, d7 + d9, d7 - d9
    m202, m101, m102, m201 = s11 + s13, s11 - s13, d11 + d13, d11 - d13
    m022, m011, m012, m021 = s15 + s17, s15 - s17, d15 + d17, d15 - d17
    m200, m020, m002 = sx + m220 + m202, sy + m220 + m022, sz + m202 + m022
    jx, jy, jz = dx + (m120 + m102), dy + (m210 + m012), dz + (m201 + m021)
    rho = f[0] + (sx + sy + sz) + (m220 + m202 + m022)
    inv = 1.0 / rho
    ux, uy, uz = jx * inv, jy * inv, jz * inv
    qx, qy, qz = jx * ux, jy * uy, jz * uz
    third = rho * (1.0 / 3.0)
    ninth = rho * (1.0 / 9.0) - (qx + qy + qz) * (1.0 / 6.0)
    tx, ty, tz = jx * (1.0 / 3.0), jy * (1.0 / 3.0), jz * (1.0 / 3.0)
    e = {
        "200": RATE2 * (m200 - third - qx),
        "020": RATE2 * (m020 - third - qy),
        "002": RATE2 * (m002 - third - qz),
        "110": RATE2 * (m110 - jx * uy),
        "101": RATE2 * (m101 - jx * uz),
        "011": RATE2 * (m011 - jy * uz),
        "120": RATE3 * (m120 - tx),
        "102": RATE3 * (m102 - tx),
        "210": RATE3 * (m210 - ty),
        "012": RATE3 * (m012 - ty),
        "201": RATE3 * (m201 - tz),
        "021": RATE3 * (m021 - tz),
        "220": RATE4 * (m220 - ninth - 0.5 * (qx + qy)),
        "202": RATE4 * (m202 - ninth - 0.5 * (qx + qz)),
        "022": RATE4 * (m022 - ninth - 0.5 * (qy + qz)),
    }
    return (ux, uy, uz), e, (dx, dy, dz, d7, d9, d11, d13, d15, d17)


def spread(t, g, a, b):
    even, odd = t + g, t - g
    plus, minus = a + b, a - b
    return [even + plus, even - plus, odd + minus, odd - minus]


def correction(e):
    q = {k: 0.25 * v for k, v in e.items()}
    xy = spread(q["220"], q["110"], q["120"], q["210"])
    xz = spread(q["202"], q["101"], q["102"], q["201"])
    yz = spread(q["022"], q["011"], q["012"], q["021"])
    faces = []
    for second, fourth, odd in (
        ("200", ("220", "202"), ("120", "102")),
        ("020", ("220", "022"), ("210", "012")),
        ("002", ("202", "022"), ("201", "021")),
    ):
        mean = 0.5 * e[second] - 2.0 * (q[fourth[0]] + q[fourth[1]])
        lean = 2.0 * (q[odd[0]] + q[odd[1]])
        faces += [mean - lean, mean + lean]
    rest = (e["220"] + e["202"] + e["022"]) - (e["200"] + e["020"] + e["002"])
    return [rest] + faces + xy + xz + yz


def covector(b):
    hx, dx = 0.5 * (b[1] + b[2]), b[1] - b[2]
    hy, dy = 0.5 * (b[3] + b[4]), b[3] - b[4]
    hz, dz = 0.5 * (b[5] + b[6]), b[5] - b[6]
    s7, d7, s9, d9 = edge(b, 7)
    s11, d11, s13, d13 = edge(b, 11)
    s15, d15, s17, d17 = edge(b, 15)
    gx, gy, gz = hx - b[0], hy - b[0], hz - b[0]
    kx, ky, kz = 0.5 * dx, 0.5 * dy, 0.5 * dz
    t = {
        "200": gx,
        "020": gy,
        "002": gz,
        "110": 0.25 * (s7 - s9),
        "101": 0.25 * (s11 - s13),
        "011": 0.25 * (s15 - s17),
        "120": 0.25 * (d7 + d9) - kx,
        "102": 0.25 * (d11 + d13) - kx,
        "210": 0.25 * (d7 - d9) - ky,
        "012": 0.25 * (d15 + d17) - ky,
        "201": 0.25 * (d11 - d13) - kz,
        "021": 0.25 * (d15 - d17) - kz,
        "220": 0.25 * (s7 + s9) - gx - hy,
        "202": 0.25 * (s11 + s13) - gx - hz,
        "022": 0.25 * (s15 + s17) - gy - hz,
    }
    return t, (dx, dy, dz, d7, d9, d11, d13, d15, d17)


def pull_back(b, t, u, fraction):
    rates = {k: (RATE2, RATE3, RATE4)[sum(map(int, k)) - 2] for k in t}
    n = {k: rates[k] * v for k, v in t.items()}
    ux, uy, uz = u
    fourth = n["220"] + n["202"] + n["022"]
    second = n["200"] + n["020"] + n["002"]
    part = fourth * (1.0 / 3.0)
    ax = n["200"] + part - 0.5 * n["022"]
    ay = n["020"] + part - 0.5 * n["202"]
    az = n["002"] + part - 0.5 * n["220"]
    rx = 2.0 * ax * ux + n["110"] * uy + n["101"] * uz
    ry = 2.0 * ay * uy + n["110"] * ux + n["011"] * uz
    rz = 2.0 * az * uz + n["101"] * ux + n["011"] * uy
    p0 = second * (1.0 / 3.0) + fourth * (1.0 / 9.0) - 0.5 * (rx * ux + ry * uy + rz * uz)
    px = rx + (n["120"] + n["102"]) * (1.0 / 3.0)
    py = ry + (n["210"] + n["012"]) * (1.0 / 3.0)
    pz = rz + (n["201"] + n["021"]) * (1.0 / 3.0)
    ex, ey, ez = p0 - n["200"], p0 - n["020"], p0 - n["002"]
    h = [p0, ex + px, ex - px, ey + py, ey - py, ez + pz, ez - pz]
    h += spread(ex - n["020"] - n["220"], -n["110"], px - n["120"], py - n["210"])
    h += spread(ex - n["002"] - n["202"], -n["101"], px - n["102"], pz - n["201"])
    h += spread(ey - n["002"] - n["022"], -n["011"], py - n["012"], pz - n["021"])
    open_part = 1.0 - fraction
    return [open_part * (b[i] + h[i]) + fraction * b[opposite[i]] for i in range(Q)]


def store_wrapped(put, first, step, value):
    row = first + step
    if row < 0:
        put(0, value[1:])
        put(CY - 1, value[:1])
    elif row + TILE > CY:
        put(row, value[:-1])
        put(0, value[-1:])
    else:
        put(row, value)


def put_moved(field, i, x, yt, value, direction):
    cx, cy, cz = (direction * c for c in velocities[i])
    if cz:
        value = pltpu.roll(value, cz % NZ, axis=1)
    x = (x + cx) & (CX - 1) if cx else x

    def put(row, part):
        field[i, x, pl.ds(row, part.shape[0]), :] = part

    store_wrapped(put, yt * TILE, cy, value)


def by_parity(axis, even, odd):
    is_odd = jnp.full(even.shape, lax.axis_index(axis) & 1, jnp.int32) == 1
    return jnp.where(is_odd, odd, even)


def pair_up(up, down, first, second):
    first[...] = by_parity("gx", down[...], up[...])
    second[...] = by_parity("gx", up[...], down[...])


def x_arrived(sign, line, first, second):
    a, b = first[line, :], second[line, :]
    return by_parity("gx", a, b) if sign == 1 else by_parity("gx", b, a)


def y_arrived(sign, line, low, high):
    return low[line, :] if sign == 1 else high[line, :]


def x_faces(fields, direction, x_up, x_down):
    for n, field in enumerate(fields):
        for sign, x, message in ((1, 0, x_up), (-1, CX - 1, x_down)):
            for k, i in enumerate(moving(0, sign, direction)):
                message[pl.ds(n * FACE + k * CY, CY), :] = field[i, x]


def y_faces(field, y_up, y_down):
    for sign, row, message in ((1, 0, y_up), (-1, CY - 1, y_down)):
        for k, i in enumerate(moving(1, sign, -1)):
            for x in range(CX):
                message[pl.ds(k * CX + x, 1), :] = field[i, x, pl.ds(row, 1), :]


def fill_x(fields, direction, first, second):
    for n, field in enumerate(fields):
        for sign, x in ((1, 0), (-1, CX - 1)):
            for k, i in enumerate(moving(0, sign, direction)):
                line = pl.ds(n * FACE + k * CY, CY)
                field[i, x] = x_arrived(sign, line, first, second)


def fill_y(fields, direction, first, second):
    for n, field in enumerate(fields):
        for sign, row in ((1, 0), (-1, CY - 1)):
            for k, i in enumerate(moving(1, sign, direction)):
                line = pl.ds(n * FACE + k * CX, CX)
                face = y_arrived(sign, line, first, second)
                for x in range(CX):
                    field[i, x, pl.ds(row, 1), :] = face[x : x + 1]


def rows(yt):
    return pl.ds(yt * TILE, TILE)


def unrolled(start, stop, count, step):
    @pl.loop(0, (stop - start) // count)
    def _(n):
        for k in range(count):
            step(start + n * count + k)


def iota(shape, dim):
    return lax.broadcasted_iota(jnp.int32, shape, dim)


def column(row, pick):
    return jnp.sum(jnp.where(pick, row, 0.0), axis=1, keepdims=True)


def block_numbers(owners, slots, table, y_up, y_down):
    shape = (64, 64)
    row, lane = iota(shape, 0), iota(shape, 1)
    same = row == lane
    owner_row, slot_row = owners[...].astype(jnp.float32), slots[...].astype(jnp.float32)
    owner_col = column(owner_row, same)
    earlier = (owner_row == owner_col) & (lane < row)
    rank = jnp.sum(jnp.where(earlier, 1.0, 0.0), axis=1, keepdims=True)
    number = owner_col * 1024.0 + column(slot_row, same) * 4.0 + rank
    wide = (64, NZ)
    spot = iota(wide, 1) == (iota(wide, 0) & 7) + 1
    spread_out = jnp.where(spot, number, 0.0)
    table[...] = jnp.zeros((16, NZ), jnp.float32)
    for xb in range(8):
        line = jnp.sum(spread_out[xb * 8 : xb * 8 + 8], axis=0, keepdims=True)
        table[pl.ds(xb + 1, 1), :] = line
    held = table[...]
    eye = iota((16, NZ), 0) == iota((16, NZ), 1)
    for yb, message in ((8, y_up), (1, y_down)):
        part = jnp.where(eye, held[:, yb : yb + 1], 0.0)
        message[pl.ds(META, 1), :] = jnp.sum(part, axis=0, keepdims=True)


def solidity(porosity, porous, walls):
    wall = walls == 1
    panel = porous.astype(jnp.float32)
    return jnp.where(wall, 1.0, panel * porosity), jnp.where(wall, 0.0, panel)


def edge_kernel(
    f_hbm, porosity_hbm, porous_hbm, walls_hbm, owners_hbm, slots_hbm,
    table, y_up, y_down, f, porosity, porous, walls, owners, slots, sems,
):
    numbers = [
        pltpu.make_async_copy(owners_hbm, owners, sems.at[0]),
        pltpu.make_async_copy(slots_hbm, slots, sems.at[1]),
    ]
    faces = [(1, CY - 1, y_up), (-1, 0, y_down)]
    lines = []
    for n, (_, y, _) in enumerate(faces):
        copies = [pltpu.make_async_copy(f_hbm.at[:, :, y, :], f.at[n], sems.at[4 * n + 2])]
        for k, (source, target) in enumerate(
            ((porosity_hbm, porosity), (porous_hbm, porous), (walls_hbm, walls))
        ):
            node = source.at[:, y, :]
            copies.append(pltpu.make_async_copy(node, target.at[n], sems.at[4 * n + 3 + k]))
        lines.append(copies)
    for copy in sum(lines, numbers):
        copy.start()
    for copy in numbers:
        copy.wait()
    block_numbers(owners, slots, table, y_up, y_down)
    for n, (sign, _, message) in enumerate(faces):
        for copy in lines[n]:
            copy.wait()
        for tile in range(CX // TILE):
            at = (n, rows(tile))
            pops = [f[n, i, rows(tile), :] for i in range(Q)]
            fraction, open_panel = solidity(porosity[at], porous[at], walls[at])
            c = correction(off_equilibrium(pops)[1])
            for k, i in enumerate(moving(1, sign, 1)):
                relaxed = pops[i] - c[i]
                change = pops[opposite[i]] - relaxed
                pair = (relaxed + fraction * change, open_panel * change)
                for field, value in enumerate(pair):
                    if velocities[i][2]:
                        value = pltpu.roll(value, velocities[i][2] % NZ, axis=1)

                    def put(row, part, base=field * FACE + k * CX, message=message):
                        message[pl.ds(base + row, part.shape[0]), :] = part

                    store_wrapped(put, tile * TILE, velocities[i][0], value)


def turn_kernel(y_first, y_second, frac, first, second, up, down):
    del frac
    for sx, message in ((1, up), (-1, down)):
        for n, sy in enumerate((1, -1)):
            k = moving(1, sy, 1).index(velocities.index((sx, sy, 0)))
            row = k * CX + (0 if sx == 1 else CX - 1)
            for field in range(2):
                line = pl.ds(field * FACE + row, 1)
                value = y_arrived(sy, line, y_first, y_second)
                message[pl.ds(2 * n + field, 1), :] = value
            numbers = y_arrived(sy, pl.ds(META, 1), y_first, y_second)
            message[pl.ds(4 + n, 1), :] = numbers
    pair_up(up, down, first, second)


def corner_arrived(sx, sy, row, messages):
    n = 0 if sy == 1 else 1
    line = pl.ds(4 + n if row == 2 else 2 * n + row, 1)
    return x_arrived(sx, line, *messages)


def forward_kernel(
    f_hbm, porosity_hbm, porous_hbm, walls_hbm, adjoint_hbm, table,
    moved, gap, adjoint, frac, mask, vel, x_first, x_second,
    f, porosity, porous, walls, x_up, x_down, f_sems, sems,
):
    def planes(n):
        part = pl.ds(n * PLANES, PLANES)
        return pltpu.make_async_copy(f_hbm.at[:, part], f.at[:, part], f_sems.at[n])

    small = [
        pltpu.make_async_copy(porosity_hbm, porosity, sems.at[0]),
        pltpu.make_async_copy(porous_hbm, porous, sems.at[1]),
        pltpu.make_async_copy(walls_hbm, walls, sems.at[2]),
    ]
    later = pltpu.make_async_copy(adjoint_hbm, adjoint, sems.at[3])
    for copy in small:
        copy.start()
    for n in range(CX // PLANES):
        planes(n).start()
    later.start()
    for copy in small:
        copy.wait()

    def plane(x):
        for yt in range(CY // TILE):
            at = (x, rows(yt))
            pops = [f[i, x, rows(yt), :] for i in range(Q)]
            fraction, open_panel = solidity(porosity[at], porous[at], walls[at])
            frac[at] = fraction
            mask[at] = open_panel
            u, e, _ = off_equilibrium(pops)
            for axis in range(3):
                vel[axis, x, rows(yt), :] = u[axis]
            c = correction(e)
            for i in range(Q):
                relaxed = pops[i] - c[i]
                change = pops[opposite[i]] - relaxed
                put_moved(gap, i, x, yt, open_panel * change, 1)
                put_moved(moved, i, x, yt, relaxed + fraction * change, 1)

    @pl.loop(0, CX // PLANES)
    def _(n):
        planes(n).wait()
        for k in range(PLANES):
            plane(n * PLANES + k)

    x_faces((moved, gap), 1, x_up, x_down)
    x_up[pl.ds(META, 1), :] = table[pl.ds(8, 1), :]
    x_down[pl.ds(META, 1), :] = table[pl.ds(1, 1), :]
    pair_up(x_up, x_down, x_first, x_second)
    later.wait()


def late_blocks(xb, halves, fields, adjoint, frac, mask, late, sums):
    for yt in range(CY // TILE):
        parts = {}
        for half in halves:
            x = xb * 2 + half
            at = (x, rows(yt))
            read = [fields[0][i, x, rows(yt), :] for i in range(Q)]
            u, e, df = off_equilibrium(read)
            b = [adjoint[i, x, rows(yt), :] for i in range(Q)]
            t, db = covector(b)
            total = sum(t[k] * e[k] for k in t) - sum(p * q for p, q in zip(db, df))
            total = mask[at] * total
            out = pull_back(b, t, u, frac[at])
            key = (0, 0)
            parts[key] = parts[key] + total if key in parts else total
            for i in range(Q):
                cx, cy, _ = velocities[i]
                key = ((half - cx) // 2, cy)
                early = out[i] * fields[1][i, x, rows(yt), :]
                parts[key] = parts[key] + early if key in parts else early
                put_moved(late, i, x, yt, out[i], -1)
        for (step, cy), part in parts.items():
            at = (xb + 1 + step, pl.ds(PAD_Y + yt * TILE - cy, TILE))
            sums[at] = sums[at] + part


def late_kernel(
    moved_in, gap_in, y_first, y_second, adjoint, frac, mask, moved, gap, late, sums
):
    del moved_in, gap_in
    fields = (moved, gap)
    fill_y(fields, 1, y_first, y_second)
    sums[...] = jnp.zeros((EXT_XB, EXT_Y, NZ), jnp.float32)

    def step(xb, halves=(0, 1)):
        late_blocks(xb, halves, fields, adjoint, frac, mask, late, sums)

    step(0, (1,))
    step(CX // 2 - 1, (0,))
    unrolled(1, CX // 2 - 1, 2, step)


def late_rest_kernel(
    late_in, sums_in, moved_in, gap_in, table, xf_in, xs_in, yf_in, ys_in,
    c_first, c_second, adjoint, frac, mask,
    late, sums, moved, gap, xf, xs, yu, yd, send_hbm,
    xu, xd, ext, ring, owner_of, scaled, send, sem,
):
    del late_in, sums_in, moved_in, gap_in
    fields = (moved, gap)
    messages = (c_first, c_second)
    fill_x(fields, 1, xf_in, xs_in)
    for sx, x in ((1, 0), (-1, CX - 1)):
        for sy, y in ((1, 0), (-1, CY - 1)):
            i = velocities.index((sx, sy, 0))
            for n, field in enumerate(fields):
                field[i, x, pl.ds(y, 1), :] = corner_arrived(sx, sy, n, messages)
    for xb, half in ((0, 0), (CX // 2 - 1, 1)):
        late_blocks(xb, (half,), fields, adjoint, frac, mask, late, sums)

    row, lane = iota((16, NZ), 0), iota((16, NZ), 1)
    numbers = pl.ds(META, 1)
    held = table[...]
    for sign, place in ((1, 0), (-1, 9)):
        here = x_arrived(sign, numbers, xf_in, xs_in)
        held = jnp.where(row == place, here, held)
    for sign, place in ((1, 0), (-1, 9)):
        here = column(y_arrived(sign, numbers, yf_in, ys_in), row == lane)
        held = jnp.where((lane == place) & (row > 0) & (row < 9), here, held)
    for sx, x in ((1, 0), (-1, 9)):
        for sy, y in ((1, 0), (-1, 9)):
            there = iota((1, NZ), 1) == (8 if sx == 1 else 1)
            here = column(corner_arrived(sx, sy, 2, messages), there)
            held = jnp.where((row == x) & (lane == y), here, held)
    ext[...] = held

    def put_lines(start, number, spot, total):
        number = number.astype(jnp.int32)
        lane = iota((total.shape[0], NZ), 1)
        spot = spot + (number & 3) if isinstance(spot, int) else spot(number & 3)
        line = pl.ds(start, total.shape[0])
        owner_of[line, :] = jnp.where(lane == jnp.right_shift(number, 10), 1.0, 0.0)
        patch = (jnp.right_shift(number, 2) & 255).astype(jnp.float32)
        value = jnp.where(lane == spot, jnp.sum(total, axis=1, keepdims=True), 0.0)
        scaled[line, :] = jnp.where(lane == spot + SLOT_LANE, patch, value)

    pick = iota((8, NZ), 1) == iota((8, NZ), 0) + 1
    for xb in range(EXT_XB):
        total = sums[xb, pl.ds(PAD_Y, 8, stride=2), :] + sums[xb, pl.ds(PAD_Y + 1, 8, stride=2), :]
        spot = 2 if xb == 0 else 4 if xb == 9 else 0
        put_lines(xb * 8, column(ext[pl.ds(xb, 1), :], pick), spot, total)
    ring[...] = jnp.zeros((32, NZ), jnp.float32)
    for xb in range(EXT_XB):
        ring[pl.ds(xb, 1), :] = sums[xb, pl.ds(PAD_Y - 1, 1), :]
        ring[pl.ds(16 + xb, 1), :] = sums[xb, pl.ds(PAD_Y + CY, 1), :]
    row = iota((16, 1), 0)
    for n, (face, corner, lane) in enumerate(((6, 10, 0), (8, 12, 9))):

        def spot(rank, face=face, corner=corner):
            side = jnp.where(row == 9, corner + 1, face + rank)
            return jnp.where(row == 0, corner, side)

        pick = (iota((16, NZ), 1) == lane) & (iota((16, NZ), 0) < EXT_XB)
        total = ring[pl.ds(16 * n, 16), :]
        put_lines(RING + 16 * n, column(ext[...], pick), spot, total)
    send[pl.ds(0, DEVICES, stride=2), :] = lax.dot_general(
        owner_of[...],
        scaled[...],
        (((0,), (0,)), ((), ())),
        precision=lax.Precision.HIGHEST,
        preferred_element_type=jnp.float32,
    )
    for there, i, x, y in corners(1):
        send[pl.ds(2 * there + 1, 1), :] = late[i, x, pl.ds(y, 1), :]
    copy = pltpu.make_async_copy(send, send_hbm, sem)
    copy.start()
    x_faces((late,), -1, xu, xd)
    y_faces(late, yu, yd)
    pair_up(xu, xd, xf, xs)
    copy.wait()


def corners(direction):
    gx, gy = lax.axis_index("gx"), lax.axis_index("gy")
    for ex in (1, -1):
        for ey in (1, -1):
            there_x = (gx + direction * ex) & (N_GX - 1)
            there_y = (gy + direction * ey) & (N_GY - 1)
            i = velocities.index((-ex, -ey, 0))
            x, y = 0 if ex == 1 else CX - 1, 0 if ey == 1 else CY - 1
            yield there_x * N_GY + there_y, i, x, y


def early_plane(x, late, frac, vel, put):
    for yt in range(CY // TILE):
        b = [late[i, x, rows(yt), :] for i in range(Q)]
        t, _ = covector(b)
        u = [vel[axis, x, rows(yt), :] for axis in range(3)]
        result = pull_back(b, t, u, frac[x, rows(yt)])
        for i in range(Q):
            put(i, yt, result[i])


def early_kernel(late_in, y_first, y_second, frac, vel, late, out, hold, sems):
    del late_in
    fill_y((late,), -1, y_first, y_second)

    def planes(n):
        part = pl.ds(1 + n * 2, 2)
        return pltpu.make_async_copy(hold.at[:, part], out.at[:, part], sems.at[n])

    @pl.loop(0, CX // 2 - 1)
    def _(n):
        for k in range(2):
            x = 1 + n * 2 + k

            def put(i, yt, value, x=x):
                hold[i, x, rows(yt), :] = value

            early_plane(x, late, frac, vel, put)
        planes(n).start()

    for n in range(CX // 2 - 1):
        planes(n).wait()


def last_kernel(
    out_in, late_in, second, first, got, frac, vel, late, out, patch_out, hold, patch, sems
):
    del out_in, late_in
    fill_x((late,), -1, first, second)
    for here, i, x, y in corners(-1):
        late[i, x, pl.ds(y, 1), :] = got[pl.ds(2 * here + 1, 1), :]
    copies = []
    for n, x in enumerate((0, CX - 1)):

        def put(i, yt, value, n=n):
            hold[n, i, rows(yt), :] = value

        early_plane(x, late, frac, vel, put)
        copies.append(pltpu.make_async_copy(hold.at[n], out.at[:, x], sems.at[n]))
        copies[n].start()
    data = got[pl.ds(0, DEVICES, stride=2), :].T
    part = 64
    for start in range(0, PATCH_DEV, part):
        number = (iota((part, DEVICES), 0) + start).astype(jnp.float32)
        total = jnp.zeros((part, DEVICES), jnp.float32)
        for k in range(PARTS):
            hit = data[SLOT_LANE + k : SLOT_LANE + k + 1] == number
            total = total + jnp.where(hit, data[k : k + 1], 0.0)
        patch[:, pl.ds(start, part)] = jnp.sum(total, axis=1)[None]
    copies.append(pltpu.make_async_copy(patch, patch_out, sems.at[2]))
    copies[2].start()
    for copy in copies:
        copy.wait()


VMEM = pl.BlockSpec(memory_space=pltpu.VMEM)
ANY = pl.BlockSpec(memory_space=pl.ANY)
LIMIT = 8 * 2**20


def vmem(*shape):
    return pltpu.VMEM(shape, jnp.float32)


def call(kernel, ins, outs, scratch=(), aliases=None, flops=0, hbm_ins=0, hbm_outs=()):
    held = [pltpu.with_memory_space_constraint(x, pltpu.HBM) for x in ins[:hbm_ins]]
    held += [pltpu.with_memory_space_constraint(x, pltpu.VMEM) for x in ins[hbm_ins:]]
    return pl.pallas_call(
        kernel,
        out_shape=[*outs, *hbm_outs],
        in_specs=[ANY] * hbm_ins + [VMEM] * (len(ins) - hbm_ins),
        out_specs=[VMEM] * len(outs) + [ANY] * len(hbm_outs),
        scratch_shapes=list(scratch),
        input_output_aliases=aliases or {},
        compiler_params=pltpu.CompilerParams(vmem_limit_bytes=LIMIT),
        cost_estimate=pl.CostEstimate(flops=flops, bytes_accessed=0, transcendentals=0),
    )(*held)


FIELD = vmem(Q, CX, CY, NZ)
NODE = vmem(CX, CY, NZ)
MESSAGE = vmem(MESSAGE_ROWS, NZ)
SHORT_MESSAGE = vmem(FACE, NZ)
LINES = vmem(LINE_COUNT, NZ)


def shift(block, axis, step):
    count = lax.axis_size(axis)
    return lax.ppermute(block, axis, [(i, (i + step) % count) for i in range(count)])


def swap(block, axis, step):
    count = lax.axis_size(axis)
    return lax.ppermute(
        block, axis, [(i, (i + (-step if i % 2 else step)) % count) for i in range(count)]
    )


def body(populations, porosity, adjoint_in, porous, walls, owners, slots):
    ints = pltpu.VMEM((CX, CY, NZ), jnp.int32)
    dma = pltpu.SemaphoreType.DMA
    table, yf, ys = call(
        edge_kernel,
        [populations, porosity, porous, walls, owners.reshape(1, 64), slots.reshape(1, 64)],
        [vmem(16, NZ), MESSAGE, MESSAGE],
        scratch=[vmem(2, Q, CX, NZ), vmem(2, CX, NZ)]
        + [pltpu.VMEM((2, CX, NZ), jnp.int32)] * 2
        + [pltpu.VMEM((1, 64), jnp.int32)] * 2
        + [dma((10,))],
        hbm_ins=6,
    )
    yf = shift(yf, "gy", 1)
    ys = shift(ys, "gy", -1)
    moved, gap, adjoint, frac, mask, vel, xf, xs = call(
        forward_kernel,
        [populations, porosity, porous, walls, adjoint_in, table],
        [FIELD] * 3 + [NODE] * 2 + [vmem(3, CX, CY, NZ), MESSAGE, MESSAGE],
        scratch=[FIELD, NODE, ints, ints, MESSAGE, MESSAGE, dma((CX // PLANES,)), dma((4,))],
        hbm_ins=5,
        flops=20_000_000,
    )
    xf = swap(xf, "gx", -1)
    xs = swap(xs, "gx", 1)
    corner = call(
        turn_kernel, [yf, ys, frac], [vmem(TILE, NZ)] * 2, scratch=[vmem(TILE, NZ)] * 2
    )
    corner = [swap(corner[0], "gx", -1), swap(corner[1], "gx", 1)]
    sums_shape = vmem(EXT_XB, EXT_Y, NZ)
    moved, gap, late, sums = call(
        late_kernel,
        [moved, gap, yf, ys, adjoint, frac, mask],
        [FIELD, FIELD, FIELD, sums_shape],
        aliases={0: 0, 1: 1},
        flops=20_000_000,
    )
    late, _, _, _, xf, xs, yf, ys, send = call(
        late_rest_kernel,
        [late, sums, moved, gap, table, xf, xs, yf, ys, *corner, adjoint, frac, mask],
        [FIELD, sums_shape, FIELD, FIELD] + [SHORT_MESSAGE] * 4,
        hbm_outs=[jax.ShapeDtypeStruct((2 * DEVICES, NZ), jnp.float32)],
        scratch=[SHORT_MESSAGE] * 2
        + [vmem(16, NZ), vmem(32, NZ), LINES, LINES, vmem(2 * DEVICES, NZ), dma],
        aliases={0: 0, 1: 1, 2: 2, 3: 3},
    )
    got = lax.all_to_all(send, ("gx", "gy"), split_axis=0, concat_axis=0, tiled=True)
    yf = shift(yf, "gy", 1)
    ys = shift(ys, "gy", -1)
    xs = swap(xs, "gx", 1)
    xf = swap(xf, "gx", -1)
    adjoint_shape = jax.ShapeDtypeStruct((Q, CX, CY, NZ), jnp.float32)
    late, adjoint_out = call(
        early_kernel,
        [late, yf, ys, frac, vel],
        [FIELD],
        hbm_outs=[adjoint_shape],
        scratch=[FIELD, dma((CX // 2 - 1,))],
        aliases={0: 0},
        flops=20_000_000,
    )
    _, adjoint_out, patch = call(
        last_kernel,
        [adjoint_out, late, xs, xf, got, frac, vel],
        [FIELD],
        hbm_ins=1,
        hbm_outs=[adjoint_shape, jax.ShapeDtypeStruct((1, PATCH_DEV), jnp.float32)],
        scratch=[vmem(2, Q, CY, NZ), vmem(1, PATCH_DEV), dma((3,))],
        aliases={0: 1, 1: 0},
    )
    return adjoint_out, patch.reshape(PATCH_DEV)


def solution(mesh):
    return jax.shard_map(
        body,
        mesh=mesh,
        in_specs=(
            P(None, "gx", "gy", None),
            P("gx", "gy", None),
            P(None, "gx", "gy", None),
            P("gx", "gy", None),
            P("gx", "gy", None),
            P("gx", "gy", None, None),
            P("gx", "gy", None),
        ),
        out_specs=(P(None, "gx", "gy", None), P(("gx", "gy"))),
        check_vma=False,
    )
```

```python
import jax
import jax.numpy as jnp
from jax import lax
from jax.experimental import pallas as pl
from jax.experimental.pallas import tpu as pltpu
from jax.sharding import PartitionSpec as P

Q = 19
CX = 16
CY = 16
NZ = 128
TILE = 8
PAD_Y = 8
EXT_Y = 32
EXT_XB = 10
RING = 80
LINE_COUNT = 112
DEVICES = 128
N_GX, N_GY = 8, 16
PATCH_DEV = 256
SLOT_LANE = 64
PARTS = 14
FACE = 80
META = 160
MESSAGE_ROWS = 168
PLANES = 4

velocities = [
    (0, 0, 0),
    (1, 0, 0),
    (-1, 0, 0),
    (0, 1, 0),
    (0, -1, 0),
    (0, 0, 1),
    (0, 0, -1),
    (1, 1, 0),
    (-1, -1, 0),
    (1, -1, 0),
    (-1, 1, 0),
    (1, 0, 1),
    (-1, 0, -1),
    (1, 0, -1),
    (-1, 0, 1),
    (0, 1, 1),
    (0, -1, -1),
    (0, 1, -1),
    (0, -1, 1),
]
opposite = [0, 2, 1, 4, 3, 6, 5, 8, 7, 10, 9, 12, 11, 14, 13, 16, 15, 18, 17]
RATE2, RATE3, RATE4 = 1.25, 1.5, 1.4


def moving(axis, sign, direction):
    return [i for i in range(Q) if direction * velocities[i][axis] == sign]


def edge(f, first):
    s, d = f[first] + f[first + 1], f[first] - f[first + 1]
    s2, d2 = f[first + 2] + f[first + 3], f[first + 2] - f[first + 3]
    return s, d, s2, d2


def off_equilibrium(f):
    sx, dx = f[1] + f[2], f[1] - f[2]
    sy, dy = f[3] + f[4], f[3] - f[4]
    sz, dz = f[5] + f[6], f[5] - f[6]
    s7, d7, s9, d9 = edge(f, 7)
    s11, d11, s13, d13 = edge(f, 11)
    s15, d15, s17, d17 = edge(f, 15)
    m220, m110, m120, m210 = s7 + s9, s7 - s9, d7 + d9, d7 - d9
    m202, m101, m102, m201 = s11 + s13, s11 - s13, d11 + d13, d11 - d13
    m022, m011, m012, m021 = s15 + s17, s15 - s17, d15 + d17, d15 - d17
    m200, m020, m002 = sx + m220 + m202, sy + m220 + m022, sz + m202 + m022
    jx, jy, jz = dx + (m120 + m102), dy + (m210 + m012), dz + (m201 + m021)
    rho = f[0] + (sx + sy + sz) + (m220 + m202 + m022)
    inv = 1.0 / rho
    ux, uy, uz = jx * inv, jy * inv, jz * inv
    qx, qy, qz = jx * ux, jy * uy, jz * uz
    third = rho * (1.0 / 3.0)
    ninth = rho * (1.0 / 9.0) - (qx + qy + qz) * (1.0 / 6.0)
    tx, ty, tz = jx * (1.0 / 3.0), jy * (1.0 / 3.0), jz * (1.0 / 3.0)
    e = {
        "200": RATE2 * (m200 - third - qx),
        "020": RATE2 * (m020 - third - qy),
        "002": RATE2 * (m002 - third - qz),
        "110": RATE2 * (m110 - jx * uy),
        "101": RATE2 * (m101 - jx * uz),
        "011": RATE2 * (m011 - jy * uz),
        "120": RATE3 * (m120 - tx),
        "102": RATE3 * (m102 - tx),
        "210": RATE3 * (m210 - ty),
        "012": RATE3 * (m012 - ty),
        "201": RATE3 * (m201 - tz),
        "021": RATE3 * (m021 - tz),
        "220": RATE4 * (m220 - ninth - 0.5 * (qx + qy)),
        "202": RATE4 * (m202 - ninth - 0.5 * (qx + qz)),
        "022": RATE4 * (m022 - ninth - 0.5 * (qy + qz)),
    }
    return (ux, uy, uz), e, (dx, dy, dz, d7, d9, d11, d13, d15, d17)


def spread(t, g, a, b):
    even, odd = t + g, t - g
    plus, minus = a + b, a - b
    return [even + plus, even - plus, odd + minus, odd - minus]


def correction(e):
    q = {k: 0.25 * v for k, v in e.items()}
    xy = spread(q["220"], q["110"], q["120"], q["210"])
    xz = spread(q["202"], q["101"], q["102"], q["201"])
    yz = spread(q["022"], q["011"], q["012"], q["021"])
    faces = []
    for second, fourth, odd in (
        ("200", ("220", "202"), ("120", "102")),
        ("020", ("220", "022"), ("210", "012")),
        ("002", ("202", "022"), ("201", "021")),
    ):
        mean = 0.5 * e[second] - 2.0 * (q[fourth[0]] + q[fourth[1]])
        lean = 2.0 * (q[odd[0]] + q[odd[1]])
        faces += [mean - lean, mean + lean]
    rest = (e["220"] + e["202"] + e["022"]) - (e["200"] + e["020"] + e["002"])
    return [rest] + faces + xy + xz + yz


def covector(b):
    hx, dx = 0.5 * (b[1] + b[2]), b[1] - b[2]
    hy, dy = 0.5 * (b[3] + b[4]), b[3] - b[4]
    hz, dz = 0.5 * (b[5] + b[6]), b[5] - b[6]
    s7, d7, s9, d9 = edge(b, 7)
    s11, d11, s13, d13 = edge(b, 11)
    s15, d15, s17, d17 = edge(b, 15)
    gx, gy, gz = hx - b[0], hy - b[0], hz - b[0]
    kx, ky, kz = 0.5 * dx, 0.5 * dy, 0.5 * dz
    t = {
        "200": gx,
        "020": gy,
        "002": gz,
        "110": 0.25 * (s7 - s9),
        "101": 0.25 * (s11 - s13),
        "011": 0.25 * (s15 - s17),
        "120": 0.25 * (d7 + d9) - kx,
        "102": 0.25 * (d11 + d13) - kx,
        "210": 0.25 * (d7 - d9) - ky,
        "012": 0.25 * (d15 + d17) - ky,
        "201": 0.25 * (d11 - d13) - kz,
        "021": 0.25 * (d15 - d17) - kz,
        "220": 0.25 * (s7 + s9) - gx - hy,
        "202": 0.25 * (s11 + s13) - gx - hz,
        "022": 0.25 * (s15 + s17) - gy - hz,
    }
    return t, (dx, dy, dz, d7, d9, d11, d13, d15, d17)


def pull_back(b, t, u, fraction):
    rates = {k: (RATE2, RATE3, RATE4)[sum(map(int, k)) - 2] for k in t}
    n = {k: rates[k] * v for k, v in t.items()}
    ux, uy, uz = u
    fourth = n["220"] + n["202"] + n["022"]
    second = n["200"] + n["020"] + n["002"]
    part = fourth * (1.0 / 3.0)
    ax = n["200"] + part - 0.5 * n["022"]
    ay = n["020"] + part - 0.5 * n["202"]
    az = n["002"] + part - 0.5 * n["220"]
    rx = 2.0 * ax * ux + n["110"] * uy + n["101"] * uz
    ry = 2.0 * ay * uy + n["110"] * ux + n["011"] * uz
    rz = 2.0 * az * uz + n["101"] * ux + n["011"] * uy
    p0 = second * (1.0 / 3.0) + fourth * (1.0 / 9.0) - 0.5 * (rx * ux + ry * uy + rz * uz)
    px = rx + (n["120"] + n["102"]) * (1.0 / 3.0)
    py = ry + (n["210"] + n["012"]) * (1.0 / 3.0)
    pz = rz + (n["201"] + n["021"]) * (1.0 / 3.0)
    ex, ey, ez = p0 - n["200"], p0 - n["020"], p0 - n["002"]
    h = [p0, ex + px, ex - px, ey + py, ey - py, ez + pz, ez - pz]
    h += spread(ex - n["020"] - n["220"], -n["110"], px - n["120"], py - n["210"])
    h += spread(ex - n["002"] - n["202"], -n["101"], px - n["102"], pz - n["201"])
    h += spread(ey - n["002"] - n["022"], -n["011"], py - n["012"], pz - n["021"])
    open_part = 1.0 - fraction
    return [open_part * (b[i] + h[i]) + fraction * b[opposite[i]] for i in range(Q)]


def store_wrapped(put, first, step, value):
    row = first + step
    if row < 0:
        put(0, value[1:])
        put(CY - 1, value[:1])
    elif row + TILE > CY:
        put(row, value[:-1])
        put(0, value[-1:])
    else:
        put(row, value)


def put_moved(field, i, x, yt, value, direction):
    cx, cy, cz = (direction * c for c in velocities[i])
    if cz:
        value = pltpu.roll(value, cz % NZ, axis=1)
    x = (x + cx) & (CX - 1) if cx else x

    def put(row, part):
        field[i, x, pl.ds(row, part.shape[0]), :] = part

    store_wrapped(put, yt * TILE, cy, value)


def by_parity(axis, even, odd):
    is_odd = jnp.full(even.shape, lax.axis_index(axis) & 1, jnp.int32) == 1
    return jnp.where(is_odd, odd, even)


def pair_up(up, down, first, second):
    first[...] = by_parity("gx", down[...], up[...])
    second[...] = by_parity("gx", up[...], down[...])


def x_arrived(sign, line, first, second):
    a, b = first[line, :], second[line, :]
    return by_parity("gx", a, b) if sign == 1 else by_parity("gx", b, a)


def y_arrived(sign, line, low, high):
    return low[line, :] if sign == 1 else high[line, :]


def x_faces(fields, direction, x_up, x_down):
    for n, field in enumerate(fields):
        for sign, x, message in ((1, 0, x_up), (-1, CX - 1, x_down)):
            for k, i in enumerate(moving(0, sign, direction)):
                message[pl.ds(n * FACE + k * CY, CY), :] = field[i, x]


def y_faces(field, y_up, y_down):
    for sign, row, message in ((1, 0, y_up), (-1, CY - 1, y_down)):
        for k, i in enumerate(moving(1, sign, -1)):
            for x in range(CX):
                message[pl.ds(k * CX + x, 1), :] = field[i, x, pl.ds(row, 1), :]


def fill_x(fields, direction, first, second):
    for n, field in enumerate(fields):
        for sign, x in ((1, 0), (-1, CX - 1)):
            for k, i in enumerate(moving(0, sign, direction)):
                line = pl.ds(n * FACE + k * CY, CY)
                field[i, x] = x_arrived(sign, line, first, second)


def fill_y(fields, direction, first, second):
    for n, field in enumerate(fields):
        for sign, row in ((1, 0), (-1, CY - 1)):
            for k, i in enumerate(moving(1, sign, direction)):
                line = pl.ds(n * FACE + k * CX, CX)
                face = y_arrived(sign, line, first, second)
                for x in range(CX):
                    field[i, x, pl.ds(row, 1), :] = face[x : x + 1]


def rows(yt):
    return pl.ds(yt * TILE, TILE)


def unrolled(start, stop, count, step):
    @pl.loop(0, (stop - start) // count)
    def _(n):
        for k in range(count):
            step(start + n * count + k)


def iota(shape, dim):
    return lax.broadcasted_iota(jnp.int32, shape, dim)


def column(row, pick):
    return jnp.sum(jnp.where(pick, row, 0.0), axis=1, keepdims=True)


def block_numbers(owners, slots, table, y_up, y_down):
    shape = (64, 64)
    row, lane = iota(shape, 0), iota(shape, 1)
    same = row == lane
    owner_row, slot_row = owners[...].astype(jnp.float32), slots[...].astype(jnp.float32)
    owner_col = column(owner_row, same)
    earlier = (owner_row == owner_col) & (lane < row)
    rank = jnp.sum(jnp.where(earlier, 1.0, 0.0), axis=1, keepdims=True)
    number = owner_col * 1024.0 + column(slot_row, same) * 4.0 + rank
    wide = (64, NZ)
    spot = iota(wide, 1) == (iota(wide, 0) & 7) + 1
    spread_out = jnp.where(spot, number, 0.0)
    table[...] = jnp.zeros((16, NZ), jnp.float32)
    for xb in range(8):
        line = jnp.sum(spread_out[xb * 8 : xb * 8 + 8], axis=0, keepdims=True)
        table[pl.ds(xb + 1, 1), :] = line
    held = table[...]
    eye = iota((16, NZ), 0) == iota((16, NZ), 1)
    for yb, message in ((8, y_up), (1, y_down)):
        part = jnp.where(eye, held[:, yb : yb + 1], 0.0)
        message[pl.ds(META, 1), :] = jnp.sum(part, axis=0, keepdims=True)


def solidity(porosity, porous, walls):
    wall = walls == 1
    panel = porous.astype(jnp.float32)
    return jnp.where(wall, 1.0, panel * porosity), jnp.where(wall, 0.0, panel)


def edge_kernel(
    f_hbm, porosity_hbm, porous_hbm, walls_hbm, owners_hbm, slots_hbm,
    table, y_up, y_down, f, porosity, porous, walls, owners, slots, sems,
):
    numbers = [
        pltpu.make_async_copy(owners_hbm, owners, sems.at[0]),
        pltpu.make_async_copy(slots_hbm, slots, sems.at[1]),
    ]
    faces = [(1, CY - 1, y_up), (-1, 0, y_down)]
    lines = []
    for n, (_, y, _) in enumerate(faces):
        copies = [pltpu.make_async_copy(f_hbm.at[:, :, y, :], f.at[n], sems.at[4 * n + 2])]
        for k, (source, target) in enumerate(
            ((porosity_hbm, porosity), (porous_hbm, porous), (walls_hbm, walls))
        ):
            node = source.at[:, y, :]
            copies.append(pltpu.make_async_copy(node, target.at[n], sems.at[4 * n + 3 + k]))
        lines.append(copies)
    for copy in sum(lines, numbers):
        copy.start()
    for copy in numbers:
        copy.wait()
    block_numbers(owners, slots, table, y_up, y_down)
    for n, (sign, _, message) in enumerate(faces):
        for copy in lines[n]:
            copy.wait()
        for tile in range(CX // TILE):
            at = (n, rows(tile))
            pops = [f[n, i, rows(tile), :] for i in range(Q)]
            fraction, open_panel = solidity(porosity[at], porous[at], walls[at])
            c = correction(off_equilibrium(pops)[1])
            for k, i in enumerate(moving(1, sign, 1)):
                relaxed = pops[i] - c[i]
                change = pops[opposite[i]] - relaxed
                pair = (relaxed + fraction * change, open_panel * change)
                for field, value in enumerate(pair):
                    if velocities[i][2]:
                        value = pltpu.roll(value, velocities[i][2] % NZ, axis=1)

                    def put(row, part, base=field * FACE + k * CX, message=message):
                        message[pl.ds(base + row, part.shape[0]), :] = part

                    store_wrapped(put, tile * TILE, velocities[i][0], value)


def turn_kernel(y_first, y_second, frac, first, second, up, down):
    del frac
    for sx, message in ((1, up), (-1, down)):
        for n, sy in enumerate((1, -1)):
            k = moving(1, sy, 1).index(velocities.index((sx, sy, 0)))
            row = k * CX + (0 if sx == 1 else CX - 1)
            for field in range(2):
                line = pl.ds(field * FACE + row, 1)
                value = y_arrived(sy, line, y_first, y_second)
                message[pl.ds(2 * n + field, 1), :] = value
            numbers = y_arrived(sy, pl.ds(META, 1), y_first, y_second)
            message[pl.ds(4 + n, 1), :] = numbers
    pair_up(up, down, first, second)


def corner_arrived(sx, sy, row, messages):
    n = 0 if sy == 1 else 1
    line = pl.ds(4 + n if row == 2 else 2 * n + row, 1)
    return x_arrived(sx, line, *messages)


def forward_kernel(
    f_hbm, porosity_hbm, porous_hbm, walls_hbm, adjoint_hbm, table,
    moved, gap, adjoint, frac, mask, vel, x_first, x_second,
    f, porosity, porous, walls, x_up, x_down, f_sems, sems,
):
    def planes(n):
        part = pl.ds(n * PLANES, PLANES)
        return pltpu.make_async_copy(f_hbm.at[:, part], f.at[:, part], f_sems.at[n])

    small = [
        pltpu.make_async_copy(porosity_hbm, porosity, sems.at[0]),
        pltpu.make_async_copy(porous_hbm, porous, sems.at[1]),
        pltpu.make_async_copy(walls_hbm, walls, sems.at[2]),
    ]
    later = pltpu.make_async_copy(adjoint_hbm, adjoint, sems.at[3])
    for copy in small:
        copy.start()
    for n in range(CX // PLANES):
        planes(n).start()
    later.start()
    for copy in small:
        copy.wait()

    def plane(x):
        for yt in range(CY // TILE):
            at = (x, rows(yt))
            pops = [f[i, x, rows(yt), :] for i in range(Q)]
            fraction, open_panel = solidity(porosity[at], porous[at], walls[at])
            frac[at] = fraction
            mask[at] = open_panel
            u, e, _ = off_equilibrium(pops)
            for axis in range(3):
                vel[axis, x, rows(yt), :] = u[axis]
            c = correction(e)
            for i in range(Q):
                relaxed = pops[i] - c[i]
                change = pops[opposite[i]] - relaxed
                put_moved(gap, i, x, yt, open_panel * change, 1)
                put_moved(moved, i, x, yt, relaxed + fraction * change, 1)

    @pl.loop(0, CX // PLANES)
    def _(n):
        planes(n).wait()
        for k in range(PLANES):
            plane(n * PLANES + k)

    x_faces((moved, gap), 1, x_up, x_down)
    x_up[pl.ds(META, 1), :] = table[pl.ds(8, 1), :]
    x_down[pl.ds(META, 1), :] = table[pl.ds(1, 1), :]
    pair_up(x_up, x_down, x_first, x_second)
    later.wait()


def late_blocks(xb, halves, fields, adjoint, frac, mask, late, sums):
    for yt in range(CY // TILE):
        parts = {}
        for half in halves:
            x = xb * 2 + half
            at = (x, rows(yt))
            read = [fields[0][i, x, rows(yt), :] for i in range(Q)]
            u, e, df = off_equilibrium(read)
            b = [adjoint[i, x, rows(yt), :] for i in range(Q)]
            t, db = covector(b)
            total = sum(t[k] * e[k] for k in t) - sum(p * q for p, q in zip(db, df))
            total = mask[at] * total
            out = pull_back(b, t, u, frac[at])
            key = (0, 0)
            parts[key] = parts[key] + total if key in parts else total
            for i in range(Q):
                cx, cy, _ = velocities[i]
                key = ((half - cx) // 2, cy)
                early = out[i] * fields[1][i, x, rows(yt), :]
                parts[key] = parts[key] + early if key in parts else early
                put_moved(late, i, x, yt, out[i], -1)
        for (step, cy), part in parts.items():
            at = (xb + 1 + step, pl.ds(PAD_Y + yt * TILE - cy, TILE))
            sums[at] = sums[at] + part


def late_kernel(
    moved_in, gap_in, y_first, y_second, adjoint, frac, mask, moved, gap, late, sums
):
    del moved_in, gap_in
    fields = (moved, gap)
    fill_y(fields, 1, y_first, y_second)
    sums[...] = jnp.zeros((EXT_XB, EXT_Y, NZ), jnp.float32)

    def step(xb, halves=(0, 1)):
        late_blocks(xb, halves, fields, adjoint, frac, mask, late, sums)

    step(0, (1,))
    step(CX // 2 - 1, (0,))
    unrolled(1, CX // 2 - 1, 2, step)


def late_rest_kernel(
    late_in, sums_in, moved_in, gap_in, table, xs_in, xf_in, yf_in, ys_in,
    c_first, c_second, adjoint, frac, mask,
    late, sums, moved, gap, xf, xs, yu, yd, send_hbm,
    xu, xd, ext, ring, owner_of, scaled, send, sem,
):
    del late_in, sums_in, moved_in, gap_in
    fields = (moved, gap)
    messages = (c_first, c_second)
    fill_x(fields, 1, xf_in, xs_in)
    for sx, x in ((1, 0), (-1, CX - 1)):
        for sy, y in ((1, 0), (-1, CY - 1)):
            i = velocities.index((sx, sy, 0))
            for n, field in enumerate(fields):
                field[i, x, pl.ds(y, 1), :] = corner_arrived(sx, sy, n, messages)
    for xb, half in ((0, 0), (CX // 2 - 1, 1)):
        late_blocks(xb, (half,), fields, adjoint, frac, mask, late, sums)

    row, lane = iota((16, NZ), 0), iota((16, NZ), 1)
    numbers = pl.ds(META, 1)
    held = table[...]
    for sign, place in ((1, 0), (-1, 9)):
        here = x_arrived(sign, numbers, xf_in, xs_in)
        held = jnp.where(row == place, here, held)
    for sign, place in ((1, 0), (-1, 9)):
        here = column(y_arrived(sign, numbers, yf_in, ys_in), row == lane)
        held = jnp.where((lane == place) & (row > 0) & (row < 9), here, held)
    for sx, x in ((1, 0), (-1, 9)):
        for sy, y in ((1, 0), (-1, 9)):
            there = iota((1, NZ), 1) == (8 if sx == 1 else 1)
            here = column(corner_arrived(sx, sy, 2, messages), there)
            held = jnp.where((row == x) & (lane == y), here, held)
    ext[...] = held

    def put_lines(start, number, spot, total):
        number = number.astype(jnp.int32)
        lane = iota((total.shape[0], NZ), 1)
        spot = spot + (number & 3) if isinstance(spot, int) else spot(number & 3)
        line = pl.ds(start, total.shape[0])
        owner_of[line, :] = jnp.where(lane == jnp.right_shift(number, 10), 1.0, 0.0)
        patch = (jnp.right_shift(number, 2) & 255).astype(jnp.float32)
        value = jnp.where(lane == spot, jnp.sum(total, axis=1, keepdims=True), 0.0)
        scaled[line, :] = jnp.where(lane == spot + SLOT_LANE, patch, value)

    pick = iota((8, NZ), 1) == iota((8, NZ), 0) + 1
    for xb in range(EXT_XB):
        total = sums[xb, pl.ds(PAD_Y, 8, stride=2), :] + sums[xb, pl.ds(PAD_Y + 1, 8, stride=2), :]
        spot = 2 if xb == 0 else 4 if xb == 9 else 0
        put_lines(xb * 8, column(ext[pl.ds(xb, 1), :], pick), spot, total)
    ring[...] = jnp.zeros((32, NZ), jnp.float32)
    for xb in range(EXT_XB):
        ring[pl.ds(xb, 1), :] = sums[xb, pl.ds(PAD_Y - 1, 1), :]
        ring[pl.ds(16 + xb, 1), :] = sums[xb, pl.ds(PAD_Y + CY, 1), :]
    row = iota((16, 1), 0)
    for n, (face, corner, lane) in enumerate(((6, 10, 0), (8, 12, 9))):

        def spot(rank, face=face, corner=corner):
            side = jnp.where(row == 9, corner + 1, face + rank)
            return jnp.where(row == 0, corner, side)

        pick = (iota((16, NZ), 1) == lane) & (iota((16, NZ), 0) < EXT_XB)
        total = ring[pl.ds(16 * n, 16), :]
        put_lines(RING + 16 * n, column(ext[...], pick), spot, total)
    send[pl.ds(0, DEVICES, stride=2), :] = lax.dot_general(
        owner_of[...],
        scaled[...],
        (((0,), (0,)), ((), ())),
        precision=lax.Precision.HIGHEST,
        preferred_element_type=jnp.float32,
    )
    for there, i, x, y in corners(1):
        send[pl.ds(2 * there + 1, 1), :] = late[i, x, pl.ds(y, 1), :]
    copy = pltpu.make_async_copy(send, send_hbm, sem)
    copy.start()
    x_faces((late,), -1, xu, xd)
    y_faces(late, yu, yd)
    pair_up(xu, xd, xf, xs)
    copy.wait()


def corners(direction):
    gx, gy = lax.axis_index("gx"), lax.axis_index("gy")
    for ex in (1, -1):
        for ey in (1, -1):
            there_x = (gx + direction * ex) & (N_GX - 1)
            there_y = (gy + direction * ey) & (N_GY - 1)
            i = velocities.index((-ex, -ey, 0))
            x, y = 0 if ex == 1 else CX - 1, 0 if ey == 1 else CY - 1
            yield there_x * N_GY + there_y, i, x, y


def early_plane(x, late, frac, vel, put):
    for yt in range(CY // TILE):
        b = [late[i, x, rows(yt), :] for i in range(Q)]
        t, _ = covector(b)
        u = [vel[axis, x, rows(yt), :] for axis in range(3)]
        result = pull_back(b, t, u, frac[x, rows(yt)])
        for i in range(Q):
            put(i, yt, result[i])


def early_kernel(late_in, y_first, y_second, frac, vel, late, out, hold, sems):
    del late_in
    fill_y((late,), -1, y_first, y_second)

    def planes(n):
        part = pl.ds(1 + n * 2, 2)
        return pltpu.make_async_copy(hold.at[:, part], out.at[:, part], sems.at[n])

    @pl.loop(0, CX // 2 - 1)
    def _(n):
        for k in range(2):
            x = 1 + n * 2 + k

            def put(i, yt, value, x=x):
                hold[i, x, rows(yt), :] = value

            early_plane(x, late, frac, vel, put)
        planes(n).start()

    for n in range(CX // 2 - 1):
        planes(n).wait()


def last_kernel(
    out_in, late_in, second, first, got, frac, vel, late, out, patch_out, hold, patch, sems
):
    del out_in, late_in
    fill_x((late,), -1, first, second)
    for here, i, x, y in corners(-1):
        late[i, x, pl.ds(y, 1), :] = got[pl.ds(2 * here + 1, 1), :]
    copies = []
    for n, x in enumerate((0, CX - 1)):

        def put(i, yt, value, n=n):
            hold[n, i, rows(yt), :] = value

        early_plane(x, late, frac, vel, put)
        copies.append(pltpu.make_async_copy(hold.at[n], out.at[:, x], sems.at[n]))
        copies[n].start()
    data = got[pl.ds(0, DEVICES, stride=2), :].T
    part = 64
    for start in range(0, PATCH_DEV, part):
        number = (iota((part, DEVICES), 0) + start).astype(jnp.float32)
        total = jnp.zeros((part, DEVICES), jnp.float32)
        for k in range(PARTS):
            hit = data[SLOT_LANE + k : SLOT_LANE + k + 1] == number
            total = total + jnp.where(hit, data[k : k + 1], 0.0)
        patch[:, pl.ds(start, part)] = jnp.sum(total, axis=1)[None]
    copies.append(pltpu.make_async_copy(patch, patch_out, sems.at[2]))
    copies[2].start()
    for copy in copies:
        copy.wait()


VMEM = pl.BlockSpec(memory_space=pltpu.VMEM)
ANY = pl.BlockSpec(memory_space=pl.ANY)
LIMIT = 8 * 2**20


def vmem(*shape):
    return pltpu.VMEM(shape, jnp.float32)


def call(kernel, ins, outs, scratch=(), aliases=None, flops=0, hbm_ins=0, hbm_outs=()):
    held = [pltpu.with_memory_space_constraint(x, pltpu.HBM) for x in ins[:hbm_ins]]
    held += [pltpu.with_memory_space_constraint(x, pltpu.VMEM) for x in ins[hbm_ins:]]
    return pl.pallas_call(
        kernel,
        out_shape=[*outs, *hbm_outs],
        in_specs=[ANY] * hbm_ins + [VMEM] * (len(ins) - hbm_ins),
        out_specs=[VMEM] * len(outs) + [ANY] * len(hbm_outs),
        scratch_shapes=list(scratch),
        input_output_aliases=aliases or {},
        compiler_params=pltpu.CompilerParams(vmem_limit_bytes=LIMIT),
        cost_estimate=pl.CostEstimate(flops=flops, bytes_accessed=0, transcendentals=0),
    )(*held)


FIELD = vmem(Q, CX, CY, NZ)
NODE = vmem(CX, CY, NZ)
MESSAGE = vmem(MESSAGE_ROWS, NZ)
SHORT_MESSAGE = vmem(FACE, NZ)
LINES = vmem(LINE_COUNT, NZ)


def shift(block, axis, step):
    count = lax.axis_size(axis)
    return lax.ppermute(block, axis, [(i, (i + step) % count) for i in range(count)])


def swap(block, axis, step):
    count = lax.axis_size(axis)
    return lax.ppermute(
        block, axis, [(i, (i + (-step if i % 2 else step)) % count) for i in range(count)]
    )


def body(populations, porosity, adjoint_in, porous, walls, owners, slots):
    ints = pltpu.VMEM((CX, CY, NZ), jnp.int32)
    dma = pltpu.SemaphoreType.DMA
    table, yf, ys = call(
        edge_kernel,
        [populations, porosity, porous, walls, owners.reshape(1, 64), slots.reshape(1, 64)],
        [vmem(16, NZ), MESSAGE, MESSAGE],
        scratch=[vmem(2, Q, CX, NZ), vmem(2, CX, NZ)]
        + [pltpu.VMEM((2, CX, NZ), jnp.int32)] * 2
        + [pltpu.VMEM((1, 64), jnp.int32)] * 2
        + [dma((10,))],
        hbm_ins=6,
    )
    yf = shift(yf, "gy", 1)
    ys = shift(ys, "gy", -1)
    moved, gap, adjoint, frac, mask, vel, xf, xs = call(
        forward_kernel,
        [populations, porosity, porous, walls, adjoint_in, table],
        [FIELD] * 3 + [NODE] * 2 + [vmem(3, CX, CY, NZ), MESSAGE, MESSAGE],
        scratch=[FIELD, NODE, ints, ints, MESSAGE, MESSAGE, dma((CX // PLANES,)), dma((4,))],
        hbm_ins=5,
        flops=20_000_000,
    )
    xs = swap(xs, "gx", 1)
    xf = swap(xf, "gx", -1)
    corner = call(
        turn_kernel, [yf, ys, frac], [vmem(TILE, NZ)] * 2, scratch=[vmem(TILE, NZ)] * 2
    )
    corner = [swap(corner[0], "gx", -1), swap(corner[1], "gx", 1)]
    sums_shape = vmem(EXT_XB, EXT_Y, NZ)
    moved, gap, late, sums = call(
        late_kernel,
        [moved, gap, yf, ys, adjoint, frac, mask],
        [FIELD, FIELD, FIELD, sums_shape],
        aliases={0: 0, 1: 1},
        flops=20_000_000,
    )
    late, _, _, _, xf, xs, yf, ys, send = call(
        late_rest_kernel,
        [late, sums, moved, gap, table, xs, xf, yf, ys, *corner, adjoint, frac, mask],
        [FIELD, sums_shape, FIELD, FIELD] + [SHORT_MESSAGE] * 4,
        hbm_outs=[jax.ShapeDtypeStruct((2 * DEVICES, NZ), jnp.float32)],
        scratch=[SHORT_MESSAGE] * 2
        + [vmem(16, NZ), vmem(32, NZ), LINES, LINES, vmem(2 * DEVICES, NZ), dma],
        aliases={0: 0, 1: 1, 2: 2, 3: 3},
    )
    got = lax.all_to_all(send, ("gx", "gy"), split_axis=0, concat_axis=0, tiled=True)
    yf = shift(yf, "gy", 1)
    ys = shift(ys, "gy", -1)
    xs = swap(xs, "gx", 1)
    xf = swap(xf, "gx", -1)
    adjoint_shape = jax.ShapeDtypeStruct((Q, CX, CY, NZ), jnp.float32)
    late, adjoint_out = call(
        early_kernel,
        [late, yf, ys, frac, vel],
        [FIELD],
        hbm_outs=[adjoint_shape],
        scratch=[FIELD, dma((CX // 2 - 1,))],
        aliases={0: 0},
        flops=20_000_000,
    )
    _, adjoint_out, patch = call(
        last_kernel,
        [adjoint_out, late, xs, xf, got, frac, vel],
        [FIELD],
        hbm_ins=1,
        hbm_outs=[adjoint_shape, jax.ShapeDtypeStruct((1, PATCH_DEV), jnp.float32)],
        scratch=[vmem(2, Q, CY, NZ), vmem(1, PATCH_DEV), dma((3,))],
        aliases={0: 1, 1: 0},
    )
    return adjoint_out, patch.reshape(PATCH_DEV)


def solution(mesh):
    return jax.shard_map(
        body,
        mesh=mesh,
        in_specs=(
            P(None, "gx", "gy", None),
            P("gx", "gy", None),
            P(None, "gx", "gy", None),
            P("gx", "gy", None),
            P("gx", "gy", None),
            P("gx", "gy", None, None),
            P("gx", "gy", None),
        ),
        out_specs=(P(None, "gx", "gy", None), P(("gx", "gy"))),
        check_vma=False,
    )
```

```python
import jax
import jax.numpy as jnp
from jax import lax
from jax.experimental import pallas as pl
from jax.experimental.pallas import tpu as pltpu
from jax.sharding import PartitionSpec as P

Q = 19
CX = 16
CY = 16
NZ = 128
TILE = 8
PAD_Y = 8
EXT_Y = 32
EXT_XB = 10
RING = 80
LINE_COUNT = 112
DEVICES = 128
N_GX, N_GY = 8, 16
PATCH_DEV = 256
SLOT_LANE = 64
PARTS = 14
FACE = 80
META = 160
MESSAGE_ROWS = 168
PLANES = 4

velocities = [
    (0, 0, 0),
    (1, 0, 0),
    (-1, 0, 0),
    (0, 1, 0),
    (0, -1, 0),
    (0, 0, 1),
    (0, 0, -1),
    (1, 1, 0),
    (-1, -1, 0),
    (1, -1, 0),
    (-1, 1, 0),
    (1, 0, 1),
    (-1, 0, -1),
    (1, 0, -1),
    (-1, 0, 1),
    (0, 1, 1),
    (0, -1, -1),
    (0, 1, -1),
    (0, -1, 1),
]
opposite = [0, 2, 1, 4, 3, 6, 5, 8, 7, 10, 9, 12, 11, 14, 13, 16, 15, 18, 17]
RATE2, RATE3, RATE4 = 1.25, 1.5, 1.4


def moving(axis, sign, direction):
    return [i for i in range(Q) if direction * velocities[i][axis] == sign]


def edge(f, first):
    s, d = f[first] + f[first + 1], f[first] - f[first + 1]
    s2, d2 = f[first + 2] + f[first + 3], f[first + 2] - f[first + 3]
    return s, d, s2, d2


def off_equilibrium(f):
    sx, dx = f[1] + f[2], f[1] - f[2]
    sy, dy = f[3] + f[4], f[3] - f[4]
    sz, dz = f[5] + f[6], f[5] - f[6]
    s7, d7, s9, d9 = edge(f, 7)
    s11, d11, s13, d13 = edge(f, 11)
    s15, d15, s17, d17 = edge(f, 15)
    m220, m110, m120, m210 = s7 + s9, s7 - s9, d7 + d9, d7 - d9
    m202, m101, m102, m201 = s11 + s13, s11 - s13, d11 + d13, d11 - d13
    m022, m011, m012, m021 = s15 + s17, s15 - s17, d15 + d17, d15 - d17
    m200, m020, m002 = sx + m220 + m202, sy + m220 + m022, sz + m202 + m022
    jx, jy, jz = dx + (m120 + m102), dy + (m210 + m012), dz + (m201 + m021)
    rho = f[0] + (sx + sy + sz) + (m220 + m202 + m022)
    inv = 1.0 / rho
    ux, uy, uz = jx * inv, jy * inv, jz * inv
    qx, qy, qz = jx * ux, jy * uy, jz * uz
    third = rho * (1.0 / 3.0)
    ninth = rho * (1.0 / 9.0) - (qx + qy + qz) * (1.0 / 6.0)
    tx, ty, tz = jx * (1.0 / 3.0), jy * (1.0 / 3.0), jz * (1.0 / 3.0)
    e = {
        "200": RATE2 * (m200 - third - qx),
        "020": RATE2 * (m020 - third - qy),
        "002": RATE2 * (m002 - third - qz),
        "110": RATE2 * (m110 - jx * uy),
        "101": RATE2 * (m101 - jx * uz),
        "011": RATE2 * (m011 - jy * uz),
        "120": RATE3 * (m120 - tx),
        "102": RATE3 * (m102 - tx),
        "210": RATE3 * (m210 - ty),
        "012": RATE3 * (m012 - ty),
        "201": RATE3 * (m201 - tz),
        "021": RATE3 * (m021 - tz),
        "220": RATE4 * (m220 - ninth - 0.5 * (qx + qy)),
        "202": RATE4 * (m202 - ninth - 0.5 * (qx + qz)),
        "022": RATE4 * (m022 - ninth - 0.5 * (qy + qz)),
    }
    return (ux, uy, uz), e, (dx, dy, dz, d7, d9, d11, d13, d15, d17)


def spread(t, g, a, b):
    even, odd = t + g, t - g
    plus, minus = a + b, a - b
    return [even + plus, even - plus, odd + minus, odd - minus]


def correction(e):
    q = {k: 0.25 * v for k, v in e.items()}
    xy = spread(q["220"], q["110"], q["120"], q["210"])
    xz = spread(q["202"], q["101"], q["102"], q["201"])
    yz = spread(q["022"], q["011"], q["012"], q["021"])
    faces = []
    for second, fourth, odd in (
        ("200", ("220", "202"), ("120", "102")),
        ("020", ("220", "022"), ("210", "012")),
        ("002", ("202", "022"), ("201", "021")),
    ):
        mean = 0.5 * e[second] - 2.0 * (q[fourth[0]] + q[fourth[1]])
        lean = 2.0 * (q[odd[0]] + q[odd[1]])
        faces += [mean - lean, mean + lean]
    rest = (e["220"] + e["202"] + e["022"]) - (e["200"] + e["020"] + e["002"])
    return [rest] + faces + xy + xz + yz


def covector(b):
    hx, dx = 0.5 * (b[1] + b[2]), b[1] - b[2]
    hy, dy = 0.5 * (b[3] + b[4]), b[3] - b[4]
    hz, dz = 0.5 * (b[5] + b[6]), b[5] - b[6]
    s7, d7, s9, d9 = edge(b, 7)
    s11, d11, s13, d13 = edge(b, 11)
    s15, d15, s17, d17 = edge(b, 15)
    gx, gy, gz = hx - b[0], hy - b[0], hz - b[0]
    kx, ky, kz = 0.5 * dx, 0.5 * dy, 0.5 * dz
    t = {
        "200": gx,
        "020": gy,
        "002": gz,
        "110": 0.25 * (s7 - s9),
        "101": 0.25 * (s11 - s13),
        "011": 0.25 * (s15 - s17),
        "120": 0.25 * (d7 + d9) - kx,
        "102": 0.25 * (d11 + d13) - kx,
        "210": 0.25 * (d7 - d9) - ky,
        "012": 0.25 * (d15 + d17) - ky,
        "201": 0.25 * (d11 - d13) - kz,
        "021": 0.25 * (d15 - d17) - kz,
        "220": 0.25 * (s7 + s9) - gx - hy,
        "202": 0.25 * (s11 + s13) - gx - hz,
        "022": 0.25 * (s15 + s17) - gy - hz,
    }
    return t, (dx, dy, dz, d7, d9, d11, d13, d15, d17)


def pull_back(b, t, u, fraction):
    rates = {k: (RATE2, RATE3, RATE4)[sum(map(int, k)) - 2] for k in t}
    n = {k: rates[k] * v for k, v in t.items()}
    ux, uy, uz = u
    fourth = n["220"] + n["202"] + n["022"]
    second = n["200"] + n["020"] + n["002"]
    part = fourth * (1.0 / 3.0)
    ax = n["200"] + part - 0.5 * n["022"]
    ay = n["020"] + part - 0.5 * n["202"]
    az = n["002"] + part - 0.5 * n["220"]
    rx = 2.0 * ax * ux + n["110"] * uy + n["101"] * uz
    ry = 2.0 * ay * uy + n["110"] * ux + n["011"] * uz
    rz = 2.0 * az * uz + n["101"] * ux + n["011"] * uy
    p0 = second * (1.0 / 3.0) + fourth * (1.0 / 9.0) - 0.5 * (rx * ux + ry * uy + rz * uz)
    px = rx + (n["120"] + n["102"]) * (1.0 / 3.0)
    py = ry + (n["210"] + n["012"]) * (1.0 / 3.0)
    pz = rz + (n["201"] + n["021"]) * (1.0 / 3.0)
    ex, ey, ez = p0 - n["200"], p0 - n["020"], p0 - n["002"]
    h = [p0, ex + px, ex - px, ey + py, ey - py, ez + pz, ez - pz]
    h += spread(ex - n["020"] - n["220"], -n["110"], px - n["120"], py - n["210"])
    h += spread(ex - n["002"] - n["202"], -n["101"], px - n["102"], pz - n["201"])
    h += spread(ey - n["002"] - n["022"], -n["011"], py - n["012"], pz - n["021"])
    open_part = 1.0 - fraction
    return [open_part * (b[i] + h[i]) + fraction * b[opposite[i]] for i in range(Q)]


def store_wrapped(put, first, step, value):
    row = first + step
    if row < 0:
        put(0, value[1:])
        put(CY - 1, value[:1])
    elif row + TILE > CY:
        put(row, value[:-1])
        put(0, value[-1:])
    else:
        put(row, value)


def put_moved(field, i, x, yt, value, direction):
    cx, cy, cz = (direction * c for c in velocities[i])
    if cz:
        value = pltpu.roll(value, cz % NZ, axis=1)
    x = (x + cx) & (CX - 1) if cx else x

    def put(row, part):
        field[i, x, pl.ds(row, part.shape[0]), :] = part

    store_wrapped(put, yt * TILE, cy, value)


def by_parity(axis, even, odd):
    is_odd = jnp.full(even.shape, lax.axis_index(axis) & 1, jnp.int32) == 1
    return jnp.where(is_odd, odd, even)


def pair_up(up, down, first, second):
    first[...] = by_parity("gx", down[...], up[...])
    second[...] = by_parity("gx", up[...], down[...])


def x_arrived(sign, line, first, second):
    a, b = first[line, :], second[line, :]
    return by_parity("gx", a, b) if sign == 1 else by_parity("gx", b, a)


def y_arrived(sign, line, low, high):
    return low[line, :] if sign == 1 else high[line, :]


def x_faces(fields, direction, x_up, x_down):
    for n, field in enumerate(fields):
        for sign, x, message in ((1, 0, x_up), (-1, CX - 1, x_down)):
            for k, i in enumerate(moving(0, sign, direction)):
                message[pl.ds(n * FACE + k * CY, CY), :] = field[i, x]


def y_faces(field, y_up, y_down):
    for sign, row, message in ((1, 0, y_up), (-1, CY - 1, y_down)):
        for k, i in enumerate(moving(1, sign, -1)):
            for x in range(CX):
                message[pl.ds(k * CX + x, 1), :] = field[i, x, pl.ds(row, 1), :]


def fill_x(fields, direction, first, second):
    for n, field in enumerate(fields):
        for sign, x in ((1, 0), (-1, CX - 1)):
            for k, i in enumerate(moving(0, sign, direction)):
                line = pl.ds(n * FACE + k * CY, CY)
                field[i, x] = x_arrived(sign, line, first, second)


def fill_y(fields, direction, first, second):
    for n, field in enumerate(fields):
        for sign, row in ((1, 0), (-1, CY - 1)):
            for k, i in enumerate(moving(1, sign, direction)):
                line = pl.ds(n * FACE + k * CX, CX)
                face = y_arrived(sign, line, first, second)
                for x in range(CX):
                    field[i, x, pl.ds(row, 1), :] = face[x : x + 1]


def rows(yt):
    return pl.ds(yt * TILE, TILE)


def unrolled(start, stop, count, step):
    @pl.loop(0, (stop - start) // count)
    def _(n):
        for k in range(count):
            step(start + n * count + k)


def iota(shape, dim):
    return lax.broadcasted_iota(jnp.int32, shape, dim)


def column(row, pick):
    return jnp.sum(jnp.where(pick, row, 0.0), axis=1, keepdims=True)


def block_numbers(owners, slots, table, y_up, y_down):
    shape = (64, 64)
    row, lane = iota(shape, 0), iota(shape, 1)
    same = row == lane
    owner_row, slot_row = owners[...].astype(jnp.float32), slots[...].astype(jnp.float32)
    owner_col = column(owner_row, same)
    earlier = (owner_row == owner_col) & (lane < row)
    rank = jnp.sum(jnp.where(earlier, 1.0, 0.0), axis=1, keepdims=True)
    number = owner_col * 1024.0 + column(slot_row, same) * 4.0 + rank
    wide = (64, NZ)
    spot = iota(wide, 1) == (iota(wide, 0) & 7) + 1
    spread_out = jnp.where(spot, number, 0.0)
    table[...] = jnp.zeros((16, NZ), jnp.float32)
    for xb in range(8):
        line = jnp.sum(spread_out[xb * 8 : xb * 8 + 8], axis=0, keepdims=True)
        table[pl.ds(xb + 1, 1), :] = line
    held = table[...]
    eye = iota((16, NZ), 0) == iota((16, NZ), 1)
    for yb, message in ((8, y_up), (1, y_down)):
        part = jnp.where(eye, held[:, yb : yb + 1], 0.0)
        message[pl.ds(META, 1), :] = jnp.sum(part, axis=0, keepdims=True)


def solidity(porosity, porous, walls):
    wall = walls == 1
    panel = porous.astype(jnp.float32)
    return jnp.where(wall, 1.0, panel * porosity), jnp.where(wall, 0.0, panel)


def edge_kernel(
    f_hbm, porosity_hbm, porous_hbm, walls_hbm, owners_hbm, slots_hbm,
    table, y_up, y_down, f, porosity, porous, walls, owners, slots, sems,
):
    numbers = [
        pltpu.make_async_copy(owners_hbm, owners, sems.at[0]),
        pltpu.make_async_copy(slots_hbm, slots, sems.at[1]),
    ]
    faces = [(1, CY - 1, y_up), (-1, 0, y_down)]
    lines = []
    for n, (_, y, _) in enumerate(faces):
        copies = [pltpu.make_async_copy(f_hbm.at[:, :, y, :], f.at[n], sems.at[4 * n + 2])]
        for k, (source, target) in enumerate(
            ((porosity_hbm, porosity), (porous_hbm, porous), (walls_hbm, walls))
        ):
            node = source.at[:, y, :]
            copies.append(pltpu.make_async_copy(node, target.at[n], sems.at[4 * n + 3 + k]))
        lines.append(copies)
    for copy in sum(lines, numbers):
        copy.start()
    for copy in numbers:
        copy.wait()
    block_numbers(owners, slots, table, y_up, y_down)
    for n, (sign, _, message) in enumerate(faces):
        for copy in lines[n]:
            copy.wait()
        for tile in range(CX // TILE):
            at = (n, rows(tile))
            pops = [f[n, i, rows(tile), :] for i in range(Q)]
            fraction, open_panel = solidity(porosity[at], porous[at], walls[at])
            c = correction(off_equilibrium(pops)[1])
            for k, i in enumerate(moving(1, sign, 1)):
                relaxed = pops[i] - c[i]
                change = pops[opposite[i]] - relaxed
                pair = (relaxed + fraction * change, open_panel * change)
                for field, value in enumerate(pair):
                    if velocities[i][2]:
                        value = pltpu.roll(value, velocities[i][2] % NZ, axis=1)

                    def put(row, part, base=field * FACE + k * CX, message=message):
                        message[pl.ds(base + row, part.shape[0]), :] = part

                    store_wrapped(put, tile * TILE, velocities[i][0], value)


def turn_kernel(y_first, y_second, frac, first, second, up, down):
    del frac
    for sx, message in ((1, up), (-1, down)):
        for n, sy in enumerate((1, -1)):
            k = moving(1, sy, 1).index(velocities.index((sx, sy, 0)))
            row = k * CX + (0 if sx == 1 else CX - 1)
            for field in range(2):
                line = pl.ds(field * FACE + row, 1)
                value = y_arrived(sy, line, y_first, y_second)
                message[pl.ds(2 * n + field, 1), :] = value
            numbers = y_arrived(sy, pl.ds(META, 1), y_first, y_second)
            message[pl.ds(4 + n, 1), :] = numbers
    pair_up(up, down, first, second)


def corner_arrived(sx, sy, row, messages):
    n = 0 if sy == 1 else 1
    line = pl.ds(4 + n if row == 2 else 2 * n + row, 1)
    return x_arrived(sx, line, *messages)


def forward_kernel(
    f_hbm, porosity_hbm, porous_hbm, walls_hbm, adjoint_hbm, table,
    moved, gap, adjoint, frac, mask, vel, x_first, x_second,
    f, porosity, porous, walls, x_up, x_down, f_sems, sems,
):
    def planes(n):
        part = pl.ds(n * PLANES, PLANES)
        return pltpu.make_async_copy(f_hbm.at[:, part], f.at[:, part], f_sems.at[n])

    small = [
        pltpu.make_async_copy(porosity_hbm, porosity, sems.at[0]),
        pltpu.make_async_copy(porous_hbm, porous, sems.at[1]),
        pltpu.make_async_copy(walls_hbm, walls, sems.at[2]),
    ]
    later = pltpu.make_async_copy(adjoint_hbm, adjoint, sems.at[3])
    for copy in small:
        copy.start()
    for n in range(CX // PLANES):
        planes(n).start()
    later.start()
    for copy in small:
        copy.wait()

    def plane(x):
        for yt in range(CY // TILE):
            at = (x, rows(yt))
            pops = [f[i, x, rows(yt), :] for i in range(Q)]
            fraction, open_panel = solidity(porosity[at], porous[at], walls[at])
            frac[at] = fraction
            mask[at] = open_panel
            u, e, _ = off_equilibrium(pops)
            for axis in range(3):
                vel[axis, x, rows(yt), :] = u[axis]
            c = correction(e)
            for i in range(Q):
                relaxed = pops[i] - c[i]
                change = pops[opposite[i]] - relaxed
                put_moved(gap, i, x, yt, open_panel * change, 1)
                put_moved(moved, i, x, yt, relaxed + fraction * change, 1)

    @pl.loop(0, CX // PLANES)
    def _(n):
        planes(n).wait()
        for k in range(PLANES):
            plane(n * PLANES + k)

    x_faces((moved, gap), 1, x_up, x_down)
    x_up[pl.ds(META, 1), :] = table[pl.ds(8, 1), :]
    x_down[pl.ds(META, 1), :] = table[pl.ds(1, 1), :]
    pair_up(x_up, x_down, x_first, x_second)
    later.wait()


def late_blocks(xb, halves, fields, adjoint, frac, mask, late, sums):
    for yt in range(CY // TILE):
        parts = {}
        for half in halves:
            x = xb * 2 + half
            at = (x, rows(yt))
            read = [fields[0][i, x, rows(yt), :] for i in range(Q)]
            u, e, df = off_equilibrium(read)
            b = [adjoint[i, x, rows(yt), :] for i in range(Q)]
            t, db = covector(b)
            total = sum(t[k] * e[k] for k in t) - sum(p * q for p, q in zip(db, df))
            total = mask[at] * total
            out = pull_back(b, t, u, frac[at])
            key = (0, 0)
            parts[key] = parts[key] + total if key in parts else total
            for i in range(Q):
                cx, cy, _ = velocities[i]
                key = ((half - cx) // 2, cy)
                early = out[i] * fields[1][i, x, rows(yt), :]
                parts[key] = parts[key] + early if key in parts else early
                put_moved(late, i, x, yt, out[i], -1)
        for (step, cy), part in parts.items():
            at = (xb + 1 + step, pl.ds(PAD_Y + yt * TILE - cy, TILE))
            sums[at] = sums[at] + part


def late_kernel(
    moved_in, gap_in, y_first, y_second, adjoint, frac, mask, moved, gap, late, sums
):
    del moved_in, gap_in
    fields = (moved, gap)
    fill_y(fields, 1, y_first, y_second)
    sums[...] = jnp.zeros((EXT_XB, EXT_Y, NZ), jnp.float32)

    def step(xb, halves=(0, 1)):
        late_blocks(xb, halves, fields, adjoint, frac, mask, late, sums)

    step(0, (1,))
    step(CX // 2 - 1, (0,))
    unrolled(1, CX // 2 - 1, 2, step)


def late_rest_kernel(
    late_in, sums_in, moved_in, gap_in, table, xs_in, xf_in, yf_in, ys_in,
    c_first, c_second, adjoint, frac, mask,
    late, sums, moved, gap, xf, xs, yu, yd, send_hbm,
    xu, xd, ext, ring, owner_of, scaled, send, sem,
):
    del late_in, sums_in, moved_in, gap_in
    fields = (moved, gap)
    messages = (c_first, c_second)
    fill_x(fields, 1, xf_in, xs_in)
    for sx, x in ((1, 0), (-1, CX - 1)):
        for sy, y in ((1, 0), (-1, CY - 1)):
            i = velocities.index((sx, sy, 0))
            for n, field in enumerate(fields):
                field[i, x, pl.ds(y, 1), :] = corner_arrived(sx, sy, n, messages)
    for xb, half in ((0, 0), (CX // 2 - 1, 1)):
        late_blocks(xb, (half,), fields, adjoint, frac, mask, late, sums)

    row, lane = iota((16, NZ), 0), iota((16, NZ), 1)
    numbers = pl.ds(META, 1)
    held = table[...]
    for sign, place in ((1, 0), (-1, 9)):
        here = x_arrived(sign, numbers, xf_in, xs_in)
        held = jnp.where(row == place, here, held)
    for sign, place in ((1, 0), (-1, 9)):
        here = column(y_arrived(sign, numbers, yf_in, ys_in), row == lane)
        held = jnp.where((lane == place) & (row > 0) & (row < 9), here, held)
    for sx, x in ((1, 0), (-1, 9)):
        for sy, y in ((1, 0), (-1, 9)):
            there = iota((1, NZ), 1) == (8 if sx == 1 else 1)
            here = column(corner_arrived(sx, sy, 2, messages), there)
            held = jnp.where((row == x) & (lane == y), here, held)
    ext[...] = held

    def put_lines(start, number, spot, total):
        number = number.astype(jnp.int32)
        lane = iota((total.shape[0], NZ), 1)
        spot = spot + (number & 3) if isinstance(spot, int) else spot(number & 3)
        line = pl.ds(start, total.shape[0])
        owner_of[line, :] = jnp.where(lane == jnp.right_shift(number, 10), 1.0, 0.0)
        patch = (jnp.right_shift(number, 2) & 255).astype(jnp.float32)
        value = jnp.where(lane == spot, jnp.sum(total, axis=1, keepdims=True), 0.0)
        scaled[line, :] = jnp.where(lane == spot + SLOT_LANE, patch, value)

    pick = iota((8, NZ), 1) == iota((8, NZ), 0) + 1
    for xb in range(EXT_XB):
        total = sums[xb, pl.ds(PAD_Y, 8, stride=2), :] + sums[xb, pl.ds(PAD_Y + 1, 8, stride=2), :]
        spot = 2 if xb == 0 else 4 if xb == 9 else 0
        put_lines(xb * 8, column(ext[pl.ds(xb, 1), :], pick), spot, total)
    ring[...] = jnp.zeros((32, NZ), jnp.float32)
    for xb in range(EXT_XB):
        ring[pl.ds(xb, 1), :] = sums[xb, pl.ds(PAD_Y - 1, 1), :]
        ring[pl.ds(16 + xb, 1), :] = sums[xb, pl.ds(PAD_Y + CY, 1), :]
    row = iota((16, 1), 0)
    for n, (face, corner, lane) in enumerate(((6, 10, 0), (8, 12, 9))):

        def spot(rank, face=face, corner=corner):
            side = jnp.where(row == 9, corner + 1, face + rank)
            return jnp.where(row == 0, corner, side)

        pick = (iota((16, NZ), 1) == lane) & (iota((16, NZ), 0) < EXT_XB)
        total = ring[pl.ds(16 * n, 16), :]
        put_lines(RING + 16 * n, column(ext[...], pick), spot, total)
    send[pl.ds(0, DEVICES, stride=2), :] = lax.dot_general(
        owner_of[...],
        scaled[...],
        (((0,), (0,)), ((), ())),
        precision=lax.Precision.HIGHEST,
        preferred_element_type=jnp.float32,
    )
    for there, i, x, y in corners(1):
        send[pl.ds(2 * there + 1, 1), :] = late[i, x, pl.ds(y, 1), :]
    copy = pltpu.make_async_copy(send, send_hbm, sem)
    copy.start()
    x_faces((late,), -1, xu, xd)
    y_faces(late, yu, yd)
    pair_up(xu, xd, xf, xs)
    copy.wait()


def corners(direction):
    gx, gy = lax.axis_index("gx"), lax.axis_index("gy")
    for ex in (1, -1):
        for ey in (1, -1):
            there_x = (gx + direction * ex) & (N_GX - 1)
            there_y = (gy + direction * ey) & (N_GY - 1)
            i = velocities.index((-ex, -ey, 0))
            x, y = 0 if ex == 1 else CX - 1, 0 if ey == 1 else CY - 1
            yield there_x * N_GY + there_y, i, x, y


def early_plane(x, late, frac, vel, put):
    for yt in range(CY // TILE):
        b = [late[i, x, rows(yt), :] for i in range(Q)]
        t, _ = covector(b)
        u = [vel[axis, x, rows(yt), :] for axis in range(3)]
        result = pull_back(b, t, u, frac[x, rows(yt)])
        for i in range(Q):
            put(i, yt, result[i])


def early_kernel(late_in, y_first, y_second, frac, vel, late, out, hold, sems):
    del late_in
    fill_y((late,), -1, y_first, y_second)

    def copy(x):
        return pltpu.make_async_copy(hold.at[:, x], out.at[:, x], sems.at[x])

    def step(x):
        def put(i, yt, value):
            hold[i, x, rows(yt), :] = value

        early_plane(x, late, frac, vel, put)
        copy(x).start()

    unrolled(1, CX - 1, 7, step)
    for x in range(1, CX - 1):
        copy(x).wait()


def last_kernel(
    out_in, late_in, second, first, got, frac, vel, late, out, patch_out, hold, patch, sems
):
    del out_in, late_in
    fill_x((late,), -1, first, second)
    for here, i, x, y in corners(-1):
        late[i, x, pl.ds(y, 1), :] = got[pl.ds(2 * here + 1, 1), :]
    copies = []
    for n, x in enumerate((0, CX - 1)):

        def put(i, yt, value, n=n):
            hold[n, i, rows(yt), :] = value

        early_plane(x, late, frac, vel, put)
        copies.append(pltpu.make_async_copy(hold.at[n], out.at[:, x], sems.at[n]))
        copies[n].start()
    data = got[pl.ds(0, DEVICES, stride=2), :].T
    part = 64
    for start in range(0, PATCH_DEV, part):
        number = (iota((part, DEVICES), 0) + start).astype(jnp.float32)
        total = jnp.zeros((part, DEVICES), jnp.float32)
        for k in range(PARTS):
            hit = data[SLOT_LANE + k : SLOT_LANE + k + 1] == number
            total = total + jnp.where(hit, data[k : k + 1], 0.0)
        patch[:, pl.ds(start, part)] = jnp.sum(total, axis=1)[None]
    copies.append(pltpu.make_async_copy(patch, patch_out, sems.at[2]))
    copies[2].start()
    for copy in copies:
        copy.wait()


VMEM = pl.BlockSpec(memory_space=pltpu.VMEM)
ANY = pl.BlockSpec(memory_space=pl.ANY)
LIMIT = 8 * 2**20


def vmem(*shape):
    return pltpu.VMEM(shape, jnp.float32)


def call(kernel, ins, outs, scratch=(), aliases=None, flops=0, hbm_ins=0, hbm_outs=()):
    held = [pltpu.with_memory_space_constraint(x, pltpu.HBM) for x in ins[:hbm_ins]]
    held += [pltpu.with_memory_space_constraint(x, pltpu.VMEM) for x in ins[hbm_ins:]]
    return pl.pallas_call(
        kernel,
        out_shape=[*outs, *hbm_outs],
        in_specs=[ANY] * hbm_ins + [VMEM] * (len(ins) - hbm_ins),
        out_specs=[VMEM] * len(outs) + [ANY] * len(hbm_outs),
        scratch_shapes=list(scratch),
        input_output_aliases=aliases or {},
        compiler_params=pltpu.CompilerParams(vmem_limit_bytes=LIMIT),
        cost_estimate=pl.CostEstimate(flops=flops, bytes_accessed=0, transcendentals=0),
    )(*held)


FIELD = vmem(Q, CX, CY, NZ)
NODE = vmem(CX, CY, NZ)
MESSAGE = vmem(MESSAGE_ROWS, NZ)
SHORT_MESSAGE = vmem(FACE, NZ)
LINES = vmem(LINE_COUNT, NZ)


def shift(block, axis, step):
    count = lax.axis_size(axis)
    return lax.ppermute(block, axis, [(i, (i + step) % count) for i in range(count)])


def swap(block, axis, step):
    count = lax.axis_size(axis)
    return lax.ppermute(
        block, axis, [(i, (i + (-step if i % 2 else step)) % count) for i in range(count)]
    )


def body(populations, porosity, adjoint_in, porous, walls, owners, slots):
    ints = pltpu.VMEM((CX, CY, NZ), jnp.int32)
    dma = pltpu.SemaphoreType.DMA
    table, yf, ys = call(
        edge_kernel,
        [populations, porosity, porous, walls, owners.reshape(1, 64), slots.reshape(1, 64)],
        [vmem(16, NZ), MESSAGE, MESSAGE],
        scratch=[vmem(2, Q, CX, NZ), vmem(2, CX, NZ)]
        + [pltpu.VMEM((2, CX, NZ), jnp.int32)] * 2
        + [pltpu.VMEM((1, 64), jnp.int32)] * 2
        + [dma((10,))],
        hbm_ins=6,
    )
    yf = shift(yf, "gy", 1)
    ys = shift(ys, "gy", -1)
    moved, gap, adjoint, frac, mask, vel, xf, xs = call(
        forward_kernel,
        [populations, porosity, porous, walls, adjoint_in, table],
        [FIELD] * 3 + [NODE] * 2 + [vmem(3, CX, CY, NZ), MESSAGE, MESSAGE],
        scratch=[FIELD, NODE, ints, ints, MESSAGE, MESSAGE, dma((CX // PLANES,)), dma((4,))],
        hbm_ins=5,
        flops=20_000_000,
    )
    xs = swap(xs, "gx", 1)
    xf = swap(xf, "gx", -1)
    corner = call(
        turn_kernel, [yf, ys, frac], [vmem(TILE, NZ)] * 2, scratch=[vmem(TILE, NZ)] * 2
    )
    corner = [swap(corner[0], "gx", -1), swap(corner[1], "gx", 1)]
    sums_shape = vmem(EXT_XB, EXT_Y, NZ)
    moved, gap, late, sums = call(
        late_kernel,
        [moved, gap, yf, ys, adjoint, frac, mask],
        [FIELD, FIELD, FIELD, sums_shape],
        aliases={0: 0, 1: 1},
        flops=20_000_000,
    )
    late, _, _, _, xf, xs, yf, ys, send = call(
        late_rest_kernel,
        [late, sums, moved, gap, table, xs, xf, yf, ys, *corner, adjoint, frac, mask],
        [FIELD, sums_shape, FIELD, FIELD] + [SHORT_MESSAGE] * 4,
        hbm_outs=[jax.ShapeDtypeStruct((2 * DEVICES, NZ), jnp.float32)],
        scratch=[SHORT_MESSAGE] * 2
        + [vmem(16, NZ), vmem(32, NZ), LINES, LINES, vmem(2 * DEVICES, NZ), dma],
        aliases={0: 0, 1: 1, 2: 2, 3: 3},
    )
    got = lax.all_to_all(send, ("gx", "gy"), split_axis=0, concat_axis=0, tiled=True)
    yf = shift(yf, "gy", 1)
    ys = shift(ys, "gy", -1)
    xs = swap(xs, "gx", 1)
    xf = swap(xf, "gx", -1)
    adjoint_shape = jax.ShapeDtypeStruct((Q, CX, CY, NZ), jnp.float32)
    late, adjoint_out = call(
        early_kernel,
        [late, yf, ys, frac, vel],
        [FIELD],
        hbm_outs=[adjoint_shape],
        scratch=[FIELD, dma((CX,))],
        aliases={0: 0},
        flops=20_000_000,
    )
    _, adjoint_out, patch = call(
        last_kernel,
        [adjoint_out, late, xs, xf, got, frac, vel],
        [FIELD],
        hbm_ins=1,
        hbm_outs=[adjoint_shape, jax.ShapeDtypeStruct((1, PATCH_DEV), jnp.float32)],
        scratch=[vmem(2, Q, CY, NZ), vmem(1, PATCH_DEV), dma((3,))],
        aliases={0: 1, 1: 0},
    )
    return adjoint_out, patch.reshape(PATCH_DEV)


def solution(mesh):
    return jax.shard_map(
        body,
        mesh=mesh,
        in_specs=(
            P(None, "gx", "gy", None),
            P("gx", "gy", None),
            P(None, "gx", "gy", None),
            P("gx", "gy", None),
            P("gx", "gy", None),
            P("gx", "gy", None, None),
            P("gx", "gy", None),
        ),
        out_specs=(P(None, "gx", "gy", None), P(("gx", "gy"))),
        check_vma=False,
    )
```
